32 devices in a mesh: gx: 4 (over y, core), gy: 4 (over z), gz: 2 (over x).
Axes of the slice: x: 2, y: 2, z: 4, core: 2. Of those that a mesh axis runs over, the one named last changes fastest.
Arguments:
- wavefunctions: float32 [48, 48, 24, 256], P('gx', 'gy', 'gz'), may hold values from -6 to 6
- cell_matrices: bfloat16 [8, 8, 4, 343, 343], P('gx', 'gy', 'gz'), may hold values from -0.078125 to 0.078125
- projectors: float32 [32, 16, 1728], P(('gx', 'gy', 'gz')), may hold values from -0.14433756 to 0.14433756
- slot_atoms: int32 [32, 16], P(('gx', 'gy', 'gz')), may hold values from 0 to 64, as said below
- atom_coupling: float32 [64], replicated, may hold values from 0.5 to 3
Outputs:
- filtered: float32 [48, 48, 24, 256], P('gx', 'gy', 'gz')
The draws below stay inside these ranges and needn't reach their ends.
Inputs may be any that keep to these rules, and one draw needn't show every extreme that they name: `slot_atoms`: atom a belongs to device a // 2. The live slots of device d name distinct atoms whose owners lie 0 or 1 below d along each of gx, gy, gz (periodically); 64 marks an empty slot, and some device has all 16 slots live.
All inputs are finite; a program needn't handle non-finite values.
Results may differ from the reference program's by a relative error of at most 0.00045.
Values may be sent and summed in bfloat16 or wider, within the bound.
No kernel may reach another device: no remote copies, remote signals or barrier semaphores. Data moves between devices by JAX's collectives and lax.ppermute only.
A program may use at most 64 MiB of HBM per device.

```python
import jax
import jax.numpy as jnp
from jax import lax

CELL_NODES = 343
WAVES = 256
DEGREE = 2
ATOM_DEV = 2
SLOTS = 16
NATOMS = 64
NODES_DEV = 1728
NNX = 48
NNY = 48
NNZ = 24
NCX = 8
NCY = 8
NCZ = 4
N_GX = 4
N_GY = 4
N_GZ = 2
DEVICES = 32


def draw_slot_atoms(key, part):
    candidates = 8 * ATOM_DEV
    device_keys = jax.random.split(jax.random.fold_in(key, 11), DEVICES)
    orders = jax.vmap(lambda one_key: jax.random.permutation(one_key, candidates))(device_keys)
    live_count = jax.random.randint(jax.random.fold_in(key, 12), (DEVICES,), 1, SLOTS // 4 + 2)
    busy_pick = jax.random.randint(jax.random.fold_in(key, 13), (DEVICES,), 0, 16)
    full_device = jax.random.randint(jax.random.fold_in(key, 14), (), 0, DEVICES)
    device_ids = jnp.arange(DEVICES)
    live_count = jnp.where((busy_pick == 0) | (device_ids == full_device), SLOTS, live_count)
    live_count = jnp.minimum(live_count, SLOTS)
    index_x = device_ids // (N_GY * N_GZ)
    index_y = device_ids // N_GZ % N_GY
    index_z = device_ids % N_GZ
    offsets = orders // ATOM_DEV
    within = orders % ATOM_DEV
    owner_x = (index_x[:, None] - offsets // 4) % N_GX
    owner_y = (index_y[:, None] - offsets // 2 % 2) % N_GY
    owner_z = (index_z[:, None] - offsets % 2) % N_GZ
    owner = (owner_x * N_GY + owner_y) * N_GZ + owner_z
    atom_ids = owner * ATOM_DEV + within
    positions = jnp.arange(SLOTS)
    return jnp.where(positions[None, :] < live_count[:, None], atom_ids[:, :SLOTS], NATOMS).astype(jnp.int32)


def block_levels(own_key, shape, shards, low, largest):
    def one(axis_at, parts):
        draws = jax.random.uniform(jax.random.fold_in(jax.random.fold_in(own_key, 6), axis_at), (parts,), jnp.float32, low / len(shards), largest / len(shards))
        return jnp.repeat(jnp.exp(draws), shape[axis_at] // parts).reshape((-1,) + (1,) * (len(shape) - axis_at - 1))

    level = one(*shards[0])
    for cut in shards[1:]:
        level = level * one(*cut)
    return level


def noise(rng, shape, deviation, most, cuts=(), held_as=jnp.bfloat16):
    factor_of = block_levels(rng, shape, cuts, -0.22, 0.18) if cuts else 1.0
    values = jax.random.normal(rng, shape, jnp.float32) * deviation * factor_of
    return jnp.minimum(jnp.maximum(values, -most), most).astype(held_as)


def setup_inputs(seed: int = 0) -> dict:
    streams_of = jax.random.split(jax.random.key(seed), 6)
    wavefunctions = noise(streams_of[0], (NNX, NNY, NNZ, WAVES), 1.0, 6.0, ((0, 4), (1, 4), (2, 2)), jnp.float32)
    cell_matrices = noise(streams_of[1], (NCX, NCY, NCZ, CELL_NODES, CELL_NODES), (16 * CELL_NODES) ** -0.5, 0.078125, ((0, 4), (1, 4), (2, 2)))
    projectors = noise(streams_of[2], (DEVICES, SLOTS, NODES_DEV), (1.0 / NODES_DEV ** 0.5), 0.14433756, ((0, 32),), jnp.float32)
    slot_atoms = draw_slot_atoms(jax.random.fold_in(streams_of[5], 71), 0)
    atom_coupling = jnp.clip(jax.random.uniform(streams_of[4], (NATOMS,), jnp.float32, 0.5, 3.0), 0.5, 3.0)
    return dict(wavefunctions=wavefunctions, cell_matrices=cell_matrices, projectors=projectors, slot_atoms=slot_atoms, atom_coupling=atom_coupling)


def extend_global(values, axis_pos):
    first_plane = lax.slice_in_dim(values, 0, 1, axis=axis_pos + 1)
    return jnp.concatenate([values, jnp.roll(first_plane, -1, axis=axis_pos)], axis=axis_pos + 1)


def fold_global(values, axis_pos):
    span_nodes = values.shape[axis_pos + 1]
    inner_part = lax.slice_in_dim(values, 0, span_nodes - 1, axis=axis_pos + 1)
    last_plane = lax.slice_in_dim(values, span_nodes - 1, span_nodes, axis=axis_pos + 1)
    front_plane = lax.slice_in_dim(inner_part, 0, 1, axis=axis_pos + 1) + jnp.roll(last_plane, 1, axis=axis_pos)
    return jnp.concatenate([front_plane, lax.slice_in_dim(inner_part, 1, span_nodes - 1, axis=axis_pos + 1)], axis=axis_pos + 1)


def cell_image(field_now, cell_matrices):
    cells_x, cells_y, cells_z = cell_matrices.shape[0], cell_matrices.shape[1], cell_matrices.shape[2]
    wave_count = field_now.shape[3]
    node_order = field_now.shape[0] // cells_x
    side_nodes = node_order + 1
    rounded = lax.optimization_barrier(field_now.astype(jnp.bfloat16)).astype(jnp.float32)
    values = rounded.reshape(cells_x, node_order, cells_y, node_order, cells_z, node_order, wave_count)
    values = extend_global(values, 0)
    values = extend_global(values, 2)
    values = extend_global(values, 4)
    stacked = values.transpose(0, 2, 4, 1, 3, 5, 6).reshape(cells_x, cells_y, cells_z, side_nodes ** 3, wave_count)
    product = jnp.einsum("xyzmn,xyznw->xyzmw", cell_matrices.astype(jnp.float32), stacked)
    product = product.reshape(cells_x, cells_y, cells_z, side_nodes, side_nodes, side_nodes, wave_count)
    product = product.transpose(0, 3, 1, 4, 2, 5, 6)
    product = fold_global(product, 4)
    product = fold_global(product, 2)
    product = fold_global(product, 0)
    return product.reshape(field_now.shape)


def nonlocal_image(field_now, projectors, slot_atoms, atom_coupling):
    grid_x, grid_y, grid_z, wave_count = field_now.shape
    block_x = grid_x // N_GX
    block_y = grid_y // N_GY
    block_z = grid_z // N_GZ
    blocks = field_now.reshape(N_GX, block_x, N_GY, block_y, N_GZ, block_z, wave_count)
    blocks = blocks.transpose(0, 2, 4, 1, 3, 5, 6).reshape(DEVICES, block_x * block_y * block_z, wave_count)
    coefficients = jnp.einsum("dsn,dnw->dsw", projectors, blocks, precision=lax.Precision.HIGHEST)
    slot_count = projectors.shape[1]
    atom_count = atom_coupling.shape[0]
    flat_coef = coefficients.reshape(DEVICES * slot_count, wave_count)
    columns = jnp.arange(atom_count).astype(jnp.int32)
    selector = (slot_atoms.reshape(-1)[:, None] == columns[None, :]).astype(jnp.float32)
    atom_totals = jnp.dot(selector.T, flat_coef, precision=lax.Precision.HIGHEST)
    weighted = atom_totals * atom_coupling[:, None]
    back = jnp.dot(selector, weighted, precision=lax.Precision.HIGHEST).reshape(DEVICES, slot_count, wave_count)
    image = jnp.einsum("dsn,dsw->dnw", projectors, back, precision=lax.Precision.HIGHEST)
    image = image.reshape(N_GX, N_GY, N_GZ, block_x, block_y, block_z, wave_count).transpose(0, 3, 1, 4, 2, 5, 6)
    return image.reshape(field_now.shape)


def reference(wavefunctions, cell_matrices, projectors, slot_atoms, atom_coupling):
    def apply_operator(field_now):
        return cell_image(field_now, cell_matrices) + nonlocal_image(field_now, projectors, slot_atoms, atom_coupling)

    previous = wavefunctions
    current = apply_operator(wavefunctions)
    for repeat in range(DEGREE - 1):
        following = 2.0 * apply_operator(current) - previous
        previous, current = current, following
    return current
```

```python
import functools

import jax
import jax.numpy as jnp
from jax import lax
from jax.experimental import pallas as pl
from jax.experimental.pallas import tpu as pltpu
from jax.sharding import PartitionSpec as P

AXES = ("gx", "gy", "gz")
F32 = jnp.float32
BF16 = jnp.bfloat16
LIMIT = 32 * 1024 * 1024


def up_to(value, unit):
    return -(-value // unit) * unit


def shifted(value, shift):
    sizes = [lax.axis_size(axis) for axis in AXES]
    pairs = []
    for x in range(sizes[0]):
        for y in range(sizes[1]):
            for z in range(sizes[2]):
                here = (x * sizes[1] + y) * sizes[2] + z
                there = [(p + s) % n for p, s, n in zip((x, y, z), shift, sizes)]
                pairs.append((here, (there[0] * sizes[1] + there[1]) * sizes[2] + there[2]))
    return lax.ppermute(value, AXES, pairs)


def halves(value):
    high = value.astype(BF16).astype(F32)
    return high, value - high


def put_split(rows_ref, start, value):
    count = value.shape[0]
    high, low = halves(value)
    rows_ref[start : start + count] = high
    rows_ref[start + count : start + 2 * count] = low


def get_split(rows_ref, start, count):
    return rows_ref[start : start + count] + rows_ref[start + count : start + 2 * count]


class Sizes:
    def __init__(self, field_shape, cell_shape, locals_count):
        self.bx, self.by, self.bz, self.waves = field_shape
        self.cells = cell_shape[:3]
        self.order = self.bx // cell_shape[0]
        self.side = self.order + 1
        self.group = up_to(self.side, 8)
        self.padded = up_to(self.side * self.side * self.group, 16)
        self.bzp = up_to(self.bz, 16)
        self.locals = locals_count
        self.half = locals_count // 2
        self.quarter = locals_count // 4
        self.own = locals_count // 8
        self.x_rows = self.by * self.bz
        self.y_rows = (self.bx + 1) * self.bz
        self.z_rows = (self.bx + 1) * self.by
        self.yz_rows = self.bx + 1
        self.x_msg = up_to(self.x_rows + 2 * self.half, 16)
        self.y_msg = up_to(self.y_rows + 2 * self.own, 16)
        self.z_msg = up_to(self.z_rows + 2 * self.own, 16)
        self.yz_msg = up_to(self.yz_rows + 2 * self.own, 16)
        self.nodes_padded = self.bx * self.by * self.bzp

    def rows(self, count, dtype=F32):
        return jax.ShapeDtypeStruct((count, self.waves), dtype)

    def scratch(self, *shape):
        return pltpu.VMEM(shape + (self.waves,), F32)


def call(body, sizes, outs, scratch, args):
    return pl.pallas_call(
        functools.partial(body, sizes),
        out_shape=outs,
        in_specs=[pl.BlockSpec(memory_space=pltpu.VMEM) for _ in args],
        out_specs=[pl.BlockSpec(memory_space=pltpu.VMEM) for _ in outs],
        scratch_shapes=scratch,
        compiler_params=pltpu.CompilerParams(vmem_limit_bytes=LIMIT),
    )(*args)


def projector_body(s, rows_ref, by_node_ref, by_atom_ref, tall_ref, wide_ref):
    rows = rows_ref[...]
    high, low = halves(rows)
    low = low.astype(BF16).astype(F32)
    tall_ref[...] = jnp.concatenate([high, low, high], axis=0).T
    wide_ref[...] = jnp.zeros(wide_ref.shape, F32)
    for g in range(s.bx * s.by):
        wide_ref[g, 0 : s.bz, :] = tall_ref[g * s.bz : (g + 1) * s.bz, :]
    wide = wide_ref[...].reshape(s.nodes_padded, 3 * s.locals)
    by_node_ref[...] = wide.astype(BF16)
    by_atom_ref[...] = wide.T[0 : 2 * s.locals].astype(BF16)


def coefficients(s, by_atom_ref, wide_ref):
    field = wide_ref[...].reshape(s.nodes_padded, s.waves)
    high = field.astype(BF16)
    low = (field - high.astype(F32)).astype(BF16)
    with_high = jnp.dot(by_atom_ref[...], high, preferred_element_type=F32)
    with_low = jnp.dot(by_atom_ref[0 : s.locals], low, preferred_element_type=F32)
    return with_high[0 : s.locals] + with_high[s.locals : 2 * s.locals] + with_low


def send_down_x(s, by_atom_ref, wide_ref, rows_ref, msg_ref, kept_ref):
    total = coefficients(s, by_atom_ref, wide_ref)
    kept_ref[...] = total[0 : s.half]
    rows_ref[...] = jnp.zeros(rows_ref.shape, F32)
    for y in range(s.by):
        rows_ref[y * s.bz : (y + 1) * s.bz] = wide_ref[0, y, 0 : s.bz]
    put_split(rows_ref, s.x_rows, total[s.half : 2 * s.half])
    msg_ref[...] = rows_ref[...].astype(BF16)


def first_body(s, field_ref, by_atom_ref, msg_ref, kept_ref, wide_ref, rows_ref):
    wide_ref[:, :, 0 : s.bz, :] = field_ref[...]
    wide_ref[:, :, s.bz : s.bzp, :] = jnp.zeros((s.bx, s.by, s.bzp - s.bz, s.waves), F32)
    send_down_x(s, by_atom_ref, wide_ref, rows_ref, msg_ref, kept_ref)


def down_body(s, field_ref, from_x_ref, kept_ref, y_msg_ref, z_msg_ref, yz_msg_ref, part_ref, x_ref, y_ref, z_ref, yz_ref):
    x_ref[...] = from_x_ref[...].astype(F32)
    total = kept_ref[...] + get_split(x_ref, s.x_rows, s.half)
    y_ref[...] = jnp.zeros(y_ref.shape, F32)
    z_ref[...] = jnp.zeros(z_ref.shape, F32)
    yz_ref[...] = jnp.zeros(yz_ref.shape, F32)
    for x in range(s.bx):
        y_ref[x * s.bz : (x + 1) * s.bz] = field_ref[x, 0]
        z_ref[x * s.by : (x + 1) * s.by] = field_ref[x, :, 0, :]
        yz_ref[x : x + 1] = field_ref[x, 0, 0:1, :]
    y_ref[s.bx * s.bz : s.y_rows] = x_ref[0 : s.bz]
    for y in range(s.by):
        z_ref[s.bx * s.by + y : s.bx * s.by + y + 1] = x_ref[y * s.bz : y * s.bz + 1]
    yz_ref[s.bx : s.bx + 1] = x_ref[0:1]
    own = s.own
    part_ref[...] = total[0:own]
    put_split(z_ref, s.z_rows, total[own : 2 * own])
    put_split(y_ref, s.y_rows, total[2 * own : 3 * own])
    put_split(yz_ref, s.yz_rows, total[3 * own : 4 * own])
    y_msg_ref[...] = y_ref[...].astype(BF16)
    z_msg_ref[...] = z_ref[...].astype(BF16)
    yz_msg_ref[...] = yz_ref[...].astype(BF16)


def cell_body(
    s, field_ref, matrix_ref, from_x_ref, from_y_ref, from_z_ref, from_yz_ref, part_ref, weight_ref,
    block_ref, y_msg_ref, z_msg_ref, yz_msg_ref, own_ref,
    values_ref, sums_ref, x_ref, y_ref, z_ref, yz_ref,
):
    order, side, group = s.order, s.side, s.group
    cells_x, cells_y, cells_z = s.cells
    x_ref[...] = from_x_ref[...].astype(F32)
    y_ref[...] = from_y_ref[...].astype(F32)
    z_ref[...] = from_z_ref[...].astype(F32)
    yz_ref[...] = from_yz_ref[...].astype(F32)
    for k in range(cells_z):
        first = k * order
        count = min(group, s.bz - first)
        values_ref[k, 0 : s.bx, 0 : s.by, 0:count, :] = field_ref[:, :, first : first + count, :]
        for y in range(s.by):
            values_ref[k, s.bx, y, 0:count, :] = x_ref[y * s.bz + first : y * s.bz + first + count]
        for x in range(s.bx + 1):
            values_ref[k, x, s.by, 0:count, :] = y_ref[x * s.bz + first : x * s.bz + first + count]
        if count < group:
            values_ref[k, :, :, count:group, :] = jnp.zeros((s.bx + 1, s.by + 1, group - count, s.waves), F32)
    k = cells_z - 1
    for x in range(s.bx + 1):
        values_ref[k, x, 0 : s.by, order, :] = z_ref[x * s.by : (x + 1) * s.by]
        values_ref[k, x, s.by, order : order + 1, :] = yz_ref[x : x + 1]
    sums_ref[...] = jnp.zeros(sums_ref.shape, F32)
    used = side * side * group
    for i in range(cells_x):
        for j in range(cells_y):
            for k in range(cells_z):
                span_x = slice(i * order, i * order + side)
                span_y = slice(j * order, j * order + side)
                values = values_ref[k, span_x, span_y].reshape(used, s.waves)
                if s.padded > used:
                    values = jnp.concatenate([values, jnp.zeros((s.padded - used, s.waves), F32)], axis=0)
                product = jnp.dot(matrix_ref[i, j, k], values.astype(BF16), preferred_element_type=F32)
                sums_ref[k, span_x, span_y] += product[0:used].reshape(side, side, group, s.waves)
    own = s.own
    total = part_ref[...] + get_split(z_ref, s.z_rows, own) + get_split(y_ref, s.y_rows, own) + get_split(yz_ref, s.yz_rows, own)
    total = total * weight_ref[...]
    own_ref[...] = total
    for k in range(cells_z):
        first = k * order
        block_ref[:, :, first : first + order, :] = sums_ref[k, :, 0 : s.by, 0:order, :]
        if k:
            block_ref[:, :, first : first + 1, :] += sums_ref[k - 1, :, 0 : s.by, order : order + 1, :]
    y_ref[...] = jnp.zeros(y_ref.shape, F32)
    z_ref[...] = jnp.zeros(z_ref.shape, F32)
    yz_ref[...] = jnp.zeros(yz_ref.shape, F32)
    last = cells_z - 1
    for x in range(s.bx + 1):
        for k in range(cells_z):
            at = x * s.bz + k * order
            y_ref[at : at + order] = sums_ref[k, x, s.by, 0:order, :]
            if k:
                y_ref[at : at + 1] += sums_ref[k - 1, x, s.by, order : order + 1, :]
        z_ref[x * s.by : (x + 1) * s.by] = sums_ref[last, x, 0 : s.by, order, :]
        yz_ref[x : x + 1] = sums_ref[last, x, s.by, order : order + 1, :]
    put_split(y_ref, s.y_rows, total)
    put_split(z_ref, s.z_rows, total)
    put_split(yz_ref, s.yz_rows, total)
    y_msg_ref[...] = y_ref[...].astype(BF16)
    z_msg_ref[...] = z_ref[...].astype(BF16)
    yz_msg_ref[...] = yz_ref[...].astype(BF16)


def up_body(s, block_ref, from_y_ref, from_z_ref, from_yz_ref, own_ref, x_msg_ref, spread_ref, x_ref, y_ref, z_ref, yz_ref):
    y_ref[...] = from_y_ref[...].astype(F32)
    z_ref[...] = from_z_ref[...].astype(F32)
    yz_ref[...] = from_yz_ref[...].astype(F32)
    x_ref[...] = jnp.zeros(x_ref.shape, F32)
    for y in range(s.by):
        x_ref[y * s.bz : (y + 1) * s.bz] = block_ref[s.bx, y]
    x_ref[0 : s.bz] += y_ref[s.bx * s.bz : s.y_rows]
    for y in range(s.by):
        x_ref[y * s.bz : y * s.bz + 1] += z_ref[s.bx * s.by + y : s.bx * s.by + y + 1]
    x_ref[0:1] += yz_ref[s.bx : s.bx + 1]
    own = s.own
    spread = jnp.concatenate(
        [own_ref[...], get_split(z_ref, s.z_rows, own), get_split(y_ref, s.y_rows, own), get_split(yz_ref, s.yz_rows, own)], axis=0
    )
    spread_ref[...] = spread
    put_split(x_ref, s.x_rows, spread)
    x_msg_ref[...] = x_ref[...].astype(BF16)


def assemble(s, block_ref, from_x_ref, from_y_ref, from_z_ref, from_yz_ref, spread_ref, by_node_ref, wide_ref, x_ref, y_ref, z_ref, yz_ref):
    x_ref[...] = from_x_ref[...].astype(F32)
    y_ref[...] = from_y_ref[...].astype(F32)
    z_ref[...] = from_z_ref[...].astype(F32)
    yz_ref[...] = from_yz_ref[...].astype(F32)
    totals = jnp.concatenate([spread_ref[...], get_split(x_ref, s.x_rows, s.half)], axis=0)
    high, low = halves(totals)
    stacked = jnp.concatenate([high, high, low], axis=0).astype(BF16)
    image = jnp.dot(by_node_ref[...], stacked, preferred_element_type=F32)
    wide_ref[...] = image.reshape(s.bx, s.by, s.bzp, s.waves)
    wide_ref[:, :, 0 : s.bz, :] += block_ref[0 : s.bx]
    for y in range(s.by):
        wide_ref[0, y, 0 : s.bz, :] += x_ref[y * s.bz : (y + 1) * s.bz]
    for x in range(s.bx):
        wide_ref[x, 0, 0 : s.bz, :] += y_ref[x * s.bz : (x + 1) * s.bz]
        wide_ref[x, :, 0, :] += z_ref[x * s.by : (x + 1) * s.by]
        wide_ref[x, 0, 0:1, :] += yz_ref[x : x + 1]


def middle_body(
    s, block_ref, from_x_ref, from_y_ref, from_z_ref, from_yz_ref, spread_ref, by_node_ref, by_atom_ref,
    field_ref, msg_ref, kept_ref, wide_ref, x_ref, y_ref, z_ref, yz_ref,
):
    assemble(s, block_ref, from_x_ref, from_y_ref, from_z_ref, from_yz_ref, spread_ref, by_node_ref, wide_ref, x_ref, y_ref, z_ref, yz_ref)
    field_ref[...] = wide_ref[:, :, 0 : s.bz, :]
    send_down_x(s, by_atom_ref, wide_ref, x_ref, msg_ref, kept_ref)


def last_body(
    s, start_ref, block_ref, from_x_ref, from_y_ref, from_z_ref, from_yz_ref, spread_ref, by_node_ref,
    out_ref, wide_ref, x_ref, y_ref, z_ref, yz_ref,
):
    assemble(s, block_ref, from_x_ref, from_y_ref, from_z_ref, from_yz_ref, spread_ref, by_node_ref, wide_ref, x_ref, y_ref, z_ref, yz_ref)
    out_ref[...] = 2.0 * wide_ref[:, :, 0 : s.bz, :] - start_ref[...]


def atom_rows(proj_rows, slot_ids, atom_count):
    size_x, size_y, size_z = (lax.axis_size(axis) for axis in AXES)
    index_x, index_y, index_z = (lax.axis_index(axis) for axis in AXES)
    per_device = atom_count // (size_x * size_y * size_z)
    owner = slot_ids // per_device
    delta_x = (index_x - owner // (size_y * size_z)) % size_x
    delta_y = (index_y - owner // size_z % size_y) % size_y
    delta_z = (index_z - owner % size_z) % size_z
    local_slot = ((delta_x * 2 + delta_y) * 2 + delta_z) * per_device + slot_ids % per_device
    local_slot = jnp.where(slot_ids < atom_count, local_slot, -1)
    columns = lax.iota(jnp.int32, 8 * per_device)
    selector = (columns[:, None] == local_slot[None, :]).astype(F32)
    return jnp.dot(selector, proj_rows, precision=lax.Precision.HIGHEST, preferred_element_type=F32)


def regrouped(s, cell_matrices):
    row = lax.iota(jnp.int32, s.padded)
    node = jnp.where(row % s.group < s.side, row // s.group * s.side + row % s.group, -1)
    spread = (node[:, None] == lax.iota(jnp.int32, cell_matrices.shape[3])[None, :]).astype(BF16)
    wide = jnp.einsum("xyzmn,cn->xyzmc", cell_matrices, spread, preferred_element_type=BF16)
    return jnp.einsum("rm,xyzmc->xyzrc", spread, wide, preferred_element_type=BF16)


def local(wavefunctions, cell_matrices, projectors, slot_atoms, atom_coupling):
    atom_count = atom_coupling.shape[0]
    devices = 1
    for axis in AXES:
        devices *= lax.axis_size(axis)
    per_device = atom_count // devices
    s = Sizes(wavefunctions.shape, cell_matrices.shape, 8 * per_device)
    index = (lax.axis_index("gx") * lax.axis_size("gy") + lax.axis_index("gy")) * lax.axis_size("gz") + lax.axis_index("gz")
    weight = lax.dynamic_slice_in_dim(atom_coupling, index * per_device, per_device)
    weight = jnp.broadcast_to(weight[:, None], (per_device, s.waves))
    rows = atom_rows(projectors[0], slot_atoms[0], atom_count)
    by_node, by_atom = call(
        projector_body,
        s,
        [jax.ShapeDtypeStruct((s.nodes_padded, 3 * s.locals), BF16), jax.ShapeDtypeStruct((2 * s.locals, s.nodes_padded), BF16)],
        [pltpu.VMEM((s.bx * s.by * s.bz, 3 * s.locals), F32), pltpu.VMEM((s.bx * s.by, s.bzp, 3 * s.locals), F32)],
        [rows],
    )
    matrices = regrouped(s, cell_matrices)
    wide = s.scratch(s.bx, s.by, s.bzp)
    x_rows, y_rows, z_rows, yz_rows = (s.scratch(n) for n in (s.x_msg, s.y_msg, s.z_msg, s.yz_msg))
    side_msgs = [s.rows(s.y_msg, BF16), s.rows(s.z_msg, BF16), s.rows(s.yz_msg, BF16)]
    sum_shape = (s.cells[2], s.bx + 1, s.by + 1, s.group)
    down_x, kept = call(first_body, s, [s.rows(s.x_msg, BF16), s.rows(s.half)], [wide, x_rows], [wavefunctions, by_atom])
    field = wavefunctions
    for step in range(2):
        from_x = shifted(down_x, (-1, 0, 0))
        y_msg, z_msg, yz_msg, part = call(
            down_body, s, side_msgs + [s.rows(s.own)], [x_rows, y_rows, z_rows, yz_rows], [field, from_x, kept]
        )
        from_y = shifted(y_msg, (0, -1, 0))
        from_z = shifted(z_msg, (0, 0, -1))
        from_yz = shifted(yz_msg, (0, -1, -1))
        block, y_msg, z_msg, yz_msg, own = call(
            cell_body,
            s,
            [jax.ShapeDtypeStruct((s.bx + 1, s.by, s.bz, s.waves), F32)] + side_msgs + [s.rows(s.own)],
            [s.scratch(*sum_shape), s.scratch(*sum_shape), x_rows, y_rows, z_rows, yz_rows],
            [field, matrices, from_x, from_y, from_z, from_yz, part, weight],
        )
        from_y = shifted(y_msg, (0, 1, 0))
        from_z = shifted(z_msg, (0, 0, 1))
        from_yz = shifted(yz_msg, (0, 1, 1))
        up_x, spread = call(
            up_body,
            s,
            [s.rows(s.x_msg, BF16), s.rows(s.half)],
            [x_rows, y_rows, z_rows, yz_rows],
            [block, from_y, from_z, from_yz, own],
        )
        from_x = shifted(up_x, (1, 0, 0))
        scratch = [wide, x_rows, y_rows, z_rows, yz_rows]
        received = [block, from_x, from_y, from_z, from_yz, spread, by_node]
        if step == 0:
            field, down_x, kept = call(
                middle_body,
                s,
                [jax.ShapeDtypeStruct(field.shape, F32), s.rows(s.x_msg, BF16), s.rows(s.half)],
                scratch,
                received + [by_atom],
            )
        else:
            (out,) = call(last_body, s, [jax.ShapeDtypeStruct(field.shape, F32)], scratch, [wavefunctions] + received)
    return out


def solution(mesh):
    return jax.shard_map(
        local,
        mesh=mesh,
        in_specs=(
            P("gx", "gy", "gz", None),
            P("gx", "gy", "gz", None, None),
            P(("gx", "gy", "gz"), None, None),
            P(("gx", "gy", "gz"), None),
            P(),
        ),
        out_specs=P("gx", "gy", "gz", None),
        check_vma=False,
    )
```

```python
import functools

import jax
import jax.numpy as jnp
from jax import lax
from jax.experimental import pallas as pl
from jax.experimental.pallas import tpu as pltpu
from jax.sharding import PartitionSpec as P

AXES = ("gx", "gy", "gz")
F32 = jnp.float32
BF16 = jnp.bfloat16
LIMIT = 12 * 1024 * 1024


def up_to(value, unit):
    return -(-value // unit) * unit


def shifted(value, shift):
    sizes = [lax.axis_size(axis) for axis in AXES]
    pairs = []
    for x in range(sizes[0]):
        for y in range(sizes[1]):
            for z in range(sizes[2]):
                here = (x * sizes[1] + y) * sizes[2] + z
                there = [(p + s) % n for p, s, n in zip((x, y, z), shift, sizes)]
                pairs.append((here, (there[0] * sizes[1] + there[1]) * sizes[2] + there[2]))
    return lax.ppermute(value, AXES, pairs)


def halves(value):
    high = value.astype(BF16).astype(F32)
    return high, value - high


def put_split(rows_ref, start, value):
    count = value.shape[0]
    high, low = halves(value)
    rows_ref[start : start + count] = high
    rows_ref[start + count : start + 2 * count] = low


def get_split(rows_ref, start, count):
    return rows_ref[start : start + count] + rows_ref[start + count : start + 2 * count]


class Sizes:
    def __init__(self, field_shape, cell_shape, locals_count):
        self.bx, self.by, self.bz, self.waves = field_shape
        self.cells = cell_shape[:3]
        self.order = self.bx // cell_shape[0]
        self.side = self.order + 1
        self.group = up_to(self.side, 8)
        self.padded = up_to(self.side * self.side * self.group, 16)
        self.bzp = up_to(max(self.bz + 1, (cell_shape[2] - 1) * self.order + self.group), 16)
        self.locals = locals_count
        self.half = locals_count // 2
        self.quarter = locals_count // 4
        self.own = locals_count // 8
        self.x_rows = self.by * self.bz
        self.y_rows = (self.bx + 1) * self.bz
        self.z_rows = (self.bx + 1) * self.by
        self.yz_rows = self.bx + 1
        self.x_msg = up_to(self.x_rows + 2 * self.half, 16)
        self.y_msg = up_to(self.y_rows + 2 * self.own, 16)
        self.z_msg = up_to(self.z_rows + 2 * self.own, 16)
        self.yz_msg = up_to(self.yz_rows + 2 * self.own, 16)
        self.nodes_padded = self.bx * self.by * self.bzp

    def extended(self):
        return jax.ShapeDtypeStruct((self.bx + 1, self.by + 1, self.bzp, self.waves), F32)

    def rows(self, count, dtype=F32):
        return jax.ShapeDtypeStruct((count, self.waves), dtype)

    def scratch(self, *shape):
        return pltpu.VMEM(shape + (self.waves,), F32)


VMEM = pltpu.VMEM


def call(body, sizes, outs, scratch, args, spaces=None, out_spaces=None, aliases=None):
    spaces = spaces or {}
    out_spaces = out_spaces or {}
    outs = [out_spaces.get(n, VMEM)(out.shape, out.dtype) for n, out in enumerate(outs)]
    args = [pltpu.with_memory_space_constraint(arg, spaces.get(n, VMEM)) for n, arg in enumerate(args)]
    return pl.pallas_call(
        functools.partial(body, sizes),
        out_shape=outs,
        in_specs=[pl.BlockSpec(memory_space=spaces.get(n, VMEM)) for n in range(len(args))],
        out_specs=[pl.BlockSpec(memory_space=out_spaces.get(n, VMEM)) for n in range(len(outs))],
        scratch_shapes=scratch,
        input_output_aliases=aliases or {},
        compiler_params=pltpu.CompilerParams(vmem_limit_bytes=LIMIT),
    )(*args)


def own_index():
    return (lax.axis_index("gx") * lax.axis_size("gy") + lax.axis_index("gy")) * lax.axis_size("gz") + lax.axis_index("gz")


def local_atoms(own):
    sizes = [lax.axis_size(axis) for axis in AXES]
    here = [lax.axis_index(axis) for axis in AXES]
    ids = []
    for dx in range(2):
        for dy in range(2):
            for dz in range(2):
                x, y, z = (lax.rem(h + n - d, n) for h, n, d in zip(here, sizes, (dx, dy, dz)))
                owner = (x * sizes[1] + y) * sizes[2] + z
                ids += [owner * own + a for a in range(own)]
    return jnp.stack(ids).astype(jnp.int32)


def put_face(s, rows_ref, field_ref):
    for y in range(s.by):
        rows_ref[y * s.bz : (y + 1) * s.bz] = field_ref[0, y, 0 : s.bz]


def plane_sums(s, by_atom_ref, x, plane):
    high = plane.astype(BF16)
    low = (plane - high.astype(F32)).astype(BF16)
    with_high = jnp.dot(by_atom_ref[x], high, preferred_element_type=F32)
    with_low = jnp.dot(by_atom_ref[x, 0 : s.locals], low, preferred_element_type=F32)
    return with_high[0 : s.locals] + with_high[s.locals : 2 * s.locals] + with_low


def send_down_x(s, total, field_ref, rows_ref, msg_ref, kept_ref):
    kept_ref[...] = total[0 : s.half]
    put_face(s, rows_ref, field_ref)
    rows_ref[s.x_rows :] = jnp.zeros((s.x_msg - s.x_rows, s.waves), F32)
    put_split(rows_ref, s.x_rows, total[s.half : 2 * s.half])
    msg_ref[...] = rows_ref[...].astype(BF16)


def first_body(
    s, start_hbm, rows_hbm, slots_hbm, ids_ref,
    field_ref, by_node_ref, by_atom_ref, msg_ref, kept_ref,
    start_ref, rows_ref, slots_ref, tall_ref, wide_ref, x_ref, sems, small_sems,
):
    small = [
        pltpu.make_async_copy(rows_hbm, rows_ref, small_sems.at[0]),
        pltpu.make_async_copy(slots_hbm, slots_ref, small_sems.at[1]),
    ]
    for copy in small:
        copy.start()
    copies = [pltpu.make_async_copy(start_hbm.at[x], start_ref.at[x], sems.at[x]) for x in range(s.bx)]
    for copy in copies:
        copy.start()
    for copy in small:
        copy.wait()
    selector = (ids_ref[...] == slots_ref[...]).astype(F32)
    rows = jnp.dot(selector, rows_ref[0], precision=lax.Precision.HIGHEST, preferred_element_type=F32)
    high, low = halves(rows)
    low = low.astype(BF16).astype(F32)
    tall_ref[...] = jnp.concatenate([high, low, high], axis=0).T
    wide_ref[:, s.bz : s.bzp, :] = jnp.zeros((s.bx * s.by, s.bzp - s.bz, 3 * s.locals), F32)
    for g in range(s.bx * s.by):
        wide_ref[g, 0 : s.bz, :] = tall_ref[g * s.bz : (g + 1) * s.bz, :]
    for x in range(s.bx):
        wide = wide_ref[x * s.by : (x + 1) * s.by].reshape(s.by * s.bzp, 3 * s.locals)
        by_node_ref[x] = wide.astype(BF16)
        by_atom_ref[x] = wide.T[0 : 2 * s.locals].astype(BF16)
    total = jnp.zeros((s.locals, s.waves), F32)
    for x in range(s.bx):
        copies[x].wait()
        plane = start_ref[x]
        plane = jnp.concatenate([plane, jnp.zeros((s.by, s.bzp - s.bz, s.waves), F32)], axis=1)
        field_ref[x, 0 : s.by] = plane
        total = total + plane_sums(s, by_atom_ref, x, plane.reshape(s.by * s.bzp, s.waves))
    send_down_x(s, total, field_ref, x_ref, msg_ref, kept_ref)


def down_body(s, field_ref, from_x_ref, kept_ref, y_msg_ref, z_msg_ref, yz_msg_ref, part_ref, x_ref, y_ref, z_ref, yz_ref):
    x_ref[...] = from_x_ref[...].astype(F32)
    total = kept_ref[...] + get_split(x_ref, s.x_rows, s.half)
    for ref, used in ((y_ref, s.y_rows), (z_ref, s.z_rows), (yz_ref, s.yz_rows)):
        ref[used:] = jnp.zeros((ref.shape[0] - used, s.waves), F32)
    for x in range(s.bx):
        y_ref[x * s.bz : (x + 1) * s.bz] = field_ref[x, 0, 0 : s.bz]
        z_ref[x * s.by : (x + 1) * s.by] = field_ref[x, 0 : s.by, 0, :]
        yz_ref[x : x + 1] = field_ref[x, 0, 0:1, :]
    y_ref[s.bx * s.bz : s.y_rows] = x_ref[0 : s.bz]
    for y in range(s.by):
        z_ref[s.bx * s.by + y : s.bx * s.by + y + 1] = x_ref[y * s.bz : y * s.bz + 1]
    yz_ref[s.bx : s.bx + 1] = x_ref[0:1]
    own = s.own
    part_ref[...] = total[0:own]
    put_split(z_ref, s.z_rows, total[own : 2 * own])
    put_split(y_ref, s.y_rows, total[2 * own : 3 * own])
    put_split(yz_ref, s.yz_rows, total[3 * own : 4 * own])
    y_msg_ref[...] = y_ref[...].astype(BF16)
    z_msg_ref[...] = z_ref[...].astype(BF16)
    yz_msg_ref[...] = yz_ref[...].astype(BF16)


def cell_body(
    s, before_ref, matrix_ref, from_x_ref, from_y_ref, from_z_ref, from_yz_ref, part_ref, weight_ref,
    field_ref, block_ref, y_msg_ref, z_msg_ref, yz_msg_ref, own_ref,
    sums_ref, x_ref, y_ref, z_ref, yz_ref,
):
    del before_ref
    order, side, group = s.order, s.side, s.group
    cells_x, cells_y, cells_z = s.cells
    x_ref[...] = from_x_ref[...].astype(F32)
    y_ref[...] = from_y_ref[...].astype(F32)
    z_ref[...] = from_z_ref[...].astype(F32)
    yz_ref[...] = from_yz_ref[...].astype(F32)
    rest = jnp.zeros((s.bzp - s.bz, s.waves), F32)
    for y in range(s.by):
        field_ref[s.bx, y, 0 : s.bz, :] = x_ref[y * s.bz : (y + 1) * s.bz]
        field_ref[s.bx, y, s.bz :, :] = rest
    for x in range(s.bx + 1):
        field_ref[x, s.by, 0 : s.bz, :] = y_ref[x * s.bz : (x + 1) * s.bz]
        field_ref[x, s.by, s.bz :, :] = rest
        field_ref[x, 0 : s.by, s.bz, :] = z_ref[x * s.by : (x + 1) * s.by]
        field_ref[x, s.by, s.bz : s.bz + 1, :] = yz_ref[x : x + 1]
    used = side * side * group
    for i in range(cells_x):
        for j in range(cells_y):
            for k in range(cells_z):
                first = k * order
                values = field_ref[i * order : i * order + side, j * order : j * order + side, first : first + group]
                values = values.reshape(used, s.waves)
                if s.padded > used:
                    values = jnp.concatenate([values, jnp.zeros((s.padded - used, s.waves), F32)], axis=0)
                product = jnp.dot(matrix_ref[i, j, k], values.astype(BF16), preferred_element_type=F32)
                product = product[0:used].reshape(side, side, group, s.waves)
                x0, x1, y0, y1 = i * order, i * order + side, j * order, j * order + side
                a, b = int(i > 0), int(j > 0)
                sums_ref[k, x0 + a : x1, y0 + b : y1] = product[a:, b:]
                if a:
                    sums_ref[k, x0, y0 + b : y1] += product[0, b:]
                if b:
                    sums_ref[k, x0 + a : x1, y0] += product[a:, 0]
                if a and b:
                    sums_ref[k, x0, y0] += product[0, 0]
    own = s.own
    total = part_ref[...] + get_split(z_ref, s.z_rows, own) + get_split(y_ref, s.y_rows, own) + get_split(yz_ref, s.yz_rows, own)
    total = total * weight_ref[...]
    own_ref[...] = total
    last = cells_z - 1
    for x in range(s.bx + 1):
        z_ref[x * s.by : (x + 1) * s.by] = sums_ref[last, x, 0 : s.by, order, :]
        yz_ref[x : x + 1] = sums_ref[last, x, s.by, order : order + 1, :]
        for k in range(cells_z):
            at = x * s.bz + k * order
            y_ref[at : at + order] = sums_ref[k, x, s.by, 0:order, :]
            if k:
                y_ref[at : at + 1] += sums_ref[k - 1, x, s.by, order : order + 1, :]
    put_split(y_ref, s.y_rows, total)
    put_split(z_ref, s.z_rows, total)
    put_split(yz_ref, s.yz_rows, total)
    y_msg_ref[...] = y_ref[...].astype(BF16)
    z_msg_ref[...] = z_ref[...].astype(BF16)
    yz_msg_ref[...] = yz_ref[...].astype(BF16)
    for x in range(s.bx + 1):
        block_ref[x, :, 0:group, :] = sums_ref[0, x, 0 : s.by]
        block_ref[x, :, group:, :] = jnp.zeros((s.by, s.bzp - group, s.waves), F32)
        for k in range(1, cells_z):
            block_ref[x, :, k * order : k * order + group, :] += sums_ref[k, x, 0 : s.by]


def up_body(s, block_ref, from_y_ref, from_z_ref, from_yz_ref, own_ref, x_msg_ref, spread_ref, x_ref, y_ref, z_ref, yz_ref):
    y_ref[...] = from_y_ref[...].astype(F32)
    z_ref[...] = from_z_ref[...].astype(F32)
    yz_ref[...] = from_yz_ref[...].astype(F32)
    x_ref[s.x_rows :] = jnp.zeros((s.x_msg - s.x_rows, s.waves), F32)
    for y in range(s.by):
        x_ref[y * s.bz : (y + 1) * s.bz] = block_ref[s.bx, y, 0 : s.bz]
    x_ref[0 : s.bz] += y_ref[s.bx * s.bz : s.y_rows]
    for y in range(s.by):
        x_ref[y * s.bz : y * s.bz + 1] += z_ref[s.bx * s.by + y : s.bx * s.by + y + 1]
    x_ref[0:1] += yz_ref[s.bx : s.bx + 1]
    own = s.own
    spread = jnp.concatenate(
        [own_ref[...], get_split(z_ref, s.z_rows, own), get_split(y_ref, s.y_rows, own), get_split(yz_ref, s.yz_rows, own)], axis=0
    )
    spread_ref[...] = spread
    put_split(x_ref, s.x_rows, spread)
    x_msg_ref[...] = x_ref[...].astype(BF16)


def stacked_totals(s, from_x_ref, spread_ref, x_ref):
    totals = jnp.concatenate([spread_ref[...], get_split(x_ref, s.x_rows, s.half)], axis=0)
    high, low = halves(totals)
    return jnp.concatenate([high, high, low], axis=0).astype(BF16)


def widen(s, received_ref, rows_ref, wide_ref, count):
    rows_ref[...] = received_ref[...].astype(F32)
    wide_ref[:, s.bz :, :] = jnp.zeros((count, s.bzp - s.bz, s.waves), F32)
    for n in range(count):
        wide_ref[n, 0 : s.bz] = rows_ref[n * s.bz : (n + 1) * s.bz]


def image_plane(s, x, block_ref, by_node_ref, stacked, wide_x_ref, wide_y_ref, z_ref, yz_ref, plane_ref):
    image = jnp.dot(by_node_ref[x], stacked, preferred_element_type=F32).reshape(s.by, s.bzp, s.waves)
    plane = image + block_ref[x]
    if x == 0:
        plane = plane + wide_x_ref[...]
    plane_ref[...] = plane
    plane_ref[0] += wide_y_ref[x]
    plane_ref[:, 0, :] += z_ref[x * s.by : (x + 1) * s.by]
    plane_ref[0, 0:1, :] += yz_ref[x : x + 1]


def middle_body(
    s, block_ref, from_x_ref, from_y_ref, from_z_ref, from_yz_ref, spread_ref, by_node_ref, by_atom_ref,
    field_ref, msg_ref, kept_ref, x_ref, y_ref, z_ref, yz_ref, wide_x_ref, wide_y_ref,
):
    widen(s, from_x_ref, x_ref, wide_x_ref, s.by)
    widen(s, from_y_ref, y_ref, wide_y_ref, s.bx)
    z_ref[...] = from_z_ref[...].astype(F32)
    yz_ref[...] = from_yz_ref[...].astype(F32)
    stacked = stacked_totals(s, from_x_ref, spread_ref, x_ref)
    total = jnp.zeros((s.locals, s.waves), F32)
    for x in range(s.bx):
        plane_ref = field_ref.at[x, 0 : s.by]
        image_plane(s, x, block_ref, by_node_ref, stacked, wide_x_ref, wide_y_ref, z_ref, yz_ref, plane_ref)
        total = total + plane_sums(s, by_atom_ref, x, plane_ref[...].reshape(s.by * s.bzp, s.waves))
    send_down_x(s, total, field_ref, x_ref, msg_ref, kept_ref)


def last_body(
    s, start_ref, block_ref, from_x_ref, from_y_ref, from_z_ref, from_yz_ref, spread_ref, by_node_ref,
    out_hbm, x_ref, y_ref, z_ref, yz_ref, wide_x_ref, wide_y_ref, plane_ref, out_ref, sems,
):
    widen(s, from_x_ref, x_ref, wide_x_ref, s.by)
    widen(s, from_y_ref, y_ref, wide_y_ref, s.bx)
    z_ref[...] = from_z_ref[...].astype(F32)
    yz_ref[...] = from_yz_ref[...].astype(F32)
    stacked = stacked_totals(s, from_x_ref, spread_ref, x_ref)
    copies = []
    for x in range(s.bx):
        image_plane(s, x, block_ref, by_node_ref, stacked, wide_x_ref, wide_y_ref, z_ref, yz_ref, plane_ref)
        out_ref[x] = 2.0 * plane_ref[:, 0 : s.bz] - start_ref[x]
        copies.append(pltpu.make_async_copy(out_ref.at[x], out_hbm.at[x], sems.at[x]))
        copies[x].start()
    for copy in copies:
        copy.wait()


def node_of(s, rows):
    return jnp.where(rows % s.group < s.side, rows // s.group * s.side + rows % s.group, -1)


def matrix_body(s, wide_ref, spread_ref, out_ref):
    nodes = wide_ref.shape[3]
    for i in range(s.cells[0]):
        for j in range(s.cells[1]):
            for k in range(s.cells[2]):
                for first in range(0, s.padded, 256):
                    end = min(first + 256, s.padded)
                    low = first // s.group * s.side // 16 * 16
                    high = min(nodes, up_to(-(-end // s.group) * s.side, 16))
                    part = jnp.dot(spread_ref[first:end, low:high], wide_ref[i, j, k, low:high], preferred_element_type=F32)
                    out_ref[i, j, k, first:end] = part.astype(BF16)


def regrouped(s, cell_matrices):
    nodes = cell_matrices.shape[3]
    spread = (node_of(s, lax.iota(jnp.int32, s.padded))[:, None] == lax.iota(jnp.int32, nodes)[None, :]).astype(BF16)
    wide = jnp.einsum("xyzmn,cn->xyzmc", cell_matrices, spread, preferred_element_type=BF16)
    shape = cell_matrices.shape[:3] + (s.padded, s.padded)
    return call(matrix_body, s, [jax.ShapeDtypeStruct(shape, BF16)], [], [wide, spread])[0]


def local(wavefunctions, cell_matrices, projectors, slot_atoms, atom_coupling):
    atom_count = atom_coupling.shape[0]
    devices = 1
    for axis in AXES:
        devices *= lax.axis_size(axis)
    per_device = atom_count // devices
    s = Sizes(wavefunctions.shape, cell_matrices.shape, 8 * per_device)
    weight = lax.dynamic_slice_in_dim(atom_coupling, own_index() * per_device, per_device)
    weight = jnp.broadcast_to(weight[:, None], (per_device, s.waves))
    ids = local_atoms(per_device)[:, None]
    matrices = regrouped(s, cell_matrices)
    x_rows, y_rows, z_rows, yz_rows = (s.scratch(n) for n in (s.x_msg, s.y_msg, s.z_msg, s.yz_msg))
    wide_x, wide_y = s.scratch(s.by, s.bzp), s.scratch(s.bx, s.bzp)
    side_msgs = [s.rows(s.y_msg, BF16), s.rows(s.z_msg, BF16), s.rows(s.yz_msg, BF16)]
    plane = s.by * s.bzp
    field, by_node, by_atom, down_x, kept = call(
        first_body,
        s,
        [
            s.extended(),
            jax.ShapeDtypeStruct((s.bx, plane, 3 * s.locals), BF16),
            jax.ShapeDtypeStruct((s.bx, 2 * s.locals, plane), BF16),
            s.rows(s.x_msg, BF16),
            s.rows(s.half),
        ],
        [
            s.scratch(s.bx, s.by, s.bz),
            pltpu.VMEM(projectors.shape, F32),
            pltpu.VMEM(slot_atoms.shape, jnp.int32),
            pltpu.VMEM((s.bx * s.by * s.bz, 3 * s.locals), F32),
            pltpu.VMEM((s.bx * s.by, s.bzp, 3 * s.locals), F32),
            x_rows,
            pltpu.SemaphoreType.DMA((s.bx,)),
            pltpu.SemaphoreType.DMA((2,)),
        ],
        [wavefunctions, projectors, slot_atoms, ids],
        spaces={0: pltpu.HBM, 1: pltpu.HBM, 2: pltpu.HBM},
    )
    for step in range(2):
        from_x = shifted(down_x, (-1, 0, 0))
        y_msg, z_msg, yz_msg, part = call(
            down_body, s, side_msgs + [s.rows(s.own)], [x_rows, y_rows, z_rows, yz_rows], [field, from_x, kept]
        )
        from_y = shifted(y_msg, (0, -1, 0))
        from_z = shifted(z_msg, (0, 0, -1))
        from_yz = shifted(yz_msg, (0, -1, -1))
        field, block, y_msg, z_msg, yz_msg, own = call(
            cell_body,
            s,
            [s.extended(), jax.ShapeDtypeStruct((s.bx + 1, s.by, s.bzp, s.waves), F32)] + side_msgs + [s.rows(s.own)],
            [s.scratch(s.cells[2], s.bx + 1, s.by + 1, s.group), x_rows, y_rows, z_rows, yz_rows],
            [field, matrices, from_x, from_y, from_z, from_yz, part, weight],
            aliases={0: 0},
        )
        from_y = shifted(y_msg, (0, 1, 0))
        from_z = shifted(z_msg, (0, 0, 1))
        from_yz = shifted(yz_msg, (0, 1, 1))
        up_x, spread = call(
            up_body,
            s,
            [s.rows(s.x_msg, BF16), s.rows(s.half)],
            [x_rows, y_rows, z_rows, yz_rows],
            [block, from_y, from_z, from_yz, own],
        )
        from_x = shifted(up_x, (1, 0, 0))
        scratch = [x_rows, y_rows, z_rows, yz_rows, wide_x, wide_y]
        received = [block, from_x, from_y, from_z, from_yz, spread, by_node]
        if step == 0:
            field, down_x, kept = call(
                middle_body, s, [s.extended(), s.rows(s.x_msg, BF16), s.rows(s.half)], scratch, received + [by_atom]
            )
        else:
            (out,) = call(
                last_body,
                s,
                [jax.ShapeDtypeStruct(wavefunctions.shape, F32)],
                scratch
                + [s.scratch(s.by, s.bzp)]
                + [s.scratch(s.bx, s.by, s.bz), pltpu.SemaphoreType.DMA((s.bx,))],
                [wavefunctions] + received,
                out_spaces={0: pltpu.HBM},
            )
    return out


def solution(mesh):
    return jax.shard_map(
        local,
        mesh=mesh,
        in_specs=(
            P("gx", "gy", "gz", None),
            P("gx", "gy", "gz", None, None),
            P(("gx", "gy", "gz"), None, None),
            P(("gx", "gy", "gz"), None),
            P(),
        ),
        out_specs=P("gx", "gy", "gz", None),
        check_vma=False,
    )
```

```python
import functools

import jax
import jax.numpy as jnp
from jax import lax
from jax.experimental import pallas as pl
from jax.experimental.pallas import tpu as pltpu
from jax.sharding import PartitionSpec as P

AXES = ("gx", "gy", "gz")
F32 = jnp.float32
BF16 = jnp.bfloat16
LIMIT = 12 * 1024 * 1024


def up_to(value, unit):
    return -(-value // unit) * unit


def shifted(value, shift):
    sizes = [lax.axis_size(axis) for axis in AXES]
    pairs = []
    for x in range(sizes[0]):
        for y in range(sizes[1]):
            for z in range(sizes[2]):
                here = (x * sizes[1] + y) * sizes[2] + z
                there = [(p + s) % n for p, s, n in zip((x, y, z), shift, sizes)]
                pairs.append((here, (there[0] * sizes[1] + there[1]) * sizes[2] + there[2]))
    return lax.ppermute(value, AXES, pairs)


def halves(value):
    high = value.astype(BF16).astype(F32)
    return high, value - high


def put_split(rows_ref, start, value):
    count = value.shape[0]
    high, low = halves(value)
    rows_ref[start : start + count] = high
    rows_ref[start + count : start + 2 * count] = low


def get_split(rows_ref, start, count):
    return rows_ref[start : start + count] + rows_ref[start + count : start + 2 * count]


class Sizes:
    def __init__(self, field_shape, cell_shape, locals_count):
        self.bx, self.by, self.bz, self.waves = field_shape
        self.cells = cell_shape[:3]
        self.order = self.bx // cell_shape[0]
        self.side = self.order + 1
        self.group = up_to(self.side, 8)
        self.padded = up_to(self.side * self.side * self.group, 16)
        self.bzp = up_to(max(self.bz + 1, (cell_shape[2] - 1) * self.order + self.group), 16)
        self.locals = locals_count
        self.few = max(n for n in (1, 2, 3, 4) if self.bx % n == 0)
        self.half = locals_count // 2
        self.quarter = locals_count // 4
        self.own = locals_count // 8
        self.x_rows = self.by * self.bz
        self.y_rows = (self.bx + 1) * self.bz
        self.z_rows = (self.bx + 1) * self.by
        self.yz_rows = self.bx + 1
        self.x_msg = up_to(self.x_rows + 2 * self.half, 16)
        self.y_msg = up_to(self.y_rows + 2 * self.own, 16)
        self.z_msg = up_to(self.z_rows + 2 * self.own, 16)
        self.yz_msg = up_to(self.yz_rows + 2 * self.own, 16)
        self.nodes_padded = self.bx * self.by * self.bzp

    def extended(self):
        return jax.ShapeDtypeStruct((self.bx + 1, self.by + 1, self.bzp, self.waves), F32)

    def rows(self, count, dtype=F32):
        return jax.ShapeDtypeStruct((count, self.waves), dtype)

    def scratch(self, *shape):
        return pltpu.VMEM(shape + (self.waves,), F32)


VMEM = pltpu.VMEM


def call(body, sizes, outs, scratch, args, spaces=None, out_spaces=None, aliases=None, extra=()):
    spaces = spaces or {}
    out_spaces = out_spaces or {}
    outs = [out_spaces.get(n, VMEM)(out.shape, out.dtype) for n, out in enumerate(outs)]
    args = [pltpu.with_memory_space_constraint(arg, spaces.get(n, VMEM)) for n, arg in enumerate(args)]
    return pl.pallas_call(
        functools.partial(body, sizes, *extra),
        out_shape=outs,
        in_specs=[pl.BlockSpec(memory_space=spaces.get(n, VMEM)) for n in range(len(args))],
        out_specs=[pl.BlockSpec(memory_space=out_spaces.get(n, VMEM)) for n in range(len(outs))],
        scratch_shapes=scratch,
        input_output_aliases=aliases or {},
        compiler_params=pltpu.CompilerParams(vmem_limit_bytes=LIMIT),
    )(*args)


def local_atoms(own):
    sizes = [lax.axis_size(axis) for axis in AXES]
    here = [lax.axis_index(axis) for axis in AXES]
    ids = []
    for dx in range(2):
        for dy in range(2):
            for dz in range(2):
                x, y, z = (lax.rem(h + n - d, n) for h, n, d in zip(here, sizes, (dx, dy, dz)))
                owner = (x * sizes[1] + y) * sizes[2] + z
                ids += [owner * own + a for a in range(own)]
    return jnp.stack(ids).astype(jnp.int32)


def put_face(s, rows_ref, field_ref):
    for y in range(s.by):
        rows_ref[y * s.bz : (y + 1) * s.bz] = field_ref[0, y, 0 : s.bz]


def plane_sums(s, by_atom_ref, x, plane):
    high = plane.astype(BF16)
    low = (plane - high.astype(F32)).astype(BF16)
    with_high = jnp.dot(by_atom_ref[x], high, preferred_element_type=F32)
    with_low = jnp.dot(by_atom_ref[x, 0 : s.locals], low, preferred_element_type=F32)
    return with_high[0 : s.locals] + with_high[s.locals : 2 * s.locals] + with_low


def send_down_x(s, total, field_ref, rows_ref, msg_ref, kept_ref):
    kept_ref[...] = total[0 : s.half]
    put_face(s, rows_ref, field_ref)
    rows_ref[s.x_rows :] = jnp.zeros((s.x_msg - s.x_rows, s.waves), F32)
    put_split(rows_ref, s.x_rows, total[s.half : 2 * s.half])
    msg_ref[...] = rows_ref[...].astype(BF16)


def first_body(
    s, start_hbm, rows_hbm, slots_hbm, coupling_hbm, ids_ref,
    field_ref, by_node_ref, by_atom_ref, msg_ref, kept_ref, weight_ref,
    start_ref, rows_ref, slots_ref, coupling_ref, tall_ref, wide_ref, x_ref, sems, small_sems,
):
    small = [
        pltpu.make_async_copy(rows_hbm, rows_ref, small_sems.at[0]),
        pltpu.make_async_copy(slots_hbm, slots_ref, small_sems.at[1]),
        pltpu.make_async_copy(coupling_hbm, coupling_ref, small_sems.at[2]),
    ]
    for copy in small:
        copy.start()
    few = s.few
    copies = []
    for n in range(s.bx // few):
        span = pl.ds(n * few, few)
        copies.append(pltpu.make_async_copy(start_hbm.at[span], start_ref.at[span], sems.at[n]))
        copies[n].start()
    for copy in small:
        copy.wait()
    selector = (ids_ref[...] == slots_ref[...]).astype(F32)
    rows = jnp.dot(selector, rows_ref[0], precision=lax.Precision.HIGHEST, preferred_element_type=F32)
    high, low = halves(rows)
    low = low.astype(BF16).astype(F32)
    tall_ref[...] = jnp.concatenate([high, low, high], axis=0).T
    wide_ref[:, s.bz : s.bzp, :] = jnp.zeros((s.bx * s.by, s.bzp - s.bz, 3 * s.locals), F32)
    for g in range(s.bx * s.by):
        wide_ref[g, 0 : s.bz, :] = tall_ref[g * s.bz : (g + 1) * s.bz, :]
    for x in range(s.bx):
        wide = wide_ref[x * s.by : (x + 1) * s.by].reshape(s.by * s.bzp, 3 * s.locals)
        by_node_ref[x] = wide.astype(BF16)
        by_atom_ref[x] = wide.T[0 : 2 * s.locals].astype(BF16)
    total = jnp.zeros((s.locals, s.waves), F32)
    for n in range(s.bx // few):
        copies[n].wait()
        planes = start_ref[n * few : (n + 1) * few]
        planes = jnp.concatenate([planes, jnp.zeros((few, s.by, s.bzp - s.bz, s.waves), F32)], axis=2)
        field_ref[n * few : (n + 1) * few, 0 : s.by] = planes
        for x in range(few):
            total = total + plane_sums(s, by_atom_ref, n * few + x, planes[x].reshape(s.by * s.bzp, s.waves))
    send_down_x(s, total, field_ref, x_ref, msg_ref, kept_ref)
    atoms = lax.broadcasted_iota(jnp.int32, (s.own, coupling_ref.shape[1]), 1)
    weight = jnp.sum(jnp.where(atoms == ids_ref[0 : s.own], coupling_ref[...], 0.0), axis=1, keepdims=True)
    weight_ref[...] = jnp.broadcast_to(weight, weight_ref.shape)


def down_body(s, field_ref, from_x_ref, kept_ref, early_ref, y_msg_ref, z_msg_ref, yz_msg_ref, part_ref, x_ref, y_ref, z_ref, yz_ref):
    del early_ref
    x_ref[...] = from_x_ref[...].astype(F32)
    total = kept_ref[...] + get_split(x_ref, s.x_rows, s.half)
    for ref, used in ((y_ref, s.y_rows), (z_ref, s.z_rows), (yz_ref, s.yz_rows)):
        ref[used:] = jnp.zeros((ref.shape[0] - used, s.waves), F32)
    for x in range(s.bx):
        y_ref[x * s.bz : (x + 1) * s.bz] = field_ref[x, 0, 0 : s.bz]
        z_ref[x * s.by : (x + 1) * s.by] = field_ref[x, 0 : s.by, 0, :]
        yz_ref[x : x + 1] = field_ref[x, 0, 0:1, :]
    y_ref[s.bx * s.bz : s.y_rows] = x_ref[0 : s.bz]
    for y in range(s.by):
        z_ref[s.bx * s.by + y : s.bx * s.by + y + 1] = x_ref[y * s.bz : y * s.bz + 1]
    yz_ref[s.bx : s.bx + 1] = x_ref[0:1]
    own = s.own
    part_ref[...] = total[0:own]
    put_split(z_ref, s.z_rows, total[own : 2 * own])
    put_split(y_ref, s.y_rows, total[2 * own : 3 * own])
    put_split(yz_ref, s.yz_rows, total[3 * own : 4 * own])
    y_msg_ref[...] = y_ref[...].astype(BF16)
    z_msg_ref[...] = z_ref[...].astype(BF16)
    yz_msg_ref[...] = yz_ref[...].astype(BF16)


def cell_body(
    s, before_ref, from_x_ref, from_y_ref, from_z_ref, from_yz_ref, part_ref, weight_ref, *refs
):
    matrix_refs, refs = refs[: s.cells[0]], refs[s.cells[0] :]
    (field_ref, block_ref, y_msg_ref, z_msg_ref, yz_msg_ref, own_ref,
     sums_ref, x_ref, y_ref, z_ref, yz_ref) = refs
    del before_ref
    order, side, group = s.order, s.side, s.group
    cells_x, cells_y, cells_z = s.cells
    x_ref[...] = from_x_ref[...].astype(F32)
    y_ref[...] = from_y_ref[...].astype(F32)
    z_ref[...] = from_z_ref[...].astype(F32)
    yz_ref[...] = from_yz_ref[...].astype(F32)
    rest = jnp.zeros((s.bzp - s.bz, s.waves), F32)
    for y in range(s.by):
        field_ref[s.bx, y, 0 : s.bz, :] = x_ref[y * s.bz : (y + 1) * s.bz]
        field_ref[s.bx, y, s.bz :, :] = rest
    for x in range(s.bx + 1):
        field_ref[x, s.by, 0 : s.bz, :] = y_ref[x * s.bz : (x + 1) * s.bz]
        field_ref[x, s.by, s.bz :, :] = rest
        field_ref[x, 0 : s.by, s.bz, :] = z_ref[x * s.by : (x + 1) * s.by]
        field_ref[x, s.by, s.bz : s.bz + 1, :] = yz_ref[x : x + 1]
    used = side * side * group
    for i in range(cells_x):
        for j in range(cells_y):
            for k in range(cells_z):
                first = k * order
                values = field_ref[i * order : i * order + side, j * order : j * order + side, first : first + group]
                values = values.reshape(used, s.waves)
                if s.padded > used:
                    values = jnp.concatenate([values, jnp.zeros((s.padded - used, s.waves), F32)], axis=0)
                product = jnp.dot(matrix_refs[i][j, k], values.astype(BF16), preferred_element_type=F32)
                product = product[0:used].reshape(side, side, group, s.waves)
                x0, x1, y0, y1 = i * order, i * order + side, j * order, j * order + side
                a, b = int(i > 0), int(j > 0)
                sums_ref[k, x0 + a : x1, y0 + b : y1] = product[a:, b:]
                if a:
                    sums_ref[k, x0, y0 + b : y1] += product[0, b:]
                if b:
                    sums_ref[k, x0 + a : x1, y0] += product[a:, 0]
                if a and b:
                    sums_ref[k, x0, y0] += product[0, 0]
    own = s.own
    total = part_ref[...] + get_split(z_ref, s.z_rows, own) + get_split(y_ref, s.y_rows, own) + get_split(yz_ref, s.yz_rows, own)
    total = total * weight_ref[...]
    own_ref[...] = total
    last = cells_z - 1
    for x in range(s.bx + 1):
        z_ref[x * s.by : (x + 1) * s.by] = sums_ref[last, x, 0 : s.by, order, :]
        yz_ref[x : x + 1] = sums_ref[last, x, s.by, order : order + 1, :]
        for k in range(cells_z):
            at = x * s.bz + k * order
            y_ref[at : at + order] = sums_ref[k, x, s.by, 0:order, :]
            if k:
                y_ref[at : at + 1] += sums_ref[k - 1, x, s.by, order : order + 1, :]
    put_split(y_ref, s.y_rows, total)
    put_split(z_ref, s.z_rows, total)
    put_split(yz_ref, s.yz_rows, total)
    y_msg_ref[...] = y_ref[...].astype(BF16)
    z_msg_ref[...] = z_ref[...].astype(BF16)
    yz_msg_ref[...] = yz_ref[...].astype(BF16)
    for x in range(s.bx + 1):
        block_ref[x, :, 0:group, :] = sums_ref[0, x, 0 : s.by]
        block_ref[x, :, group:, :] = jnp.zeros((s.by, s.bzp - group, s.waves), F32)
        for k in range(1, cells_z):
            block_ref[x, :, k * order : k * order + group, :] += sums_ref[k, x, 0 : s.by]


def up_body(s, block_ref, from_y_ref, from_z_ref, from_yz_ref, own_ref, x_msg_ref, spread_ref, x_ref, y_ref, z_ref, yz_ref):
    y_ref[...] = from_y_ref[...].astype(F32)
    z_ref[...] = from_z_ref[...].astype(F32)
    yz_ref[...] = from_yz_ref[...].astype(F32)
    x_ref[s.x_rows :] = jnp.zeros((s.x_msg - s.x_rows, s.waves), F32)
    for y in range(s.by):
        x_ref[y * s.bz : (y + 1) * s.bz] = block_ref[s.bx, y, 0 : s.bz]
    x_ref[0 : s.bz] += y_ref[s.bx * s.bz : s.y_rows]
    for y in range(s.by):
        x_ref[y * s.bz : y * s.bz + 1] += z_ref[s.bx * s.by + y : s.bx * s.by + y + 1]
    x_ref[0:1] += yz_ref[s.bx : s.bx + 1]
    own = s.own
    spread = jnp.concatenate(
        [own_ref[...], get_split(z_ref, s.z_rows, own), get_split(y_ref, s.y_rows, own), get_split(yz_ref, s.yz_rows, own)], axis=0
    )
    spread_ref[...] = spread
    put_split(x_ref, s.x_rows, spread)
    x_msg_ref[...] = x_ref[...].astype(BF16)


def stacked_totals(s, from_x_ref, spread_ref, x_ref):
    totals = jnp.concatenate([spread_ref[...], get_split(x_ref, s.x_rows, s.half)], axis=0)
    high, low = halves(totals)
    return jnp.concatenate([high, high, low], axis=0).astype(BF16)


def widen(s, received_ref, rows_ref, wide_ref, count):
    rows_ref[...] = received_ref[...].astype(F32)
    wide_ref[:, s.bz :, :] = jnp.zeros((count, s.bzp - s.bz, s.waves), F32)
    for n in range(count):
        wide_ref[n, 0 : s.bz] = rows_ref[n * s.bz : (n + 1) * s.bz]


def image_plane(s, x, block_ref, by_node_ref, stacked, wide_x_ref, wide_y_ref, z_ref, yz_ref, plane_ref):
    image = jnp.dot(by_node_ref[x], stacked, preferred_element_type=F32).reshape(s.by, s.bzp, s.waves)
    plane = image + block_ref[x]
    if x == 0:
        plane = plane + wide_x_ref[...]
    plane_ref[...] = plane
    plane_ref[0] += wide_y_ref[x]
    plane_ref[:, 0, :] += z_ref[x * s.by : (x + 1) * s.by]
    plane_ref[0, 0:1, :] += yz_ref[x : x + 1]


def middle_body(
    s, block_ref, from_x_ref, from_y_ref, from_z_ref, from_yz_ref, spread_ref, by_node_ref, by_atom_ref,
    field_ref, msg_ref, kept_ref, x_ref, y_ref, z_ref, yz_ref, wide_x_ref, wide_y_ref,
):
    widen(s, from_x_ref, x_ref, wide_x_ref, s.by)
    widen(s, from_y_ref, y_ref, wide_y_ref, s.bx)
    z_ref[...] = from_z_ref[...].astype(F32)
    yz_ref[...] = from_yz_ref[...].astype(F32)
    stacked = stacked_totals(s, from_x_ref, spread_ref, x_ref)
    total = jnp.zeros((s.locals, s.waves), F32)
    for x in range(s.bx):
        plane_ref = field_ref.at[x, 0 : s.by]
        image_plane(s, x, block_ref, by_node_ref, stacked, wide_x_ref, wide_y_ref, z_ref, yz_ref, plane_ref)
        total = total + plane_sums(s, by_atom_ref, x, plane_ref[...].reshape(s.by * s.bzp, s.waves))
    send_down_x(s, total, field_ref, x_ref, msg_ref, kept_ref)


def last_body(
    s, start_ref, block_ref, from_x_ref, from_y_ref, from_z_ref, from_yz_ref, spread_ref, by_node_ref,
    out_hbm, x_ref, y_ref, z_ref, yz_ref, wide_x_ref, wide_y_ref, plane_ref, out_ref, sems,
):
    widen(s, from_x_ref, x_ref, wide_x_ref, s.by)
    widen(s, from_y_ref, y_ref, wide_y_ref, s.bx)
    z_ref[...] = from_z_ref[...].astype(F32)
    yz_ref[...] = from_yz_ref[...].astype(F32)
    stacked = stacked_totals(s, from_x_ref, spread_ref, x_ref)
    copies = []
    for x in range(s.bx):
        image_plane(s, x, block_ref, by_node_ref, stacked, wide_x_ref, wide_y_ref, z_ref, yz_ref, plane_ref)
        out_ref[x] = 2.0 * plane_ref[:, 0 : s.bz] - start_ref[x]
        copies.append(pltpu.make_async_copy(out_ref.at[x], out_hbm.at[x], sems.at[x]))
        copies[x].start()
    for copy in copies:
        copy.wait()


def selector(count, chosen):
    row = lax.broadcasted_iota(jnp.int32, count, 0)
    column = lax.broadcasted_iota(jnp.int32, count, 1)
    return chosen(row, column).astype(F32).astype(BF16)


def matrix_body(s, part, matrix_hbm, out_ref, raw_ref, flat_ref, half_ref, sems):
    cells_y, cells_z = s.cells[1:]
    side, group = s.side, s.group
    nodes = side**3
    copies = [pltpu.make_async_copy(matrix_hbm.at[part, j], raw_ref.at[j], sems.at[j]) for j in range(cells_y)]
    for copy in copies:
        copy.start()
    wide = 256 // group * side
    spans = []
    for first in range(0, s.padded, 256):
        low = first // group * side // 128 * 128
        high = min(nodes, first // group * side + wide)
        width = min(256, s.padded - first)
        spans.append((first, low, high, selector((high - low, width), lambda m, c, low=low, first=first: (
            ((c + first) % group < side) & (m + low == (c + first) // group * side + (c + first) % group)))))
    tall = 128 // group * side
    picks = jnp.concatenate(
        [
            selector((128, tall * cells_z), lambda r, m, k=k: (r % group < side) & (m == (r // group * side + r % group) * cells_z + k))
            for k in range(cells_z)
        ],
        axis=0,
    )
    for j in range(cells_y):
        copies[j].wait()
        flat_ref[...] = raw_ref[j].reshape(nodes * cells_z, nodes)
        for first, low, high, spread in spans:
            half = jnp.dot(flat_ref[:, low:high], spread, preferred_element_type=F32)
            half_ref[:, first : first + spread.shape[1]] = half.astype(BF16)
        for first in range(0, s.padded, 128):
            count = min(128, s.padded - first)
            low = first // group * side * cells_z
            high = min(nodes * cells_z, low + tall * cells_z)
            rows = jnp.dot(picks[:, 0 : high - low], half_ref[low:high], preferred_element_type=F32).astype(BF16)
            for k in range(cells_z):
                out_ref[j, k, first : first + count] = rows[128 * k : 128 * k + count]


def regrouped(s, cell_matrices, part):
    shape = cell_matrices.shape
    nodes = shape[3]
    return call(
        matrix_body,
        s,
        [jax.ShapeDtypeStruct(shape[1:3] + (s.padded, s.padded), BF16)],
        [
            pltpu.VMEM((shape[1], nodes, shape[2], nodes), BF16),
            pltpu.VMEM((nodes * shape[2], nodes), BF16),
            pltpu.VMEM((nodes * shape[2], s.padded), BF16),
            pltpu.SemaphoreType.DMA((shape[1],)),
        ],
        [cell_matrices.transpose(0, 1, 3, 2, 4)],
        spaces={0: pltpu.HBM},
        extra=(part,),
    )[0]


def local(wavefunctions, cell_matrices, projectors, slot_atoms, atom_coupling):
    atom_count = atom_coupling.shape[0]
    devices = 1
    for axis in AXES:
        devices *= lax.axis_size(axis)
    per_device = atom_count // devices
    s = Sizes(wavefunctions.shape, cell_matrices.shape, 8 * per_device)
    ids = local_atoms(per_device)[:, None]
    matrices = [regrouped(s, cell_matrices, part) for part in range(s.cells[0])]
    x_rows, y_rows, z_rows, yz_rows = (s.scratch(n) for n in (s.x_msg, s.y_msg, s.z_msg, s.yz_msg))
    wide_x, wide_y = s.scratch(s.by, s.bzp), s.scratch(s.bx, s.bzp)
    side_msgs = [s.rows(s.y_msg, BF16), s.rows(s.z_msg, BF16), s.rows(s.yz_msg, BF16)]
    plane = s.by * s.bzp
    field, by_node, by_atom, down_x, kept, weight = call(
        first_body,
        s,
        [
            s.extended(),
            jax.ShapeDtypeStruct((s.bx, plane, 3 * s.locals), BF16),
            jax.ShapeDtypeStruct((s.bx, 2 * s.locals, plane), BF16),
            s.rows(s.x_msg, BF16),
            s.rows(s.half),
            s.rows(s.own),
        ],
        [
            s.scratch(s.bx, s.by, s.bz),
            pltpu.VMEM(projectors.shape, F32),
            pltpu.VMEM(slot_atoms.shape, jnp.int32),
            pltpu.VMEM((1, atom_count), F32),
            pltpu.VMEM((s.bx * s.by * s.bz, 3 * s.locals), F32),
            pltpu.VMEM((s.bx * s.by, s.bzp, 3 * s.locals), F32),
            x_rows,
            pltpu.SemaphoreType.DMA((s.bx,)),
            pltpu.SemaphoreType.DMA((3,)),
        ],
        [wavefunctions, projectors, slot_atoms, atom_coupling[None, :], ids],
        spaces={0: pltpu.HBM, 1: pltpu.HBM, 2: pltpu.HBM, 3: pltpu.HBM},
    )
    for step in range(2):
        from_x = shifted(down_x, (-1, 0, 0))
        y_msg, z_msg, yz_msg, part = call(
            down_body, s, side_msgs + [s.rows(s.own)], [x_rows, y_rows, z_rows, yz_rows], [field, from_x, kept, matrices[0]]
        )
        from_y = shifted(y_msg, (0, -1, 0))
        from_z = shifted(z_msg, (0, 0, -1))
        from_yz = shifted(yz_msg, (0, -1, -1))
        field, block, y_msg, z_msg, yz_msg, own = call(
            cell_body,
            s,
            [s.extended(), jax.ShapeDtypeStruct((s.bx + 1, s.by, s.bzp, s.waves), F32)] + side_msgs + [s.rows(s.own)],
            [s.scratch(s.cells[2], s.bx + 1, s.by + 1, s.group), x_rows, y_rows, z_rows, yz_rows],
            [field, from_x, from_y, from_z, from_yz, part, weight] + matrices,
            aliases={0: 0},
        )
        from_y = shifted(y_msg, (0, 1, 0))
        from_z = shifted(z_msg, (0, 0, 1))
        from_yz = shifted(yz_msg, (0, 1, 1))
        up_x, spread = call(
            up_body,
            s,
            [s.rows(s.x_msg, BF16), s.rows(s.half)],
            [x_rows, y_rows, z_rows, yz_rows],
            [block, from_y, from_z, from_yz, own],
        )
        from_x = shifted(up_x, (1, 0, 0))
        scratch = [x_rows, y_rows, z_rows, yz_rows, wide_x, wide_y]
        received = [block, from_x, from_y, from_z, from_yz, spread, by_node]
        if step == 0:
            field, down_x, kept = call(
                middle_body, s, [s.extended(), s.rows(s.x_msg, BF16), s.rows(s.half)], scratch, received + [by_atom]
            )
        else:
            (out,) = call(
                last_body,
                s,
                [jax.ShapeDtypeStruct(wavefunctions.shape, F32)],
                scratch
                + [s.scratch(s.by, s.bzp)]
                + [s.scratch(s.bx, s.by, s.bz), pltpu.SemaphoreType.DMA((s.bx,))],
                [wavefunctions] + received,
                out_spaces={0: pltpu.HBM},
            )
    return out


def solution(mesh):
    return jax.shard_map(
        local,
        mesh=mesh,
        in_specs=(
            P("gx", "gy", "gz", None),
            P("gx", "gy", "gz", None, None),
            P(("gx", "gy", "gz"), None, None),
            P(("gx", "gy", "gz"), None),
            P(),
        ),
        out_specs=P("gx", "gy", "gz", None),
        check_vma=False,
    )
```

```python
import functools

import jax
import jax.numpy as jnp
from jax import lax
from jax.experimental import pallas as pl
from jax.experimental.pallas import tpu as pltpu
from jax.sharding import PartitionSpec as P

AXES = ("gx", "gy", "gz")
F32 = jnp.float32
BF16 = jnp.bfloat16
LIMIT = 12 * 1024 * 1024


def up_to(value, unit):
    return -(-value // unit) * unit


def shifted(value, shift):
    sizes = [lax.axis_size(axis) for axis in AXES]
    pairs = []
    for x in range(sizes[0]):
        for y in range(sizes[1]):
            for z in range(sizes[2]):
                here = (x * sizes[1] + y) * sizes[2] + z
                there = [(p + s) % n for p, s, n in zip((x, y, z), shift, sizes)]
                pairs.append((here, (there[0] * sizes[1] + there[1]) * sizes[2] + there[2]))
    return lax.ppermute(value, AXES, pairs)


def halves(value):
    high = value.astype(BF16).astype(F32)
    return high, value - high


def put_split(rows_ref, start, value):
    count = value.shape[0]
    high, low = halves(value)
    rows_ref[start : start + count] = high
    rows_ref[start + count : start + 2 * count] = low


def get_split(rows_ref, start, count):
    return rows_ref[start : start + count] + rows_ref[start + count : start + 2 * count]


class Sizes:
    def __init__(self, field_shape, cell_shape, own, pairs):
        self.bx, self.by, self.bz, self.waves = field_shape
        self.cells = cell_shape[:3]
        self.order = self.bx // cell_shape[0]
        self.side = self.order + 1
        self.group = up_to(self.side, 8)
        self.padded = up_to(self.side * self.side * self.group, 16)
        self.bzp = up_to(max(self.bz + 1, (cell_shape[2] - 1) * self.order + self.group), 16)
        self.few = max(n for n in (1, 2, 3, 4) if self.bx % n == 0)
        self.pairs = pairs
        self.own = own
        self.locals = 8 * own
        self.span = self.bz + 1
        self.z_rows = self.bx * self.by
        self.x_rows = self.by * self.span
        self.y_rows = self.bx * self.span
        self.x_msg = up_to(self.x_rows + 4 * own, 16)
        self.y_msg = up_to(self.y_rows + 4 * own, 16)
        self.xy_msg = up_to(self.span + 4 * own, 16)
        self.z_plane = up_to(self.z_rows, 16)
        self.z_sums = up_to(8 * own, 16)
        self.z_both = up_to(self.z_rows + 8 * own, 16)

    def extended(self):
        return jax.ShapeDtypeStruct((self.bx + 1, self.by + 1, self.bzp, self.waves), F32)

    def block(self):
        return jax.ShapeDtypeStruct((self.bx, self.by, self.bzp, self.waves), F32)

    def rows(self, count, dtype=F32):
        return jax.ShapeDtypeStruct((count, self.waves), dtype)

    def scratch(self, *shape):
        return pltpu.VMEM(shape + (self.waves,), F32)

    def z_msgs(self, down, up):
        return [self.rows(down + up, BF16)] if self.pairs else [self.rows(down, BF16), self.rows(up, BF16)]

    def side_msgs(self):
        return [self.rows(n, BF16) for n in (self.x_msg, self.y_msg, self.xy_msg)]

    def side_rows(self):
        return [self.scratch(n) for n in (self.x_msg, self.y_msg, self.xy_msg)]


VMEM = pltpu.VMEM


def call(body, sizes, outs, scratch, args, spaces=None, out_spaces=None, aliases=None, extra=()):
    spaces = spaces or {}
    out_spaces = out_spaces or {}
    outs = [out_spaces.get(n, VMEM)(out.shape, out.dtype) for n, out in enumerate(outs)]
    args = [pltpu.with_memory_space_constraint(arg, spaces.get(n, VMEM)) for n, arg in enumerate(args)]
    return pl.pallas_call(
        functools.partial(body, sizes, *extra),
        out_shape=outs,
        in_specs=[pl.BlockSpec(memory_space=spaces.get(n, VMEM)) for n in range(len(args))],
        out_specs=[pl.BlockSpec(memory_space=out_spaces.get(n, VMEM)) for n in range(len(outs))],
        scratch_shapes=scratch,
        input_output_aliases=aliases or {},
        compiler_params=pltpu.CompilerParams(vmem_limit_bytes=LIMIT),
    )(*args)


def local_atoms(own):
    sizes = [lax.axis_size(axis) for axis in AXES]
    here = [lax.axis_index(axis) for axis in AXES]
    ids = []
    for dz in (1, 0):
        for dx in (1, 0):
            for dy in (1, 0):
                x, y, z = (lax.rem(h + n - d, n) for h, n, d in zip(here, sizes, (dx, dy, dz)))
                owner = (x * sizes[1] + y) * sizes[2] + z
                ids += [owner * own + a for a in range(own)]
    return jnp.stack(ids).astype(jnp.int32)


def blank(rows_ref, first):
    count = rows_ref.shape[0] - first
    if count:
        rows_ref[first:] = jnp.zeros((count,) + rows_ref.shape[1:], F32)


def split_sums(by_atom, count, field):
    high = field.astype(BF16)
    low = (field - high.astype(F32)).astype(BF16)
    with_high = jnp.dot(by_atom, high, preferred_element_type=F32)
    with_low = jnp.dot(by_atom[0:count], low, preferred_element_type=F32)
    return with_high[0:count] + with_high[count : 2 * count] + with_low


def put_z(s, msg_refs, down_ref, up_ref):
    if s.pairs:
        count = down_ref.shape[0]
        msg_refs[0][0:count] = down_ref[...].astype(BF16)
        msg_refs[0][count:] = up_ref[...].astype(BF16)
    else:
        msg_refs[0][...] = down_ref[...].astype(BF16)
        msg_refs[1][...] = up_ref[...].astype(BF16)


def get_z(s, msg_refs, above_ref, below_ref):
    if s.pairs:
        count = above_ref.shape[0]
        above_ref[...] = msg_refs[0][0:count].astype(F32)
        below_ref[...] = msg_refs[0][count:].astype(F32)
    else:
        above_ref[...] = msg_refs[0][...].astype(F32)
        below_ref[...] = msg_refs[1][...].astype(F32)


def columns(s, totals):
    own, half = s.own, 4 * s.own
    return [
        jnp.concatenate([totals[n * own : (n + 1) * own], totals[half + n * own : half + (n + 1) * own]], axis=0) for n in range(4)
    ]


def from_columns(s, parts):
    own = s.own
    return jnp.concatenate([part[0:own] for part in parts] + [part[own : 2 * own] for part in parts], axis=0)


def first_body(
    s, start_hbm, rows_hbm, slots_hbm, coupling_hbm, ids_ref,
    field_ref, by_node_ref, by_atom_ref, line_ref, *refs
):
    *msg_refs, total_ref, weight_ref, start_ref, rows_ref, slots_ref, coupling_ref, tall_ref, wide_ref, low_ref, high_ref, sems, small_sems = refs
    small = [
        pltpu.make_async_copy(rows_hbm, rows_ref, small_sems.at[0]),
        pltpu.make_async_copy(slots_hbm, slots_ref, small_sems.at[1]),
        pltpu.make_async_copy(coupling_hbm, coupling_ref, small_sems.at[2]),
    ]
    for copy in small:
        copy.start()
    few = s.few
    copies = []
    for n in range(s.bx // few):
        span = pl.ds(n * few, few)
        copies.append(pltpu.make_async_copy(start_hbm.at[span], start_ref.at[span], sems.at[n]))
        copies[n].start()
    for copy in small:
        copy.wait()
    selector = (ids_ref[...] == slots_ref[...]).astype(F32)
    rows = jnp.dot(selector, rows_ref[0], precision=lax.Precision.HIGHEST, preferred_element_type=F32)
    high, low = halves(rows)
    low = low.astype(BF16).astype(F32)
    tall_ref[...] = jnp.concatenate([high, low, high], axis=0).T
    wide_ref[:, s.bz : s.bzp, :] = jnp.zeros((s.bx * s.by, s.bzp - s.bz, 3 * s.locals), F32)
    for g in range(s.bx * s.by):
        wide_ref[g, 0 : s.bz, :] = tall_ref[g * s.bz : (g + 1) * s.bz, :]
    for x in range(s.bx):
        wide = wide_ref[x * s.by : (x + 1) * s.by].reshape(s.by * s.bzp, 3 * s.locals)
        by_node_ref[x] = wide.astype(BF16)
        by_atom_ref[x] = wide.T[0 : 2 * s.locals].astype(BF16)
    line_ref[...] = wide_ref[:, 0, :]
    total = jnp.zeros((s.locals, s.waves), F32)
    for n in range(s.bx // few):
        copies[n].wait()
        planes = start_ref[n * few : (n + 1) * few]
        planes = jnp.concatenate([planes, jnp.zeros((few, s.by, s.bzp - s.bz, s.waves), F32)], axis=2)
        field_ref[n * few : (n + 1) * few, 0 : s.by] = planes
        for x in range(few):
            total = total + split_sums(by_atom_ref[n * few + x], s.locals, planes[x].reshape(s.by * s.bzp, s.waves))
    total_ref[...] = total
    half = 4 * s.own
    for x in range(s.bx):
        low_ref[x * s.by : (x + 1) * s.by] = field_ref[x, 0 : s.by, 0, :]
    blank(low_ref, s.z_rows)
    blank(high_ref, 0)
    put_split(low_ref, s.z_rows, total[0:half])
    put_split(high_ref, 0, total[half:])
    put_z(s, msg_refs, low_ref, high_ref)
    atoms = lax.broadcasted_iota(jnp.int32, (s.locals, coupling_ref.shape[1]), 1)
    weight = jnp.sum(jnp.where(atoms == ids_ref[...], coupling_ref[...], 0.0), axis=1, keepdims=True)
    weight_ref[...] = jnp.broadcast_to(weight, weight_ref.shape)


def put_sides(s, field_ref, x, y, x_ref, y_ref, xy_ref):
    for n in range(s.by):
        x_ref[n * s.span : (n + 1) * s.span] = field_ref[x, n, 0 : s.span, :]
    for n in range(s.bx):
        y_ref[n * s.span : (n + 1) * s.span] = field_ref[n, y, 0 : s.span, :]
    xy_ref[0 : s.span] = field_ref[x, y, 0 : s.span, :]
    for ref, used in ((x_ref, s.x_rows), (y_ref, s.y_rows), (xy_ref, s.span)):
        blank(ref, used)


def send_sides(s, x_ref, y_ref, xy_ref, msg_refs, parts):
    for ref, used, part, msg_ref in zip((x_ref, y_ref, xy_ref), (s.x_rows, s.y_rows, s.span), parts, msg_refs):
        put_split(ref, used, part)
        msg_ref[...] = ref[...].astype(BF16)


def get_sides(s, received, x_ref, y_ref, xy_ref):
    parts = []
    for ref, used, msg_ref in zip((x_ref, y_ref, xy_ref), (s.x_rows, s.y_rows, s.span), received):
        ref[...] = msg_ref[...].astype(F32)
        parts.append(get_split(ref, used, 2 * s.own))
    return parts


def add_sides(s, field_ref, x_ref, y_ref, xy_ref):
    for n in range(s.by):
        field_ref[0, n, 0 : s.span, :] += x_ref[n * s.span : (n + 1) * s.span]
    for n in range(s.bx):
        field_ref[n, 0, 0 : s.span, :] += y_ref[n * s.span : (n + 1) * s.span]
    field_ref[0, 0, 0 : s.span, :] += xy_ref[0 : s.span]


def send_down(s, total, field_ref, msg_refs, part_ref, x_ref, y_ref, xy_ref):
    put_sides(s, field_ref, 0, 0, x_ref, y_ref, xy_ref)
    corner, x_part, y_part, own_part = columns(s, total)
    part_ref[...] = own_part
    send_sides(s, x_ref, y_ref, xy_ref, msg_refs, (x_part, y_part, corner))


def first_down_body(s, before_ref, total_ref, early_ref, *refs):
    del before_ref, early_ref
    count = 2 - s.pairs
    received, refs = refs[:count], refs[count:]
    field_ref, *msg_refs, part_ref, above_ref, below_ref, x_ref, y_ref, xy_ref = refs
    get_z(s, received, above_ref, below_ref)
    half = 4 * s.own
    total = total_ref[...] + jnp.concatenate([get_split(below_ref, 0, half), get_split(above_ref, s.z_rows, half)], axis=0)
    for x in range(s.bx):
        field_ref[x, 0 : s.by, s.bz, :] = above_ref[x * s.by : (x + 1) * s.by]
    send_down(s, total, field_ref, msg_refs, part_ref, x_ref, y_ref, xy_ref)


def cell_body(s, before_ref, from_x_ref, from_y_ref, from_xy_ref, part_ref, weight_ref, *refs):
    matrix_refs, refs = refs[: s.cells[0]], refs[s.cells[0] :]
    field_ref, block_ref, *msg_refs, own_ref, sums_ref, x_ref, y_ref, xy_ref = refs
    del before_ref
    parts = get_sides(s, (from_x_ref, from_y_ref, from_xy_ref), x_ref, y_ref, xy_ref)
    rest = jnp.zeros((s.bzp - s.span, s.waves), F32)
    for n in range(s.by):
        field_ref[s.bx, n, 0 : s.span, :] = x_ref[n * s.span : (n + 1) * s.span]
        field_ref[s.bx, n, s.span :, :] = rest
    for n in range(s.bx):
        field_ref[n, s.by, 0 : s.span, :] = y_ref[n * s.span : (n + 1) * s.span]
        field_ref[n, s.by, s.span :, :] = rest
    field_ref[s.bx, s.by, 0 : s.span, :] = xy_ref[0 : s.span]
    field_ref[s.bx, s.by, s.span :, :] = rest
    weight = columns(s, weight_ref[...])[3]
    total = (part_ref[...] + parts[0] + parts[1] + parts[2]) * weight
    own_ref[...] = total
    apply_cells(s, field_ref, matrix_refs, sums_ref)
    join_sides(s, sums_ref, x_ref, y_ref, xy_ref)
    send_sides(s, x_ref, y_ref, xy_ref, msg_refs, (total, total, total))
    join_cells(s, sums_ref, block_ref)


def apply_cells(s, field_ref, matrix_refs, sums_ref):
    order, side, group = s.order, s.side, s.group
    used = side * side * group
    for i in range(s.cells[0]):
        for j in range(s.cells[1]):
            for k in range(s.cells[2]):
                first = k * order
                values = field_ref[i * order : i * order + side, j * order : j * order + side, first : first + group]
                values = values.reshape(used, s.waves)
                if s.padded > used:
                    values = jnp.concatenate([values, jnp.zeros((s.padded - used, s.waves), F32)], axis=0)
                product = jnp.dot(matrix_refs[i][j, k], values.astype(BF16), preferred_element_type=F32)
                product = product[0:used].reshape(side, side, group, s.waves)
                x0, x1, y0, y1 = i * order, i * order + side, j * order, j * order + side
                a, b = int(i > 0), int(j > 0)
                sums_ref[k, x0 + a : x1, y0 + b : y1] = product[a:, b:]
                if a:
                    sums_ref[k, x0, y0 + b : y1] += product[0, b:]
                if b:
                    sums_ref[k, x0 + a : x1, y0] += product[a:, 0]
                if a and b:
                    sums_ref[k, x0, y0] += product[0, 0]


def join_cells(s, sums_ref, out_ref):
    count = s.by
    for x in range(s.bx):
        out_ref[x, :, 0 : s.group, :] = sums_ref[0, x, 0:count]
        out_ref[x, :, s.group :, :] = jnp.zeros((count, s.bzp - s.group, s.waves), F32)
        for k in range(1, s.cells[2]):
            out_ref[x, :, k * s.order : k * s.order + s.group, :] += sums_ref[k, x, 0:count]


def join_sides(s, sums_ref, x_ref, y_ref, xy_ref):
    last = s.cells[2] - 1

    def join(rows_ref, at, x, y):
        for k in range(s.cells[2]):
            count = s.order + int(k == last)
            first = at + k * s.order
            rows_ref[first : first + count] = sums_ref[k, x, y, 0:count, :]
            if k:
                rows_ref[first : first + 1] += sums_ref[k - 1, x, y, s.order : s.order + 1, :]

    for n in range(s.by):
        join(x_ref, n * s.span, s.bx, n)
    for n in range(s.bx):
        join(y_ref, n * s.span, n, s.by)
    join(xy_ref, 0, s.bx, s.by)
    for ref, used in ((x_ref, s.x_rows), (y_ref, s.y_rows), (xy_ref, s.span)):
        blank(ref, used)


def stacked(totals):
    high, low = halves(totals)
    return jnp.concatenate([high, high, low], axis=0).astype(BF16)


def middle_body(s, block_ref, from_x_ref, from_y_ref, from_xy_ref, own_ref, by_node_ref, *refs):
    field_ref, *msg_refs, x_ref, y_ref, xy_ref, low_ref, high_ref = refs
    x_part, y_part, corner = get_sides(s, (from_x_ref, from_y_ref, from_xy_ref), x_ref, y_ref, xy_ref)
    stack = stacked(from_columns(s, [corner, x_part, y_part, own_ref[...]]))
    for x in range(s.bx):
        image = jnp.dot(by_node_ref[x], stack, preferred_element_type=F32)
        field_ref[x, 0 : s.by] = image.reshape(s.by, s.bzp, s.waves) + block_ref[x]
    add_sides(s, field_ref, x_ref, y_ref, xy_ref)
    for x in range(s.bx):
        low_ref[x * s.by : (x + 1) * s.by] = field_ref[x, 0 : s.by, 0, :]
        high_ref[x * s.by : (x + 1) * s.by] = field_ref[x, 0 : s.by, s.bz, :]
    blank(low_ref, s.z_rows)
    blank(high_ref, s.z_rows)
    put_z(s, msg_refs, low_ref, high_ref)


def sums_body(s, field_ref, by_atom_ref, line_ref, total_ref, lowest_ref):
    total = jnp.zeros((s.locals, s.waves), F32)
    for x in range(s.bx):
        total = total + split_sums(by_atom_ref[x], s.locals, field_ref[x, 0 : s.by].reshape(s.by * s.bzp, s.waves))
    total_ref[...] = total
    lowest = line_ref[...].T[0 : 2 * s.locals]
    if s.z_plane > s.z_rows:
        lowest = jnp.concatenate([lowest, jnp.zeros((2 * s.locals, s.z_plane - s.z_rows), F32)], axis=1)
    lowest_ref[...] = lowest.astype(BF16)


def second_down_body(s, before_ref, total_ref, lowest_ref, *refs):
    del before_ref
    count = 2 - s.pairs
    received, refs = refs[:count], refs[count:]
    field_ref, *msg_refs, part_ref, above_ref, below_ref, x_ref, y_ref, xy_ref = refs
    get_z(s, received, above_ref, below_ref)
    for x in range(s.bx):
        field_ref[x, 0 : s.by, s.bz, :] += above_ref[x * s.by : (x + 1) * s.by]
        field_ref[x, 0 : s.by, 0, :] += below_ref[x * s.by : (x + 1) * s.by]
    total = total_ref[...] + split_sums(lowest_ref[...], s.locals, below_ref[...])
    send_down(s, total, field_ref, msg_refs, part_ref, x_ref, y_ref, xy_ref)


def fold_body(s, before_ref, from_x_ref, from_y_ref, from_xy_ref, own_ref, *refs):
    del before_ref
    block_ref, *msg_refs, total_ref, x_ref, y_ref, xy_ref, low_ref, high_ref = refs
    x_part, y_part, corner = get_sides(s, (from_x_ref, from_y_ref, from_xy_ref), x_ref, y_ref, xy_ref)
    total = from_columns(s, [corner, x_part, y_part, own_ref[...]])
    total_ref[...] = total
    add_sides(s, block_ref, x_ref, y_ref, xy_ref)
    half = 4 * s.own
    for x in range(s.bx):
        high_ref[x * s.by : (x + 1) * s.by] = block_ref[x, :, s.bz, :]
    blank(high_ref, s.z_rows)
    blank(low_ref, 0)
    put_split(low_ref, 0, total[0:half])
    put_split(high_ref, s.z_rows, total[half:])
    put_z(s, msg_refs, low_ref, high_ref)


def last_body(s, start_ref, block_ref, total_ref, by_node_ref, *refs):
    count = 2 - s.pairs
    received, refs = refs[:count], refs[count:]
    out_hbm, above_ref, below_ref, plane_ref, out_ref, sems = refs
    get_z(s, received, above_ref, below_ref)
    half = 4 * s.own
    total = total_ref[...] + jnp.concatenate([get_split(below_ref, s.z_rows, half), get_split(above_ref, 0, half)], axis=0)
    stack = stacked(total)
    copies = []
    for x in range(s.bx):
        image = jnp.dot(by_node_ref[x], stack, preferred_element_type=F32)
        plane_ref[...] = image.reshape(s.by, s.bzp, s.waves) + block_ref[x]
        plane_ref[:, 0, :] += below_ref[x * s.by : (x + 1) * s.by]
        out_ref[x] = 2.0 * plane_ref[:, 0 : s.bz] - start_ref[x]
        copies.append(pltpu.make_async_copy(out_ref.at[x], out_hbm.at[x], sems.at[x]))
        copies[x].start()
    for copy in copies:
        copy.wait()


def selector(count, chosen):
    row = lax.broadcasted_iota(jnp.int32, count, 0)
    column = lax.broadcasted_iota(jnp.int32, count, 1)
    return chosen(row, column).astype(F32).astype(BF16)


def matrix_body(s, part, matrix_hbm, out_ref, raw_ref, flat_ref, half_ref, sems):
    cells_y, cells_z = s.cells[1:]
    side, group = s.side, s.group
    nodes = side**3
    copies = [pltpu.make_async_copy(matrix_hbm.at[part, j], raw_ref.at[j], sems.at[j]) for j in range(cells_y)]
    for copy in copies:
        copy.start()
    wide = 256 // group * side
    spans = []
    for first in range(0, s.padded, 256):
        low = first // group * side // 128 * 128
        high = min(nodes, first // group * side + wide)
        width = min(256, s.padded - first)
        spans.append((first, low, high, selector((high - low, width), lambda m, c, low=low, first=first: (
            ((c + first) % group < side) & (m + low == (c + first) // group * side + (c + first) % group)))))
    tall = 128 // group * side
    picks = jnp.concatenate(
        [
            selector((128, tall * cells_z), lambda r, m, k=k: (r % group < side) & (m == (r // group * side + r % group) * cells_z + k))
            for k in range(cells_z)
        ],
        axis=0,
    )
    for j in range(cells_y):
        copies[j].wait()
        flat_ref[...] = raw_ref[j].reshape(nodes * cells_z, nodes)
        for first, low, high, spread in spans:
            half = jnp.dot(flat_ref[:, low:high], spread, preferred_element_type=F32)
            half_ref[:, first : first + spread.shape[1]] = half.astype(BF16)
        for first in range(0, s.padded, 128):
            count = min(128, s.padded - first)
            low = first // group * side * cells_z
            high = min(nodes * cells_z, low + tall * cells_z)
            rows = jnp.dot(picks[:, 0 : high - low], half_ref[low:high], preferred_element_type=F32).astype(BF16)
            for k in range(cells_z):
                out_ref[j, k, first : first + count] = rows[128 * k : 128 * k + count]


def regrouped(s, cell_matrices, part):
    shape = cell_matrices.shape
    nodes = shape[3]
    return call(
        matrix_body,
        s,
        [jax.ShapeDtypeStruct(shape[1:3] + (s.padded, s.padded), BF16)],
        [
            pltpu.VMEM((shape[1], nodes, shape[2], nodes), BF16),
            pltpu.VMEM((nodes * shape[2], nodes), BF16),
            pltpu.VMEM((nodes * shape[2], s.padded), BF16),
            pltpu.SemaphoreType.DMA((shape[1],)),
        ],
        [cell_matrices.transpose(0, 1, 3, 2, 4)],
        spaces={0: pltpu.HBM},
        extra=(part,),
    )[0]


def along_z(s, msgs):
    if s.pairs:
        return [shifted(msgs[0], (0, 0, 1))]
    return [shifted(msgs[0], (0, 0, -1)), shifted(msgs[1], (0, 0, 1))]


def along_xy(msgs, by):
    return [shifted(msg, (by * dx, by * dy, 0)) for msg, dx, dy in zip(msgs, (1, 0, 1), (0, 1, 1))]


def local(wavefunctions, cell_matrices, projectors, slot_atoms, atom_coupling):
    atom_count = atom_coupling.shape[0]
    devices = 1
    for axis in AXES:
        devices *= lax.axis_size(axis)
    own = atom_count // devices
    s = Sizes(wavefunctions.shape, cell_matrices.shape, own, lax.axis_size("gz") == 2)
    ids = local_atoms(own)[:, None]
    plane = s.by * s.bzp
    sides = s.side_rows()
    sums = s.scratch(s.cells[2], s.bx + 1, s.by + 1, s.group)
    field, by_node, by_atom, line, *msgs, total, weight = call(
        first_body,
        s,
        [
            s.extended(),
            jax.ShapeDtypeStruct((s.bx, plane, 3 * s.locals), BF16),
            jax.ShapeDtypeStruct((s.bx, 2 * s.locals, plane), BF16),
            jax.ShapeDtypeStruct((s.z_rows, 3 * s.locals), F32),
        ]
        + s.z_msgs(s.z_both, s.z_sums)
        + [s.rows(s.locals), s.rows(s.locals)],
        [
            s.scratch(s.bx, s.by, s.bz),
            pltpu.VMEM(projectors.shape, F32),
            pltpu.VMEM(slot_atoms.shape, jnp.int32),
            pltpu.VMEM((1, atom_count), F32),
            pltpu.VMEM((s.bx * s.by * s.bz, 3 * s.locals), F32),
            pltpu.VMEM((s.bx * s.by, s.bzp, 3 * s.locals), F32),
            s.scratch(s.z_both),
            s.scratch(s.z_sums),
            pltpu.SemaphoreType.DMA((s.bx // s.few,)),
            pltpu.SemaphoreType.DMA((3,)),
        ],
        [wavefunctions, projectors, slot_atoms, atom_coupling[None, :], ids],
        spaces={0: pltpu.HBM, 1: pltpu.HBM, 2: pltpu.HBM, 3: pltpu.HBM},
    )
    matrices = [regrouped(s, cell_matrices, part) for part in range(s.cells[0])]
    received = along_z(s, msgs)
    field, *msgs, part = call(
        first_down_body,
        s,
        [s.extended()] + s.side_msgs() + [s.rows(2 * own)],
        [s.scratch(s.z_both), s.scratch(s.z_sums)] + sides,
        [field, total, matrices[0]] + received,
        aliases={0: 0},
    )

    def cells(field, msgs, part):
        received = along_xy(msgs, -1)
        _, block, *msgs, mine = call(
            cell_body,
            s,
            [s.extended(), s.block()] + s.side_msgs() + [s.rows(2 * own)],
            [sums] + sides,
            [field] + received + [part, weight] + matrices,
            aliases={0: 0},
        )
        return block, along_xy(msgs, 1), mine

    block, received, mine = cells(field, msgs, part)
    field, *msgs = call(
        middle_body,
        s,
        [s.extended()] + s.z_msgs(s.z_plane, s.z_plane),
        sides + [s.scratch(s.z_plane), s.scratch(s.z_plane)],
        [block] + received + [mine, by_node],
    )
    received = along_z(s, msgs)
    total, lowest = call(
        sums_body,
        s,
        [s.rows(s.locals), jax.ShapeDtypeStruct((2 * s.locals, s.z_plane), BF16)],
        [],
        [field, by_atom, line],
    )
    field, *msgs, part = call(
        second_down_body,
        s,
        [s.extended()] + s.side_msgs() + [s.rows(2 * own)],
        [s.scratch(s.z_plane), s.scratch(s.z_plane)] + sides,
        [field, total, lowest] + received,
        aliases={0: 0},
    )
    block, received, mine = cells(field, msgs, part)
    block, *msgs, total = call(
        fold_body,
        s,
        [s.block()] + s.z_msgs(s.z_sums, s.z_both) + [s.rows(s.locals)],
        sides + [s.scratch(s.z_sums), s.scratch(s.z_both)],
        [block] + received + [mine],
        aliases={0: 0},
    )
    received = along_z(s, msgs)
    (out,) = call(
        last_body,
        s,
        [jax.ShapeDtypeStruct(wavefunctions.shape, F32)],
        [
            s.scratch(s.z_sums),
            s.scratch(s.z_both),
            s.scratch(s.by, s.bzp),
            s.scratch(s.bx, s.by, s.bz),
            pltpu.SemaphoreType.DMA((s.bx,)),
        ],
        [wavefunctions, block, total, by_node] + received,
        out_spaces={0: pltpu.HBM},
    )
    return out


def solution(mesh):
    return jax.shard_map(
        local,
        mesh=mesh,
        in_specs=(
            P("gx", "gy", "gz", None),
            P("gx", "gy", "gz", None, None),
            P(("gx", "gy", "gz"), None, None),
            P(("gx", "gy", "gz"), None),
            P(),
        ),
        out_specs=P("gx", "gy", "gz", None),
        check_vma=False,
    )
```

```python
import functools

import jax
import jax.numpy as jnp
from jax import lax
from jax.experimental import pallas as pl
from jax.experimental.pallas import tpu as pltpu
from jax.sharding import PartitionSpec as P

AXES = ("gx", "gy", "gz")
F32 = jnp.float32
BF16 = jnp.bfloat16
LIMIT = 12 * 1024 * 1024


def up_to(value, unit):
    return -(-value // unit) * unit


def shifted(value, shift):
    sizes = [lax.axis_size(axis) for axis in AXES]
    pairs = []
    for x in range(sizes[0]):
        for y in range(sizes[1]):
            for z in range(sizes[2]):
                here = (x * sizes[1] + y) * sizes[2] + z
                there = [(p + s) % n for p, s, n in zip((x, y, z), shift, sizes)]
                pairs.append((here, (there[0] * sizes[1] + there[1]) * sizes[2] + there[2]))
    return lax.ppermute(value, AXES, pairs)


def halves(value):
    high = value.astype(BF16).astype(F32)
    return high, value - high


def put_split(rows_ref, start, value):
    count = value.shape[0]
    high, low = halves(value)
    rows_ref[start : start + count] = high
    rows_ref[start + count : start + 2 * count] = low


def get_split(rows_ref, start, count):
    return rows_ref[start : start + count] + rows_ref[start + count : start + 2 * count]


class Sizes:
    def __init__(self, field_shape, cell_shape, own, pairs):
        self.bx, self.by, self.bz, self.waves = field_shape
        self.cells = cell_shape[:3]
        self.order = self.bx // cell_shape[0]
        self.side = self.order + 1
        self.group = up_to(self.side, 8)
        self.padded = up_to(self.side * self.side * self.group, 16)
        self.bzp = up_to(max(self.bz + 1, (cell_shape[2] - 1) * self.order + self.group), 16)
        self.few_out = max(n for n in (1, 2) if self.bx % n == 0)
        self.pairs = pairs
        self.own = own
        self.locals = 8 * own
        self.span = self.bz + 1
        self.z_rows = self.bx * self.by
        self.x_rows = self.by * self.span
        self.y_rows = self.bx * self.span
        self.x_msg = up_to(self.x_rows + 4 * own, 16)
        self.y_msg = up_to(self.y_rows + 4 * own, 16)
        self.xy_msg = up_to(self.span + 4 * own, 16)
        self.z_plane = up_to(self.z_rows, 16)
        self.z_sums = up_to(8 * own, 16)
        self.z_both = up_to(self.z_rows + 8 * own, 16)

    def extended(self):
        return jax.ShapeDtypeStruct((self.bx + 1, self.by + 1, self.bzp, self.waves), F32)

    def block(self):
        return jax.ShapeDtypeStruct((self.bx, self.by, self.bzp, self.waves), F32)

    def rows(self, count, dtype=F32):
        return jax.ShapeDtypeStruct((count, self.waves), dtype)

    def scratch(self, *shape):
        return pltpu.VMEM(shape + (self.waves,), F32)

    def z_msgs(self, down, up):
        return [self.rows(down + up, BF16)] if self.pairs else [self.rows(down, BF16), self.rows(up, BF16)]

    def side_msgs(self):
        return [self.rows(n, BF16) for n in (self.x_msg, self.y_msg, self.xy_msg)]

    def side_rows(self):
        return [self.scratch(n) for n in (self.x_msg, self.y_msg, self.xy_msg)]


VMEM = pltpu.VMEM


def call(body, sizes, outs, scratch, args, spaces=None, out_spaces=None, aliases=None, extra=()):
    spaces = spaces or {}
    out_spaces = out_spaces or {}
    outs = [out_spaces.get(n, VMEM)(out.shape, out.dtype) for n, out in enumerate(outs)]
    args = [pltpu.with_memory_space_constraint(arg, spaces.get(n, VMEM)) for n, arg in enumerate(args)]
    return pl.pallas_call(
        functools.partial(body, sizes, *extra),
        out_shape=outs,
        in_specs=[pl.BlockSpec(memory_space=spaces.get(n, VMEM)) for n in range(len(args))],
        out_specs=[pl.BlockSpec(memory_space=out_spaces.get(n, VMEM)) for n in range(len(outs))],
        scratch_shapes=scratch,
        input_output_aliases=aliases or {},
        compiler_params=pltpu.CompilerParams(vmem_limit_bytes=LIMIT),
    )(*args)


def local_atoms(own):
    sizes = [lax.axis_size(axis) for axis in AXES]
    here = [lax.axis_index(axis) for axis in AXES]
    ids = []
    for dz in (1, 0):
        for dx in (1, 0):
            for dy in (1, 0):
                x, y, z = (lax.rem(h + n - d, n) for h, n, d in zip(here, sizes, (dx, dy, dz)))
                owner = (x * sizes[1] + y) * sizes[2] + z
                ids += [owner * own + a for a in range(own)]
    return jnp.stack(ids).astype(jnp.int32)


def blank(rows_ref, first):
    count = rows_ref.shape[0] - first
    if count:
        rows_ref[first:] = jnp.zeros((count,) + rows_ref.shape[1:], F32)


def split_sums(by_atom, count, field):
    high = field.astype(BF16)
    low = (field - high.astype(F32)).astype(BF16)
    with_high = jnp.dot(by_atom, high, preferred_element_type=F32)
    with_low = jnp.dot(by_atom[0:count], low, preferred_element_type=F32)
    return with_high[0:count] + with_high[count : 2 * count] + with_low


def put_z(s, msg_refs, down_ref, up_ref):
    if s.pairs:
        count = down_ref.shape[0]
        msg_refs[0][0:count] = down_ref[...].astype(BF16)
        msg_refs[0][count:] = up_ref[...].astype(BF16)
    else:
        msg_refs[0][...] = down_ref[...].astype(BF16)
        msg_refs[1][...] = up_ref[...].astype(BF16)


def get_z(s, msg_refs, above_ref, below_ref):
    if s.pairs:
        count = above_ref.shape[0]
        above_ref[...] = msg_refs[0][0:count].astype(F32)
        below_ref[...] = msg_refs[0][count:].astype(F32)
    else:
        above_ref[...] = msg_refs[0][...].astype(F32)
        below_ref[...] = msg_refs[1][...].astype(F32)


def columns(s, totals):
    own, half = s.own, 4 * s.own
    return [
        jnp.concatenate([totals[n * own : (n + 1) * own], totals[half + n * own : half + (n + 1) * own]], axis=0) for n in range(4)
    ]


def from_columns(s, parts):
    own = s.own
    return jnp.concatenate([part[0:own] for part in parts] + [part[own : 2 * own] for part in parts], axis=0)


def first_body(
    s, start_hbm, rows_hbm, slots_hbm, coupling_hbm, ids_ref,
    field_ref, by_atom_ref, wide_ref, *refs
):
    *msg_refs, total_ref, weight_ref, start_ref, rows_ref, slots_ref, coupling_ref, tall_ref, low_ref, high_ref, sems, small_sems = refs
    small = [
        pltpu.make_async_copy(rows_hbm, rows_ref, small_sems.at[0]),
        pltpu.make_async_copy(slots_hbm, slots_ref, small_sems.at[1]),
        pltpu.make_async_copy(coupling_hbm, coupling_ref, small_sems.at[2]),
    ]
    for copy in small:
        copy.start()
    whole = pltpu.make_async_copy(start_hbm, start_ref, sems.at[0])
    whole.start()
    for copy in small:
        copy.wait()
    chosen = (ids_ref[...] == slots_ref[...]).astype(F32).astype(BF16)
    rows = rows_ref[0]
    high = rows.astype(BF16)
    low = (rows - high.astype(F32)).astype(BF16)
    parts = [jnp.dot(chosen, part, preferred_element_type=F32) for part in (high, low)]
    tall_ref[...] = jnp.concatenate(parts, axis=0).T
    wide_ref[:, s.bz : s.bzp, :] = jnp.zeros((s.bx * s.by, s.bzp - s.bz, 2 * s.locals), F32)
    for g in range(s.bx * s.by):
        wide_ref[g, 0 : s.bz, :] = tall_ref[g * s.bz : (g + 1) * s.bz, :]
    for x in range(s.bx):
        wide = wide_ref[x * s.by : (x + 1) * s.by].reshape(s.by * s.bzp, 2 * s.locals)
        by_atom_ref[x] = wide.T.astype(BF16)
    total = jnp.zeros((s.locals, s.waves), F32)
    whole.wait()
    for x in range(s.bx):
        plane = jnp.concatenate([start_ref[x], jnp.zeros((s.by, s.bzp - s.bz, s.waves), F32)], axis=1)
        field_ref[x, 0 : s.by] = plane
        total = total + split_sums(by_atom_ref[x], s.locals, plane.reshape(s.by * s.bzp, s.waves))
    total_ref[...] = total
    half = 4 * s.own
    for x in range(s.bx):
        low_ref[x * s.by : (x + 1) * s.by] = field_ref[x, 0 : s.by, 0, :]
    blank(low_ref, s.z_rows)
    blank(high_ref, 0)
    put_split(low_ref, s.z_rows, total[0:half])
    put_split(high_ref, 0, total[half:])
    put_z(s, msg_refs, low_ref, high_ref)
    atoms = lax.broadcasted_iota(jnp.int32, (s.locals, coupling_ref.shape[1]), 1)
    weight = jnp.sum(jnp.where(atoms == ids_ref[...], coupling_ref[...], 0.0), axis=1, keepdims=True)
    weight_ref[...] = jnp.broadcast_to(weight, weight_ref.shape)


def node_body(s, wide_ref, by_node_ref, lowest_ref, lowest_by_node_ref):
    for x in range(s.bx):
        wide = wide_ref[x * s.by : (x + 1) * s.by].reshape(s.by * s.bzp, 2 * s.locals)
        by_node_ref[x] = jnp.concatenate([wide, wide[:, 0 : s.locals]], axis=1).astype(BF16)
    line = wide_ref[:, 0, :]
    lowest_by_node_ref[...] = jnp.concatenate([line, line[:, 0 : s.locals]], axis=1).astype(BF16)
    lowest = line.T
    if s.z_plane > s.z_rows:
        lowest = jnp.concatenate([lowest, jnp.zeros((2 * s.locals, s.z_plane - s.z_rows), F32)], axis=1)
    lowest_ref[...] = lowest.astype(BF16)


def put_sides(s, field_ref, x, y, x_ref, y_ref, xy_ref):
    for n in range(s.by):
        x_ref[n * s.span : (n + 1) * s.span] = field_ref[x, n, 0 : s.span, :]
    for n in range(s.bx):
        y_ref[n * s.span : (n + 1) * s.span] = field_ref[n, y, 0 : s.span, :]
    xy_ref[0 : s.span] = field_ref[x, y, 0 : s.span, :]
    for ref, used in ((x_ref, s.x_rows), (y_ref, s.y_rows), (xy_ref, s.span)):
        blank(ref, used)


def send_sides(s, x_ref, y_ref, xy_ref, msg_refs, parts):
    for ref, used, part, msg_ref in zip((x_ref, y_ref, xy_ref), (s.x_rows, s.y_rows, s.span), parts, msg_refs):
        put_split(ref, used, part)
        msg_ref[...] = ref[...].astype(BF16)


def get_sides(s, received, x_ref, y_ref, xy_ref):
    parts = []
    for ref, used, msg_ref in zip((x_ref, y_ref, xy_ref), (s.x_rows, s.y_rows, s.span), received):
        ref[...] = msg_ref[...].astype(F32)
        parts.append(get_split(ref, used, 2 * s.own))
    return parts


def add_sides(s, field_ref, x_ref, y_ref, xy_ref):
    for n in range(s.by):
        field_ref[0, n, 0 : s.span, :] += x_ref[n * s.span : (n + 1) * s.span]
    for n in range(s.bx):
        field_ref[n, 0, 0 : s.span, :] += y_ref[n * s.span : (n + 1) * s.span]
    field_ref[0, 0, 0 : s.span, :] += xy_ref[0 : s.span]


def send_down(s, total, field_ref, msg_refs, part_ref, x_ref, y_ref, xy_ref):
    put_sides(s, field_ref, 0, 0, x_ref, y_ref, xy_ref)
    corner, x_part, y_part, own_part = columns(s, total)
    part_ref[...] = own_part
    send_sides(s, x_ref, y_ref, xy_ref, msg_refs, (x_part, y_part, corner))


def first_down_body(s, before_ref, total_ref, early_ref, *refs):
    del before_ref, early_ref
    count = 2 - s.pairs
    received, refs = refs[:count], refs[count:]
    field_ref, *msg_refs, part_ref, above_ref, below_ref, x_ref, y_ref, xy_ref = refs
    get_z(s, received, above_ref, below_ref)
    half = 4 * s.own
    total = total_ref[...] + jnp.concatenate([get_split(below_ref, 0, half), get_split(above_ref, s.z_rows, half)], axis=0)
    for x in range(s.bx):
        field_ref[x, 0 : s.by, s.bz, :] = above_ref[x * s.by : (x + 1) * s.by]
    send_down(s, total, field_ref, msg_refs, part_ref, x_ref, y_ref, xy_ref)


def cell_body(s, before_ref, from_x_ref, from_y_ref, from_xy_ref, part_ref, weight_ref, *refs):
    matrix_refs, refs = refs[: s.cells[0]], refs[s.cells[0] :]
    field_ref, sums_ref, *msg_refs, own_ref, x_ref, y_ref, xy_ref = refs
    del before_ref
    parts = get_sides(s, (from_x_ref, from_y_ref, from_xy_ref), x_ref, y_ref, xy_ref)
    rest = jnp.zeros((s.bzp - s.span, s.waves), F32)
    for n in range(s.by):
        field_ref[s.bx, n, 0 : s.span, :] = x_ref[n * s.span : (n + 1) * s.span]
        field_ref[s.bx, n, s.span :, :] = rest
    for n in range(s.bx):
        field_ref[n, s.by, 0 : s.span, :] = y_ref[n * s.span : (n + 1) * s.span]
        field_ref[n, s.by, s.span :, :] = rest
    field_ref[s.bx, s.by, 0 : s.span, :] = xy_ref[0 : s.span]
    field_ref[s.bx, s.by, s.span :, :] = rest
    weight = columns(s, weight_ref[...])[3]
    total = (part_ref[...] + parts[0] + parts[1] + parts[2]) * weight
    own_ref[...] = total
    apply_cells(s, field_ref, matrix_refs, sums_ref)
    join_sides(s, sums_ref, x_ref, y_ref, xy_ref)
    send_sides(s, x_ref, y_ref, xy_ref, msg_refs, (total, total, total))


def apply_cells(s, field_ref, matrix_refs, sums_ref):
    order, side, group = s.order, s.side, s.group
    used = side * side * group
    for i in range(s.cells[0]):
        for j in range(s.cells[1]):
            for k in range(s.cells[2]):
                first = k * order
                values = field_ref[i * order : i * order + side, j * order : j * order + side, first : first + group]
                values = values.reshape(used, s.waves)
                if s.padded > used:
                    values = jnp.concatenate([values, jnp.zeros((s.padded - used, s.waves), F32)], axis=0)
                product = jnp.dot(matrix_refs[i][j, k], values.astype(BF16), preferred_element_type=F32)
                product = product[0:used].reshape(side, side, group, s.waves)
                x0, x1, y0, y1 = i * order, i * order + side, j * order, j * order + side
                a, b = int(i > 0), int(j > 0)
                sums_ref[k, x0 + a : x1, y0 + b : y1] = product[a:, b:]
                if a:
                    sums_ref[k, x0, y0 + b : y1] += product[0, b:]
                if b:
                    sums_ref[k, x0 + a : x1, y0] += product[a:, 0]
                if a and b:
                    sums_ref[k, x0, y0] += product[0, 0]


def join_cells(s, sums_ref, out_ref):
    count = s.by
    for x in range(s.bx):
        out_ref[x, :, 0 : s.group, :] = sums_ref[0, x, 0:count]
        out_ref[x, :, s.group :, :] = jnp.zeros((count, s.bzp - s.group, s.waves), F32)
        for k in range(1, s.cells[2]):
            out_ref[x, :, k * s.order : k * s.order + s.group, :] += sums_ref[k, x, 0:count]


def join_sides(s, sums_ref, x_ref, y_ref, xy_ref):
    last = s.cells[2] - 1

    def join(rows_ref, at, x, y):
        for k in range(s.cells[2]):
            count = s.order + int(k == last)
            first = at + k * s.order
            rows_ref[first : first + count] = sums_ref[k, x, y, 0:count, :]
            if k:
                rows_ref[first : first + 1] += sums_ref[k - 1, x, y, s.order : s.order + 1, :]

    for n in range(s.by):
        join(x_ref, n * s.span, s.bx, n)
    for n in range(s.bx):
        join(y_ref, n * s.span, n, s.by)
    join(xy_ref, 0, s.bx, s.by)
    for ref, used in ((x_ref, s.x_rows), (y_ref, s.y_rows), (xy_ref, s.span)):
        blank(ref, used)


def stacked(totals):
    high, low = halves(totals)
    return jnp.concatenate([high, high, low], axis=0).astype(BF16)


def swap_body(s, block_ref, from_x_ref, from_y_ref, from_xy_ref, own_ref, lowest_by_node_ref, *refs):
    *msg_refs, x_ref, y_ref, xy_ref, low_ref, high_ref = refs
    x_part, y_part, corner = get_sides(s, (from_x_ref, from_y_ref, from_xy_ref), x_ref, y_ref, xy_ref)
    stack = stacked(from_columns(s, [corner, x_part, y_part, own_ref[...]]))
    low_ref[0 : s.z_rows] = jnp.dot(lowest_by_node_ref[...], stack, preferred_element_type=F32)
    for x in range(s.bx):
        low_ref[x * s.by : (x + 1) * s.by] += block_ref[x, :, 0, :]
        high_ref[x * s.by : (x + 1) * s.by] = block_ref[x, :, s.bz, :]
    for ref, z in ((low_ref, 0), (high_ref, s.bz)):
        for n in range(s.by):
            ref[n : n + 1] += x_ref[n * s.span + z : n * s.span + z + 1]
        for n in range(s.bx):
            ref[n * s.by : n * s.by + 1] += y_ref[n * s.span + z : n * s.span + z + 1]
        ref[0:1] += xy_ref[z : z + 1]
        blank(ref, s.z_rows)
    put_z(s, msg_refs, low_ref, high_ref)


def middle_body(s, block_ref, from_x_ref, from_y_ref, from_xy_ref, own_ref, by_node_ref, field_ref, x_ref, y_ref, xy_ref):
    x_part, y_part, corner = get_sides(s, (from_x_ref, from_y_ref, from_xy_ref), x_ref, y_ref, xy_ref)
    stack = stacked(from_columns(s, [corner, x_part, y_part, own_ref[...]]))
    for x in range(s.bx):
        image = jnp.dot(by_node_ref[x], stack, preferred_element_type=F32)
        field_ref[x, 0 : s.by] = image.reshape(s.by, s.bzp, s.waves) + block_ref[x]
    add_sides(s, field_ref, x_ref, y_ref, xy_ref)


def sums_body(s, field_ref, by_atom_ref, total_ref):
    total = jnp.zeros((s.locals, s.waves), F32)
    for x in range(s.bx):
        total = total + split_sums(by_atom_ref[x], s.locals, field_ref[x, 0 : s.by].reshape(s.by * s.bzp, s.waves))
    total_ref[...] = total


def second_down_body(s, before_ref, total_ref, lowest_ref, *refs):
    del before_ref
    count = 2 - s.pairs
    received, refs = refs[:count], refs[count:]
    field_ref, *msg_refs, part_ref, above_ref, below_ref, x_ref, y_ref, xy_ref = refs
    get_z(s, received, above_ref, below_ref)
    for x in range(s.bx):
        field_ref[x, 0 : s.by, s.bz, :] += above_ref[x * s.by : (x + 1) * s.by]
        field_ref[x, 0 : s.by, 0, :] += below_ref[x * s.by : (x + 1) * s.by]
    total = total_ref[...] + split_sums(lowest_ref[...], s.locals, below_ref[...])
    send_down(s, total, field_ref, msg_refs, part_ref, x_ref, y_ref, xy_ref)


def fold_body(s, before_ref, from_x_ref, from_y_ref, from_xy_ref, own_ref, *refs):
    del before_ref
    block_ref, *msg_refs, total_ref, x_ref, y_ref, xy_ref, low_ref, high_ref = refs
    x_part, y_part, corner = get_sides(s, (from_x_ref, from_y_ref, from_xy_ref), x_ref, y_ref, xy_ref)
    total = from_columns(s, [corner, x_part, y_part, own_ref[...]])
    total_ref[...] = total
    add_sides(s, block_ref, x_ref, y_ref, xy_ref)
    half = 4 * s.own
    for x in range(s.bx):
        high_ref[x * s.by : (x + 1) * s.by] = block_ref[x, :, s.bz, :]
    blank(high_ref, s.z_rows)
    blank(low_ref, 0)
    put_split(low_ref, 0, total[0:half])
    put_split(high_ref, s.z_rows, total[half:])
    put_z(s, msg_refs, low_ref, high_ref)


def last_body(s, start_ref, block_ref, total_ref, by_node_ref, *refs):
    count = 2 - s.pairs
    received, refs = refs[:count], refs[count:]
    out_hbm, above_ref, below_ref, plane_ref, out_ref, sems = refs
    get_z(s, received, above_ref, below_ref)
    half = 4 * s.own
    total = total_ref[...] + jnp.concatenate([get_split(below_ref, s.z_rows, half), get_split(above_ref, 0, half)], axis=0)
    stack = stacked(total)
    copies = []
    for x in range(s.bx):
        image = jnp.dot(by_node_ref[x], stack, preferred_element_type=F32)
        plane_ref[x] = image.reshape(s.by, s.bzp, s.waves) + block_ref[x]
        plane_ref[x, :, 0, :] += below_ref[x * s.by : (x + 1) * s.by]
        out_ref[x] = 2.0 * plane_ref[x, :, 0 : s.bz] - start_ref[x]
        if (x + 1) % s.few_out == 0:
            span = pl.ds(x + 1 - s.few_out, s.few_out)
            copies.append(pltpu.make_async_copy(out_ref.at[span], out_hbm.at[span], sems.at[x // s.few_out]))
            copies[-1].start()
    for copy in copies:
        copy.wait()


def selector(count, chosen):
    row = lax.broadcasted_iota(jnp.int32, count, 0)
    column = lax.broadcasted_iota(jnp.int32, count, 1)
    return chosen(row, column).astype(F32).astype(BF16)


def matrix_body(s, part, matrix_hbm, out_ref, raw_ref, flat_ref, half_ref, sems):
    cells_y, cells_z = s.cells[1:]
    side, group = s.side, s.group
    nodes = side**3
    copies = [pltpu.make_async_copy(matrix_hbm.at[part, j], raw_ref.at[j], sems.at[j]) for j in range(cells_y)]
    for copy in copies:
        copy.start()
    wide = 256 // group * side
    spans = []
    for first in range(0, s.padded, 256):
        low = first // group * side // 128 * 128
        high = min(nodes, first // group * side + wide)
        width = min(256, s.padded - first)
        spans.append((first, low, high, selector((high - low, width), lambda m, c, low=low, first=first: (
            ((c + first) % group < side) & (m + low == (c + first) // group * side + (c + first) % group)))))
    tall = 128 // group * side
    picks = jnp.concatenate(
        [
            selector((128, tall * cells_z), lambda r, m, k=k: (r % group < side) & (m == (r // group * side + r % group) * cells_z + k))
            for k in range(cells_z)
        ],
        axis=0,
    )
    for j in range(cells_y):
        copies[j].wait()
        flat_ref[...] = raw_ref[j].reshape(nodes * cells_z, nodes)
        for first, low, high, spread in spans:
            half = jnp.dot(flat_ref[:, low:high], spread, preferred_element_type=F32)
            half_ref[:, first : first + spread.shape[1]] = half.astype(BF16)
        for first in range(0, s.padded, 128):
            count = min(128, s.padded - first)
            low = first // group * side * cells_z
            high = min(nodes * cells_z, low + tall * cells_z)
            rows = jnp.dot(picks[:, 0 : high - low], half_ref[low:high], preferred_element_type=F32).astype(BF16)
            for k in range(cells_z):
                out_ref[j, k, first : first + count] = rows[128 * k : 128 * k + count]


def regrouped(s, cell_matrices, part):
    shape = cell_matrices.shape
    nodes = shape[3]
    return call(
        matrix_body,
        s,
        [jax.ShapeDtypeStruct(shape[1:3] + (s.padded, s.padded), BF16)],
        [
            pltpu.VMEM((shape[1], nodes, shape[2], nodes), BF16),
            pltpu.VMEM((nodes * shape[2], nodes), BF16),
            pltpu.VMEM((nodes * shape[2], s.padded), BF16),
            pltpu.SemaphoreType.DMA((shape[1],)),
        ],
        [cell_matrices.transpose(0, 1, 3, 2, 4)],
        spaces={0: pltpu.HBM},
        extra=(part,),
    )[0]


def along_z(s, msgs):
    if s.pairs:
        return [shifted(msgs[0], (0, 0, 1))]
    return [shifted(msgs[0], (0, 0, -1)), shifted(msgs[1], (0, 0, 1))]


def along_xy(msgs, by):
    return [shifted(msg, (by * dx, by * dy, 0)) for msg, dx, dy in zip(msgs, (1, 0, 1), (0, 1, 1))]


def local(wavefunctions, cell_matrices, projectors, slot_atoms, atom_coupling):
    atom_count = atom_coupling.shape[0]
    devices = 1
    for axis in AXES:
        devices *= lax.axis_size(axis)
    own = atom_count // devices
    s = Sizes(wavefunctions.shape, cell_matrices.shape, own, lax.axis_size("gz") == 2)
    ids = local_atoms(own)[:, None]
    plane = s.by * s.bzp
    sides = s.side_rows()
    field, by_atom, wide, *msgs, total, weight = call(
        first_body,
        s,
        [
            s.extended(),
            jax.ShapeDtypeStruct((s.bx, 2 * s.locals, plane), BF16),
            jax.ShapeDtypeStruct((s.z_rows, s.bzp, 2 * s.locals), F32),
        ]
        + s.z_msgs(s.z_both, s.z_sums)
        + [s.rows(s.locals), s.rows(s.locals)],
        [
            s.scratch(s.bx, s.by, s.bz),
            pltpu.VMEM(projectors.shape, F32),
            pltpu.VMEM(slot_atoms.shape, jnp.int32),
            pltpu.VMEM((1, atom_count), F32),
            pltpu.VMEM((s.bx * s.by * s.bz, 2 * s.locals), F32),
            s.scratch(s.z_both),
            s.scratch(s.z_sums),
            pltpu.SemaphoreType.DMA((1,)),
            pltpu.SemaphoreType.DMA((3,)),
        ],
        [wavefunctions, projectors, slot_atoms, atom_coupling[None, :], ids],
        spaces={0: pltpu.HBM, 1: pltpu.HBM, 2: pltpu.HBM, 3: pltpu.HBM},
    )
    matrices = [regrouped(s, cell_matrices, part) for part in range(s.cells[0])]
    received = along_z(s, msgs)
    field, *msgs, part = call(
        first_down_body,
        s,
        [s.extended()] + s.side_msgs() + [s.rows(2 * own)],
        [s.scratch(s.z_both), s.scratch(s.z_sums)] + sides,
        [field, total, matrices[0]] + received,
        aliases={0: 0},
    )

    def cells(field, msgs, part):
        received = along_xy(msgs, -1)
        _, sums, *msgs, mine = call(
            cell_body,
            s,
            [s.extended(), jax.ShapeDtypeStruct((s.cells[2], s.bx + 1, s.by + 1, s.group, s.waves), F32)]
            + s.side_msgs()
            + [s.rows(2 * own)],
            sides,
            [field] + received + [part, weight] + matrices,
            aliases={0: 0},
        )
        received = along_xy(msgs, 1)
        (block,) = call(join_cells, s, [s.block()], [], [sums])
        return block, received, mine

    block, received, mine = cells(field, msgs, part)
    by_node, lowest, lowest_by_node = call(
        node_body,
        s,
        [
            jax.ShapeDtypeStruct((s.bx, plane, 3 * s.locals), BF16),
            jax.ShapeDtypeStruct((2 * s.locals, s.z_plane), BF16),
            jax.ShapeDtypeStruct((s.z_rows, 3 * s.locals), BF16),
        ],
        [],
        [wide],
    )
    msgs = call(
        swap_body,
        s,
        s.z_msgs(s.z_plane, s.z_plane),
        sides + [s.scratch(s.z_plane), s.scratch(s.z_plane)],
        [block] + received + [mine, lowest_by_node],
    )
    swapped = along_z(s, msgs)
    (field,) = call(middle_body, s, [s.extended()], sides, [block] + received + [mine, by_node])
    received = swapped
    (total,) = call(sums_body, s, [s.rows(s.locals)], [], [field, by_atom])
    field, *msgs, part = call(
        second_down_body,
        s,
        [s.extended()] + s.side_msgs() + [s.rows(2 * own)],
        [s.scratch(s.z_plane), s.scratch(s.z_plane)] + sides,
        [field, total, lowest] + received,
        aliases={0: 0},
    )
    block, received, mine = cells(field, msgs, part)
    block, *msgs, total = call(
        fold_body,
        s,
        [s.block()] + s.z_msgs(s.z_sums, s.z_both) + [s.rows(s.locals)],
        sides + [s.scratch(s.z_sums), s.scratch(s.z_both)],
        [block] + received + [mine],
        aliases={0: 0},
    )
    received = along_z(s, msgs)
    (out,) = call(
        last_body,
        s,
        [jax.ShapeDtypeStruct(wavefunctions.shape, F32)],
        [
            s.scratch(s.z_sums),
            s.scratch(s.z_both),
            s.scratch(s.bx, s.by, s.bzp),
            s.scratch(s.bx, s.by, s.bz),
            pltpu.SemaphoreType.DMA((s.bx // s.few_out,)),
        ],
        [wavefunctions, block, total, by_node] + received,
        out_spaces={0: pltpu.HBM},
    )
    return out


def solution(mesh):
    return jax.shard_map(
        local,
        mesh=mesh,
        in_specs=(
            P("gx", "gy", "gz", None),
            P("gx", "gy", "gz", None, None),
            P(("gx", "gy", "gz"), None, None),
            P(("gx", "gy", "gz"), None),
            P(),
        ),
        out_specs=P("gx", "gy", "gz", None),
        check_vma=False,
    )
```

```python
import functools

import jax
import jax.numpy as jnp
from jax import lax
from jax.experimental import pallas as pl
from jax.experimental.pallas import tpu as pltpu
from jax.sharding import PartitionSpec as P

AXES = ("gx", "gy", "gz")
F32 = jnp.float32
BF16 = jnp.bfloat16
LIMIT = 12 * 1024 * 1024


def up_to(value, unit):
    return -(-value // unit) * unit


def shifted(value, shift):
    sizes = [lax.axis_size(axis) for axis in AXES]
    pairs = []
    for x in range(sizes[0]):
        for y in range(sizes[1]):
            for z in range(sizes[2]):
                here = (x * sizes[1] + y) * sizes[2] + z
                there = [(p + s) % n for p, s, n in zip((x, y, z), shift, sizes)]
                pairs.append((here, (there[0] * sizes[1] + there[1]) * sizes[2] + there[2]))
    return lax.ppermute(value, AXES, pairs)


def halves(value):
    high = value.astype(BF16).astype(F32)
    return high, value - high


def put_split(rows_ref, start, value):
    count = value.shape[0]
    high, low = halves(value)
    rows_ref[start : start + count] = high
    rows_ref[start + count : start + 2 * count] = low


def get_split(rows_ref, start, count):
    return rows_ref[start : start + count] + rows_ref[start + count : start + 2 * count]


class Sizes:
    def __init__(self, field_shape, cell_shape, own, pairs):
        self.bx, self.by, self.bz, self.waves = field_shape
        self.cells = cell_shape[:3]
        self.order = self.bx // cell_shape[0]
        self.side = self.order + 1
        self.group = up_to(self.side, 8)
        self.padded = up_to(self.side * self.side * self.group, 16)
        self.bzp = up_to(max(self.bz + 1, (cell_shape[2] - 1) * self.order + self.group), 16)
        self.few_out = max(n for n in (1, 2) if self.bx % n == 0)
        self.pairs = pairs
        self.own = own
        self.locals = 8 * own
        self.span = self.bz + 1
        self.z_rows = self.bx * self.by
        self.x_rows = self.by * self.span
        self.y_rows = self.bx * self.span
        self.x_msg = up_to(self.x_rows + 4 * own, 8)
        self.y_msg = up_to(self.y_rows + 4 * own, 8)
        self.xy_msg = up_to(self.span + 4 * own, 8)
        self.z_plane = up_to(self.z_rows, 16)
        self.z_sums = up_to(8 * own, 16)
        self.z_both = up_to(self.z_rows + 8 * own, 16)

    def extended(self):
        return jax.ShapeDtypeStruct((self.bx + 1, self.by + 1, self.bzp, self.waves), F32)

    def block(self):
        return jax.ShapeDtypeStruct((self.bx, self.by, self.bzp, self.waves), F32)

    def rows(self, count, dtype=F32):
        return jax.ShapeDtypeStruct((count, self.waves), dtype)

    def scratch(self, *shape):
        return pltpu.VMEM(shape + (self.waves,), F32)

    def z_msgs(self, down, up):
        return [self.rows(down + up, BF16)] if self.pairs else [self.rows(down, BF16), self.rows(up, BF16)]

    def side_msgs(self):
        return [self.rows(n, BF16) for n in (self.x_msg, self.y_msg, self.xy_msg)]

    def side_rows(self):
        return [self.scratch(n) for n in (self.x_msg, self.y_msg, self.xy_msg)]


VMEM = pltpu.VMEM


def call(body, sizes, outs, scratch, args, spaces=None, out_spaces=None, aliases=None, extra=()):
    spaces = spaces or {}
    out_spaces = out_spaces or {}
    outs = [out_spaces.get(n, VMEM)(out.shape, out.dtype) for n, out in enumerate(outs)]
    args = [pltpu.with_memory_space_constraint(arg, spaces.get(n, VMEM)) for n, arg in enumerate(args)]
    return pl.pallas_call(
        functools.partial(body, sizes, *extra),
        out_shape=outs,
        in_specs=[pl.BlockSpec(memory_space=spaces.get(n, VMEM)) for n in range(len(args))],
        out_specs=[pl.BlockSpec(memory_space=out_spaces.get(n, VMEM)) for n in range(len(outs))],
        scratch_shapes=scratch,
        input_output_aliases=aliases or {},
        compiler_params=pltpu.CompilerParams(vmem_limit_bytes=LIMIT),
    )(*args)


def local_atoms(own):
    sizes = [lax.axis_size(axis) for axis in AXES]
    here = [lax.axis_index(axis) for axis in AXES]
    ids = []
    for dz in (1, 0):
        for dx in (1, 0):
            for dy in (1, 0):
                x, y, z = (lax.rem(h + n - d, n) for h, n, d in zip(here, sizes, (dx, dy, dz)))
                owner = (x * sizes[1] + y) * sizes[2] + z
                ids += [owner * own + a for a in range(own)]
    return jnp.stack(ids).astype(jnp.int32)


def blank(rows_ref, first):
    count = rows_ref.shape[0] - first
    if count:
        rows_ref[first:] = jnp.zeros((count,) + rows_ref.shape[1:], F32)


def split_sums(by_atom, count, field):
    high = field.astype(BF16)
    low = (field - high.astype(F32)).astype(BF16)
    with_high = jnp.dot(by_atom, high, preferred_element_type=F32)
    with_low = jnp.dot(by_atom[0:count], low, preferred_element_type=F32)
    return with_high[0:count] + with_high[count : 2 * count] + with_low


def put_z(s, msg_refs, down_ref, up_ref):
    if s.pairs:
        count = down_ref.shape[0]
        msg_refs[0][0:count] = down_ref[...].astype(BF16)
        msg_refs[0][count:] = up_ref[...].astype(BF16)
    else:
        msg_refs[0][...] = down_ref[...].astype(BF16)
        msg_refs[1][...] = up_ref[...].astype(BF16)


def get_z(s, msg_refs, above_ref, below_ref):
    if s.pairs:
        count = above_ref.shape[0]
        above_ref[...] = msg_refs[0][0:count].astype(F32)
        below_ref[...] = msg_refs[0][count:].astype(F32)
    else:
        above_ref[...] = msg_refs[0][...].astype(F32)
        below_ref[...] = msg_refs[1][...].astype(F32)


def columns(s, totals):
    own, half = s.own, 4 * s.own
    return [
        jnp.concatenate([totals[n * own : (n + 1) * own], totals[half + n * own : half + (n + 1) * own]], axis=0) for n in range(4)
    ]


def from_columns(s, parts):
    own = s.own
    return jnp.concatenate([part[0:own] for part in parts] + [part[own : 2 * own] for part in parts], axis=0)


def first_body(
    s, start_hbm, rows_hbm, slots_hbm, coupling_hbm, ids_ref,
    field_ref, by_atom_ref, wide_ref, *refs
):
    *msg_refs, total_ref, weight_ref, start_ref, rows_ref, slots_ref, coupling_ref, tall_ref, low_ref, high_ref, sems, small_sems = refs
    small = [
        pltpu.make_async_copy(rows_hbm, rows_ref, small_sems.at[0]),
        pltpu.make_async_copy(slots_hbm, slots_ref, small_sems.at[1]),
        pltpu.make_async_copy(coupling_hbm, coupling_ref, small_sems.at[2]),
    ]
    for copy in small:
        copy.start()
    whole = pltpu.make_async_copy(start_hbm, start_ref, sems.at[0])
    whole.start()
    for copy in small:
        copy.wait()
    chosen = (ids_ref[...] == slots_ref[...]).astype(F32).astype(BF16)
    rows = rows_ref[0]
    high = rows.astype(BF16)
    low = (rows - high.astype(F32)).astype(BF16)
    parts = [jnp.dot(chosen, part, preferred_element_type=F32) for part in (high, low)]
    tall_ref[...] = jnp.concatenate(parts, axis=0).T
    wide_ref[:, s.bz : s.bzp, :] = jnp.zeros((s.bx * s.by, s.bzp - s.bz, 2 * s.locals), F32)
    for g in range(s.bx * s.by):
        wide_ref[g, 0 : s.bz, :] = tall_ref[g * s.bz : (g + 1) * s.bz, :]
    for x in range(s.bx):
        wide = wide_ref[x * s.by : (x + 1) * s.by].reshape(s.by * s.bzp, 2 * s.locals)
        by_atom_ref[x] = wide.T.astype(BF16)
    total = jnp.zeros((s.locals, s.waves), F32)
    whole.wait()
    for x in range(s.bx):
        plane = jnp.concatenate([start_ref[x], jnp.zeros((s.by, s.bzp - s.bz, s.waves), F32)], axis=1)
        field_ref[x, 0 : s.by] = plane
        total = total + split_sums(by_atom_ref[x], s.locals, plane.reshape(s.by * s.bzp, s.waves))
    total_ref[...] = total
    half = 4 * s.own
    for x in range(s.bx):
        low_ref[x * s.by : (x + 1) * s.by] = field_ref[x, 0 : s.by, 0, :]
    blank(low_ref, s.z_rows)
    blank(high_ref, 0)
    put_split(low_ref, s.z_rows, total[0:half])
    put_split(high_ref, 0, total[half:])
    put_z(s, msg_refs, low_ref, high_ref)
    atoms = lax.broadcasted_iota(jnp.int32, (s.locals, coupling_ref.shape[1]), 1)
    weight = jnp.sum(jnp.where(atoms == ids_ref[...], coupling_ref[...], 0.0), axis=1, keepdims=True)
    weight_ref[...] = jnp.broadcast_to(weight, weight_ref.shape)


def node_body(s, wide_ref, by_node_ref, lowest_ref, lowest_by_node_ref):
    for x in range(s.bx):
        wide = wide_ref[x * s.by : (x + 1) * s.by].reshape(s.by * s.bzp, 2 * s.locals)
        by_node_ref[x] = jnp.concatenate([wide, wide[:, 0 : s.locals]], axis=1).astype(BF16)
    line = wide_ref[:, 0, :]
    lowest_by_node_ref[...] = jnp.concatenate([line, line[:, 0 : s.locals]], axis=1).astype(BF16)
    lowest = line.T
    if s.z_plane > s.z_rows:
        lowest = jnp.concatenate([lowest, jnp.zeros((2 * s.locals, s.z_plane - s.z_rows), F32)], axis=1)
    lowest_ref[...] = lowest.astype(BF16)


def put_sides(s, field_ref, x, y, x_ref, y_ref, xy_ref):
    for n in range(s.by):
        x_ref[n * s.span : (n + 1) * s.span] = field_ref[x, n, 0 : s.span, :]
    for n in range(s.bx):
        y_ref[n * s.span : (n + 1) * s.span] = field_ref[n, y, 0 : s.span, :]
    xy_ref[0 : s.span] = field_ref[x, y, 0 : s.span, :]
    for ref, used in ((x_ref, s.x_rows), (y_ref, s.y_rows), (xy_ref, s.span)):
        blank(ref, used)


def send_sides(s, x_ref, y_ref, xy_ref, msg_refs, parts):
    for ref, used, part, msg_ref in zip((x_ref, y_ref, xy_ref), (s.x_rows, s.y_rows, s.span), parts, msg_refs):
        put_split(ref, used, part)
        msg_ref[...] = ref[...].astype(BF16)


def get_sides(s, received, x_ref, y_ref, xy_ref):
    parts = []
    for ref, used, msg_ref in zip((x_ref, y_ref, xy_ref), (s.x_rows, s.y_rows, s.span), received):
        ref[...] = msg_ref[...].astype(F32)
        parts.append(get_split(ref, used, 2 * s.own))
    return parts


def add_sides(s, field_ref, x_ref, y_ref, xy_ref):
    for n in range(s.by):
        field_ref[0, n, 0 : s.span, :] += x_ref[n * s.span : (n + 1) * s.span]
    for n in range(s.bx):
        field_ref[n, 0, 0 : s.span, :] += y_ref[n * s.span : (n + 1) * s.span]
    field_ref[0, 0, 0 : s.span, :] += xy_ref[0 : s.span]


def send_down(s, total, field_ref, msg_refs, part_ref, x_ref, y_ref, xy_ref):
    put_sides(s, field_ref, 0, 0, x_ref, y_ref, xy_ref)
    corner, x_part, y_part, own_part = columns(s, total)
    part_ref[...] = own_part
    send_sides(s, x_ref, y_ref, xy_ref, msg_refs, (x_part, y_part, corner))


def first_down_body(s, before_ref, total_ref, early_ref, *refs):
    del before_ref, early_ref
    count = 2 - s.pairs
    received, refs = refs[:count], refs[count:]
    field_ref, *msg_refs, part_ref, above_ref, below_ref, x_ref, y_ref, xy_ref = refs
    get_z(s, received, above_ref, below_ref)
    half = 4 * s.own
    total = total_ref[...] + jnp.concatenate([get_split(below_ref, 0, half), get_split(above_ref, s.z_rows, half)], axis=0)
    for x in range(s.bx):
        field_ref[x, 0 : s.by, s.bz, :] = above_ref[x * s.by : (x + 1) * s.by]
    send_down(s, total, field_ref, msg_refs, part_ref, x_ref, y_ref, xy_ref)


def cell_body(s, before_ref, from_x_ref, from_y_ref, from_xy_ref, part_ref, weight_ref, *refs):
    matrix_refs, refs = refs[: s.cells[0]], refs[s.cells[0] :]
    field_ref, sums_ref, *msg_refs, own_ref, x_ref, y_ref, xy_ref = refs
    del before_ref
    parts = get_sides(s, (from_x_ref, from_y_ref, from_xy_ref), x_ref, y_ref, xy_ref)
    rest = jnp.zeros((s.bzp - s.span, s.waves), F32)
    for n in range(s.by):
        field_ref[s.bx, n, 0 : s.span, :] = x_ref[n * s.span : (n + 1) * s.span]
        field_ref[s.bx, n, s.span :, :] = rest
    for n in range(s.bx):
        field_ref[n, s.by, 0 : s.span, :] = y_ref[n * s.span : (n + 1) * s.span]
        field_ref[n, s.by, s.span :, :] = rest
    field_ref[s.bx, s.by, 0 : s.span, :] = xy_ref[0 : s.span]
    field_ref[s.bx, s.by, s.span :, :] = rest
    weight = columns(s, weight_ref[...])[3]
    total = (part_ref[...] + parts[0] + parts[1] + parts[2]) * weight
    own_ref[...] = total
    apply_cells(s, field_ref, matrix_refs, sums_ref)
    join_sides(s, sums_ref, x_ref, y_ref, xy_ref)
    send_sides(s, x_ref, y_ref, xy_ref, msg_refs, (total, total, total))


def apply_cells(s, field_ref, matrix_refs, sums_ref):
    order, side, group = s.order, s.side, s.group
    used = side * side * group
    for i in range(s.cells[0]):
        for j in range(s.cells[1]):
            for k in range(s.cells[2]):
                first = k * order
                values = field_ref[i * order : i * order + side, j * order : j * order + side, first : first + group]
                values = values.reshape(used, s.waves)
                if s.padded > used:
                    values = jnp.concatenate([values, jnp.zeros((s.padded - used, s.waves), F32)], axis=0)
                product = jnp.dot(matrix_refs[i][j, k], values.astype(BF16), preferred_element_type=F32)
                product = product[0:used].reshape(side, side, group, s.waves)
                x0, x1, y0, y1 = i * order, i * order + side, j * order, j * order + side
                a, b = int(i > 0), int(j > 0)
                sums_ref[k, x0 + a : x1, y0 + b : y1] = product[a:, b:]
                if a:
                    sums_ref[k, x0, y0 + b : y1] += product[0, b:]
                if b:
                    sums_ref[k, x0 + a : x1, y0] += product[a:, 0]
                if a and b:
                    sums_ref[k, x0, y0] += product[0, 0]


def join_cells(s, sums_ref, out_ref):
    count = s.by
    for x in range(s.bx):
        out_ref[x, :, 0 : s.group, :] = sums_ref[0, x, 0:count]
        out_ref[x, :, s.group :, :] = jnp.zeros((count, s.bzp - s.group, s.waves), F32)
        for k in range(1, s.cells[2]):
            out_ref[x, :, k * s.order : k * s.order + s.group, :] += sums_ref[k, x, 0:count]


def join_sides(s, sums_ref, x_ref, y_ref, xy_ref):
    last = s.cells[2] - 1

    def join(rows_ref, at, x, y):
        for k in range(s.cells[2]):
            count = s.order + int(k == last)
            first = at + k * s.order
            rows_ref[first : first + count] = sums_ref[k, x, y, 0:count, :]
            if k:
                rows_ref[first : first + 1] += sums_ref[k - 1, x, y, s.order : s.order + 1, :]

    for n in range(s.by):
        join(x_ref, n * s.span, s.bx, n)
    for n in range(s.bx):
        join(y_ref, n * s.span, n, s.by)
    join(xy_ref, 0, s.bx, s.by)
    for ref, used in ((x_ref, s.x_rows), (y_ref, s.y_rows), (xy_ref, s.span)):
        blank(ref, used)


def stacked(totals):
    high, low = halves(totals)
    return jnp.concatenate([high, high, low], axis=0).astype(BF16)


def swap_body(s, block_ref, from_x_ref, from_y_ref, from_xy_ref, own_ref, lowest_by_node_ref, *refs):
    *msg_refs, x_ref, y_ref, xy_ref, low_ref, high_ref = refs
    x_part, y_part, corner = get_sides(s, (from_x_ref, from_y_ref, from_xy_ref), x_ref, y_ref, xy_ref)
    stack = stacked(from_columns(s, [corner, x_part, y_part, own_ref[...]]))
    low_ref[0 : s.z_rows] = jnp.dot(lowest_by_node_ref[...], stack, preferred_element_type=F32)
    for x in range(s.bx):
        low_ref[x * s.by : (x + 1) * s.by] += block_ref[x, :, 0, :]
        high_ref[x * s.by : (x + 1) * s.by] = block_ref[x, :, s.bz, :]
    for ref, z in ((low_ref, 0), (high_ref, s.bz)):
        for n in range(s.by):
            ref[n : n + 1] += x_ref[n * s.span + z : n * s.span + z + 1]
        for n in range(s.bx):
            ref[n * s.by : n * s.by + 1] += y_ref[n * s.span + z : n * s.span + z + 1]
        ref[0:1] += xy_ref[z : z + 1]
        blank(ref, s.z_rows)
    put_z(s, msg_refs, low_ref, high_ref)


def middle_body(s, block_ref, from_x_ref, from_y_ref, from_xy_ref, own_ref, by_node_ref, field_ref, x_ref, y_ref, xy_ref):
    x_part, y_part, corner = get_sides(s, (from_x_ref, from_y_ref, from_xy_ref), x_ref, y_ref, xy_ref)
    stack = stacked(from_columns(s, [corner, x_part, y_part, own_ref[...]]))
    for x in range(s.bx):
        image = jnp.dot(by_node_ref[x], stack, preferred_element_type=F32)
        field_ref[x, 0 : s.by] = image.reshape(s.by, s.bzp, s.waves) + block_ref[x]
    add_sides(s, field_ref, x_ref, y_ref, xy_ref)


def sums_body(s, field_ref, by_atom_ref, total_ref):
    total = jnp.zeros((s.locals, s.waves), F32)
    for x in range(s.bx):
        total = total + split_sums(by_atom_ref[x], s.locals, field_ref[x, 0 : s.by].reshape(s.by * s.bzp, s.waves))
    total_ref[...] = total


def second_down_body(s, before_ref, total_ref, lowest_ref, *refs):
    del before_ref
    count = 2 - s.pairs
    received, refs = refs[:count], refs[count:]
    field_ref, *msg_refs, part_ref, above_ref, below_ref, x_ref, y_ref, xy_ref = refs
    get_z(s, received, above_ref, below_ref)
    for x in range(s.bx):
        field_ref[x, 0 : s.by, s.bz, :] += above_ref[x * s.by : (x + 1) * s.by]
        field_ref[x, 0 : s.by, 0, :] += below_ref[x * s.by : (x + 1) * s.by]
    total = total_ref[...] + split_sums(lowest_ref[...], s.locals, below_ref[...])
    send_down(s, total, field_ref, msg_refs, part_ref, x_ref, y_ref, xy_ref)


def fold_body(s, before_ref, from_x_ref, from_y_ref, from_xy_ref, own_ref, *refs):
    del before_ref
    block_ref, *msg_refs, total_ref, x_ref, y_ref, xy_ref, low_ref, high_ref = refs
    x_part, y_part, corner = get_sides(s, (from_x_ref, from_y_ref, from_xy_ref), x_ref, y_ref, xy_ref)
    total = from_columns(s, [corner, x_part, y_part, own_ref[...]])
    total_ref[...] = total
    add_sides(s, block_ref, x_ref, y_ref, xy_ref)
    half = 4 * s.own
    for x in range(s.bx):
        high_ref[x * s.by : (x + 1) * s.by] = block_ref[x, :, s.bz, :]
    blank(high_ref, s.z_rows)
    blank(low_ref, 0)
    put_split(low_ref, 0, total[0:half])
    put_split(high_ref, s.z_rows, total[half:])
    put_z(s, msg_refs, low_ref, high_ref)


def last_body(s, start_ref, block_ref, total_ref, by_node_ref, *refs):
    count = 2 - s.pairs
    received, refs = refs[:count], refs[count:]
    out_hbm, above_ref, below_ref, plane_ref, out_ref, sems = refs
    get_z(s, received, above_ref, below_ref)
    half = 4 * s.own
    total = total_ref[...] + jnp.concatenate([get_split(below_ref, s.z_rows, half), get_split(above_ref, 0, half)], axis=0)
    stack = stacked(total)
    copies = []
    for x in range(s.bx):
        image = jnp.dot(by_node_ref[x], stack, preferred_element_type=F32)
        plane_ref[x] = image.reshape(s.by, s.bzp, s.waves) + block_ref[x]
        plane_ref[x, :, 0, :] += below_ref[x * s.by : (x + 1) * s.by]
        out_ref[x] = 2.0 * plane_ref[x, :, 0 : s.bz] - start_ref[x]
        if (x + 1) % s.few_out == 0:
            span = pl.ds(x + 1 - s.few_out, s.few_out)
            copies.append(pltpu.make_async_copy(out_ref.at[span], out_hbm.at[span], sems.at[x // s.few_out]))
            copies[-1].start()
    for copy in copies:
        copy.wait()


def selector(count, chosen):
    row = lax.broadcasted_iota(jnp.int32, count, 0)
    column = lax.broadcasted_iota(jnp.int32, count, 1)
    return chosen(row, column).astype(F32).astype(BF16)


def matrix_body(s, part, matrix_hbm, out_ref, raw_ref, flat_ref, half_ref, sems):
    cells_y, cells_z = s.cells[1:]
    side, group = s.side, s.group
    nodes = side**3
    copies = [pltpu.make_async_copy(matrix_hbm.at[part, j], raw_ref.at[j], sems.at[j]) for j in range(cells_y)]
    for copy in copies:
        copy.start()
    wide = 256 // group * side
    spans = []
    for first in range(0, s.padded, 256):
        low = first // group * side // 128 * 128
        high = min(nodes, first // group * side + wide)
        width = min(256, s.padded - first)
        spans.append((first, low, high, selector((high - low, width), lambda m, c, low=low, first=first: (
            ((c + first) % group < side) & (m + low == (c + first) // group * side + (c + first) % group)))))
    tall = 128 // group * side
    picks = jnp.concatenate(
        [
            selector((128, tall * cells_z), lambda r, m, k=k: (r % group < side) & (m == (r // group * side + r % group) * cells_z + k))
            for k in range(cells_z)
        ],
        axis=0,
    )
    for j in range(cells_y):
        copies[j].wait()
        flat_ref[...] = raw_ref[j].reshape(nodes * cells_z, nodes)
        for first, low, high, spread in spans:
            half = jnp.dot(flat_ref[:, low:high], spread, preferred_element_type=F32)
            half_ref[:, first : first + spread.shape[1]] = half.astype(BF16)
        for first in range(0, s.padded, 128):
            count = min(128, s.padded - first)
            low = first // group * side * cells_z
            high = min(nodes * cells_z, low + tall * cells_z)
            rows = jnp.dot(picks[:, 0 : high - low], half_ref[low:high], preferred_element_type=F32).astype(BF16)
            for k in range(cells_z):
                out_ref[j, k, first : first + count] = rows[128 * k : 128 * k + count]


def regrouped(s, cell_matrices, part):
    shape = cell_matrices.shape
    nodes = shape[3]
    return call(
        matrix_body,
        s,
        [jax.ShapeDtypeStruct(shape[1:3] + (s.padded, s.padded), BF16)],
        [
            pltpu.VMEM((shape[1], nodes, shape[2], nodes), BF16),
            pltpu.VMEM((nodes * shape[2], nodes), BF16),
            pltpu.VMEM((nodes * shape[2], s.padded), BF16),
            pltpu.SemaphoreType.DMA((shape[1],)),
        ],
        [cell_matrices.transpose(0, 1, 3, 2, 4)],
        spaces={0: pltpu.HBM},
        extra=(part,),
    )[0]


def along_z(s, msgs):
    if s.pairs:
        return [shifted(msgs[0], (0, 0, 1))]
    return [shifted(msgs[0], (0, 0, -1)), shifted(msgs[1], (0, 0, 1))]


def along_xy(msgs, by):
    return [shifted(msg, (by * dx, by * dy, 0)) for msg, dx, dy in zip(msgs, (1, 0, 1), (0, 1, 1))]


def local(wavefunctions, cell_matrices, projectors, slot_atoms, atom_coupling):
    atom_count = atom_coupling.shape[0]
    devices = 1
    for axis in AXES:
        devices *= lax.axis_size(axis)
    own = atom_count // devices
    s = Sizes(wavefunctions.shape, cell_matrices.shape, own, lax.axis_size("gz") == 2)
    ids = local_atoms(own)[:, None]
    plane = s.by * s.bzp
    sides = s.side_rows()
    field, by_atom, wide, *msgs, total, weight = call(
        first_body,
        s,
        [
            s.extended(),
            jax.ShapeDtypeStruct((s.bx, 2 * s.locals, plane), BF16),
            jax.ShapeDtypeStruct((s.z_rows, s.bzp, 2 * s.locals), F32),
        ]
        + s.z_msgs(s.z_both, s.z_sums)
        + [s.rows(s.locals), s.rows(s.locals)],
        [
            s.scratch(s.bx, s.by, s.bz),
            pltpu.VMEM(projectors.shape, F32),
            pltpu.VMEM(slot_atoms.shape, jnp.int32),
            pltpu.VMEM((1, atom_count), F32),
            pltpu.VMEM((s.bx * s.by * s.bz, 2 * s.locals), F32),
            s.scratch(s.z_both),
            s.scratch(s.z_sums),
            pltpu.SemaphoreType.DMA((1,)),
            pltpu.SemaphoreType.DMA((3,)),
        ],
        [wavefunctions, projectors, slot_atoms, atom_coupling[None, :], ids],
        spaces={0: pltpu.HBM, 1: pltpu.HBM, 2: pltpu.HBM, 3: pltpu.HBM},
    )
    matrices = [regrouped(s, cell_matrices, part) for part in range(s.cells[0])]
    received = along_z(s, msgs)
    field, *msgs, part = call(
        first_down_body,
        s,
        [s.extended()] + s.side_msgs() + [s.rows(2 * own)],
        [s.scratch(s.z_both), s.scratch(s.z_sums)] + sides,
        [field, total, matrices[0]] + received,
        aliases={0: 0},
    )

    def cells(field, msgs, part):
        received = along_xy(msgs, -1)
        _, sums, *msgs, mine = call(
            cell_body,
            s,
            [s.extended(), jax.ShapeDtypeStruct((s.cells[2], s.bx + 1, s.by + 1, s.group, s.waves), F32)]
            + s.side_msgs()
            + [s.rows(2 * own)],
            sides,
            [field] + received + [part, weight] + matrices,
            aliases={0: 0},
        )
        received = along_xy(msgs, 1)
        (block,) = call(join_cells, s, [s.block()], [], [sums])
        return block, received, mine

    block, received, mine = cells(field, msgs, part)
    by_node, lowest, lowest_by_node = call(
        node_body,
        s,
        [
            jax.ShapeDtypeStruct((s.bx, plane, 3 * s.locals), BF16),
            jax.ShapeDtypeStruct((2 * s.locals, s.z_plane), BF16),
            jax.ShapeDtypeStruct((s.z_rows, 3 * s.locals), BF16),
        ],
        [],
        [wide],
    )
    msgs = call(
        swap_body,
        s,
        s.z_msgs(s.z_plane, s.z_plane),
        sides + [s.scratch(s.z_plane), s.scratch(s.z_plane)],
        [block] + received + [mine, lowest_by_node],
    )
    swapped = along_z(s, msgs)
    (field,) = call(middle_body, s, [s.extended()], sides, [block] + received + [mine, by_node])
    received = swapped
    (total,) = call(sums_body, s, [s.rows(s.locals)], [], [field, by_atom])
    field, *msgs, part = call(
        second_down_body,
        s,
        [s.extended()] + s.side_msgs() + [s.rows(2 * own)],
        [s.scratch(s.z_plane), s.scratch(s.z_plane)] + sides,
        [field, total, lowest] + received,
        aliases={0: 0},
    )
    block, received, mine = cells(field, msgs, part)
    block, *msgs, total = call(
        fold_body,
        s,
        [s.block()] + s.z_msgs(s.z_sums, s.z_both) + [s.rows(s.locals)],
        sides + [s.scratch(s.z_sums), s.scratch(s.z_both)],
        [block] + received + [mine],
        aliases={0: 0},
    )
    received = along_z(s, msgs)
    (out,) = call(
        last_body,
        s,
        [jax.ShapeDtypeStruct(wavefunctions.shape, F32)],
        [
            s.scratch(s.z_sums),
            s.scratch(s.z_both),
            s.scratch(s.bx, s.by, s.bzp),
            s.scratch(s.bx, s.by, s.bz),
            pltpu.SemaphoreType.DMA((s.bx // s.few_out,)),
        ],
        [wavefunctions, block, total, by_node] + received,
        out_spaces={0: pltpu.HBM},
    )
    return out


def solution(mesh):
    return jax.shard_map(
        local,
        mesh=mesh,
        in_specs=(
            P("gx", "gy", "gz", None),
            P("gx", "gy", "gz", None, None),
            P(("gx", "gy", "gz"), None, None),
            P(("gx", "gy", "gz"), None),
            P(),
        ),
        out_specs=P("gx", "gy", "gz", None),
        check_vma=False,
    )
```

```python
import functools

import jax
import jax.numpy as jnp
from jax import lax
from jax.experimental import pallas as pl
from jax.experimental.pallas import tpu as pltpu
from jax.sharding import PartitionSpec as P

AXES = ("gx", "gy", "gz")
F32 = jnp.float32
BF16 = jnp.bfloat16
LIMIT = 12 * 1024 * 1024


def up_to(value, unit):
    return -(-value // unit) * unit


def shifted(value, shift):
    sizes = [lax.axis_size(axis) for axis in AXES]
    pairs = []
    for x in range(sizes[0]):
        for y in range(sizes[1]):
            for z in range(sizes[2]):
                here = (x * sizes[1] + y) * sizes[2] + z
                there = [(p + s) % n for p, s, n in zip((x, y, z), shift, sizes)]
                pairs.append((here, (there[0] * sizes[1] + there[1]) * sizes[2] + there[2]))
    return lax.ppermute(value, AXES, pairs)


def halves(value):
    high = value.astype(BF16).astype(F32)
    return high, value - high


def put_split(rows_ref, start, value):
    count = value.shape[0]
    high, low = halves(value)
    rows_ref[start : start + count] = high
    rows_ref[start + count : start + 2 * count] = low


def get_split(rows_ref, start, count):
    return rows_ref[start : start + count] + rows_ref[start + count : start + 2 * count]


class Sizes:
    def __init__(self, field_shape, cell_shape, own, pairs):
        self.bx, self.by, self.bz, self.waves = field_shape
        self.cells = cell_shape[:3]
        self.order = self.bx // cell_shape[0]
        self.side = self.order + 1
        self.group = up_to(self.side, 8)
        self.padded = up_to(self.side * self.side * self.group, 16)
        self.bzp = up_to(max(self.bz + 1, (cell_shape[2] - 1) * self.order + self.group), 16)
        self.few_out = max(n for n in (1, 2) if self.bx % n == 0)
        self.pairs = pairs
        self.own = own
        self.locals = 8 * own
        self.span = self.bz + 1
        self.z_rows = self.bx * self.by
        self.x_rows = self.by * self.span
        self.y_rows = self.bx * self.span
        self.x_msg = up_to(self.x_rows + 4 * own, 8)
        self.y_msg = up_to(self.y_rows + 4 * own, 8)
        self.xy_msg = up_to(self.span + 4 * own, 8)
        self.z_plane = up_to(self.z_rows, 16)
        self.z_sums = up_to(8 * own, 16)
        self.z_both = up_to(self.z_rows + 8 * own, 16)

    def extended(self):
        return jax.ShapeDtypeStruct((self.bx + 1, self.by + 1, self.bzp, self.waves), F32)

    def block(self):
        return jax.ShapeDtypeStruct((self.bx, self.by, self.bzp, self.waves), F32)

    def rows(self, count, dtype=F32):
        return jax.ShapeDtypeStruct((count, self.waves), dtype)

    def scratch(self, *shape):
        return pltpu.VMEM(shape + (self.waves,), F32)

    def z_msgs(self, down, up):
        return [self.rows(down + up, BF16)] if self.pairs else [self.rows(down, BF16), self.rows(up, BF16)]

    def side_msgs(self):
        return [self.rows(n, BF16) for n in (self.x_msg, self.y_msg, self.xy_msg)]

    def side_rows(self):
        return [self.scratch(n) for n in (self.x_msg, self.y_msg, self.xy_msg)]


VMEM = pltpu.VMEM


def call(body, sizes, outs, scratch, args, spaces=None, out_spaces=None, aliases=None, extra=()):
    spaces = spaces or {}
    out_spaces = out_spaces or {}
    outs = [out_spaces.get(n, VMEM)(out.shape, out.dtype) for n, out in enumerate(outs)]
    args = [pltpu.with_memory_space_constraint(arg, spaces.get(n, VMEM)) for n, arg in enumerate(args)]
    return pl.pallas_call(
        functools.partial(body, sizes, *extra),
        out_shape=outs,
        in_specs=[pl.BlockSpec(memory_space=spaces.get(n, VMEM)) for n in range(len(args))],
        out_specs=[pl.BlockSpec(memory_space=out_spaces.get(n, VMEM)) for n in range(len(outs))],
        scratch_shapes=scratch,
        input_output_aliases=aliases or {},
        compiler_params=pltpu.CompilerParams(vmem_limit_bytes=LIMIT),
    )(*args)


def local_atoms(own, shape):
    sizes = [lax.axis_size(axis) for axis in AXES]
    here = [lax.axis_index(axis) for axis in AXES]
    ids = []
    for dz in (1, 0):
        for dx in (1, 0):
            for dy in (1, 0):
                x, y, z = (lax.rem(h + n - d, n) for h, n, d in zip(here, sizes, (dx, dy, dz)))
                owner = (x * sizes[1] + y) * sizes[2] + z
                ids += [owner * own + a for a in range(own)]
    row = lax.broadcasted_iota(jnp.int32, shape, 0)
    table = jnp.zeros(shape, jnp.int32)
    for n, atom in enumerate(ids):
        table = jnp.where(row == n, atom, table)
    return table


def blank(rows_ref, first):
    count = rows_ref.shape[0] - first
    if count:
        rows_ref[first:] = jnp.zeros((count,) + rows_ref.shape[1:], F32)


def split_sums(by_atom, count, field):
    high = field.astype(BF16)
    low = (field - high.astype(F32)).astype(BF16)
    with_high = jnp.dot(by_atom, high, preferred_element_type=F32)
    with_low = jnp.dot(by_atom[0:count], low, preferred_element_type=F32)
    return with_high[0:count] + with_high[count : 2 * count] + with_low


def put_z(s, msg_refs, down_ref, up_ref):
    if s.pairs:
        count = down_ref.shape[0]
        msg_refs[0][0:count] = down_ref[...].astype(BF16)
        msg_refs[0][count:] = up_ref[...].astype(BF16)
    else:
        msg_refs[0][...] = down_ref[...].astype(BF16)
        msg_refs[1][...] = up_ref[...].astype(BF16)


def get_z(s, msg_refs, above_ref, below_ref):
    if s.pairs:
        count = above_ref.shape[0]
        above_ref[...] = msg_refs[0][0:count].astype(F32)
        below_ref[...] = msg_refs[0][count:].astype(F32)
    else:
        above_ref[...] = msg_refs[0][...].astype(F32)
        below_ref[...] = msg_refs[1][...].astype(F32)


def columns(s, totals):
    own, half = s.own, 4 * s.own
    return [
        jnp.concatenate([totals[n * own : (n + 1) * own], totals[half + n * own : half + (n + 1) * own]], axis=0) for n in range(4)
    ]


def from_columns(s, parts):
    own = s.own
    return jnp.concatenate([part[0:own] for part in parts] + [part[own : 2 * own] for part in parts], axis=0)


def first_body(
    s, start_hbm, rows_hbm, slots_hbm, coupling_hbm,
    field_ref, by_atom_ref, wide_ref, *refs
):
    *msg_refs, total_ref, weight_ref, start_ref, rows_ref, slots_ref, coupling_ref, tall_ref, low_ref, high_ref, sems, small_sems = refs
    small = [
        pltpu.make_async_copy(rows_hbm, rows_ref, small_sems.at[0]),
        pltpu.make_async_copy(slots_hbm, slots_ref, small_sems.at[1]),
        pltpu.make_async_copy(coupling_hbm, coupling_ref, small_sems.at[2]),
    ]
    for copy in small:
        copy.start()
    whole = pltpu.make_async_copy(start_hbm, start_ref, sems.at[0])
    whole.start()
    for copy in small:
        copy.wait()
    slots = slots_ref[...]
    chosen = (local_atoms(s.own, (s.locals, slots.shape[1])) == slots).astype(F32).astype(BF16)
    rows = rows_ref[0]
    high = rows.astype(BF16)
    low = (rows - high.astype(F32)).astype(BF16)
    parts = [jnp.dot(chosen, part, preferred_element_type=F32) for part in (high, low)]
    tall_ref[...] = jnp.concatenate(parts, axis=0).T
    wide_ref[:, s.bz : s.bzp, :] = jnp.zeros((s.bx * s.by, s.bzp - s.bz, 2 * s.locals), F32)
    for g in range(s.bx * s.by):
        wide_ref[g, 0 : s.bz, :] = tall_ref[g * s.bz : (g + 1) * s.bz, :]
    for x in range(s.bx):
        wide = wide_ref[x * s.by : (x + 1) * s.by].reshape(s.by * s.bzp, 2 * s.locals)
        by_atom_ref[x] = wide.T.astype(BF16)
    total = jnp.zeros((s.locals, s.waves), F32)
    whole.wait()
    for x in range(s.bx):
        plane = jnp.concatenate([start_ref[x], jnp.zeros((s.by, s.bzp - s.bz, s.waves), F32)], axis=1)
        field_ref[x, 0 : s.by] = plane
        total = total + split_sums(by_atom_ref[x], s.locals, plane.reshape(s.by * s.bzp, s.waves))
    total_ref[...] = total
    half = 4 * s.own
    for x in range(s.bx):
        low_ref[x * s.by : (x + 1) * s.by] = field_ref[x, 0 : s.by, 0, :]
    blank(low_ref, s.z_rows)
    blank(high_ref, 0)
    put_split(low_ref, s.z_rows, total[0:half])
    put_split(high_ref, 0, total[half:])
    put_z(s, msg_refs, low_ref, high_ref)
    atoms = lax.broadcasted_iota(jnp.int32, (s.locals, coupling_ref.shape[1]), 1)
    weight = jnp.sum(jnp.where(atoms == local_atoms(s.own, atoms.shape), coupling_ref[...], 0.0), axis=1, keepdims=True)
    weight_ref[...] = jnp.broadcast_to(weight, weight_ref.shape)


def node_body(s, wide_ref, by_node_ref, lowest_ref, lowest_by_node_ref):
    for x in range(s.bx):
        wide = wide_ref[x * s.by : (x + 1) * s.by].reshape(s.by * s.bzp, 2 * s.locals)
        by_node_ref[x] = jnp.concatenate([wide, wide[:, 0 : s.locals]], axis=1).astype(BF16)
    line = wide_ref[:, 0, :]
    lowest_by_node_ref[...] = jnp.concatenate([line, line[:, 0 : s.locals]], axis=1).astype(BF16)
    lowest = line.T
    if s.z_plane > s.z_rows:
        lowest = jnp.concatenate([lowest, jnp.zeros((2 * s.locals, s.z_plane - s.z_rows), F32)], axis=1)
    lowest_ref[...] = lowest.astype(BF16)


def put_sides(s, field_ref, x, y, x_ref, y_ref, xy_ref):
    for n in range(s.by):
        x_ref[n * s.span : (n + 1) * s.span] = field_ref[x, n, 0 : s.span, :]
    for n in range(s.bx):
        y_ref[n * s.span : (n + 1) * s.span] = field_ref[n, y, 0 : s.span, :]
    xy_ref[0 : s.span] = field_ref[x, y, 0 : s.span, :]
    for ref, used in ((x_ref, s.x_rows), (y_ref, s.y_rows), (xy_ref, s.span)):
        blank(ref, used)


def send_sides(s, x_ref, y_ref, xy_ref, msg_refs, parts):
    for ref, used, part, msg_ref in zip((x_ref, y_ref, xy_ref), (s.x_rows, s.y_rows, s.span), parts, msg_refs):
        put_split(ref, used, part)
        msg_ref[...] = ref[...].astype(BF16)


def get_sides(s, received, x_ref, y_ref, xy_ref):
    parts = []
    for ref, used, msg_ref in zip((x_ref, y_ref, xy_ref), (s.x_rows, s.y_rows, s.span), received):
        ref[...] = msg_ref[...].astype(F32)
        parts.append(get_split(ref, used, 2 * s.own))
    return parts


def add_sides(s, field_ref, x_ref, y_ref, xy_ref):
    for n in range(s.by):
        field_ref[0, n, 0 : s.span, :] += x_ref[n * s.span : (n + 1) * s.span]
    for n in range(s.bx):
        field_ref[n, 0, 0 : s.span, :] += y_ref[n * s.span : (n + 1) * s.span]
    field_ref[0, 0, 0 : s.span, :] += xy_ref[0 : s.span]


def send_down(s, total, field_ref, msg_refs, part_ref, x_ref, y_ref, xy_ref):
    put_sides(s, field_ref, 0, 0, x_ref, y_ref, xy_ref)
    corner, x_part, y_part, own_part = columns(s, total)
    part_ref[...] = own_part
    send_sides(s, x_ref, y_ref, xy_ref, msg_refs, (x_part, y_part, corner))


def first_down_body(s, before_ref, total_ref, early_ref, *refs):
    del before_ref, early_ref
    count = 2 - s.pairs
    received, refs = refs[:count], refs[count:]
    field_ref, *msg_refs, part_ref, above_ref, below_ref, x_ref, y_ref, xy_ref = refs
    get_z(s, received, above_ref, below_ref)
    half = 4 * s.own
    total = total_ref[...] + jnp.concatenate([get_split(below_ref, 0, half), get_split(above_ref, s.z_rows, half)], axis=0)
    for x in range(s.bx):
        field_ref[x, 0 : s.by, s.bz, :] = above_ref[x * s.by : (x + 1) * s.by]
    send_down(s, total, field_ref, msg_refs, part_ref, x_ref, y_ref, xy_ref)


def cell_body(s, before_ref, from_x_ref, from_y_ref, from_xy_ref, part_ref, weight_ref, *refs):
    matrix_refs, refs = refs[: s.cells[0]], refs[s.cells[0] :]
    field_ref, sums_ref, *msg_refs, own_ref, x_ref, y_ref, xy_ref = refs
    del before_ref
    parts = get_sides(s, (from_x_ref, from_y_ref, from_xy_ref), x_ref, y_ref, xy_ref)
    rest = jnp.zeros((s.bzp - s.span, s.waves), F32)
    for n in range(s.by):
        field_ref[s.bx, n, 0 : s.span, :] = x_ref[n * s.span : (n + 1) * s.span]
        field_ref[s.bx, n, s.span :, :] = rest
    for n in range(s.bx):
        field_ref[n, s.by, 0 : s.span, :] = y_ref[n * s.span : (n + 1) * s.span]
        field_ref[n, s.by, s.span :, :] = rest
    field_ref[s.bx, s.by, 0 : s.span, :] = xy_ref[0 : s.span]
    field_ref[s.bx, s.by, s.span :, :] = rest
    weight = columns(s, weight_ref[...])[3]
    total = (part_ref[...] + parts[0] + parts[1] + parts[2]) * weight
    own_ref[...] = total
    apply_cells(s, field_ref, matrix_refs, sums_ref)
    join_sides(s, sums_ref, x_ref, y_ref, xy_ref)
    send_sides(s, x_ref, y_ref, xy_ref, msg_refs, (total, total, total))


def apply_cells(s, field_ref, matrix_refs, sums_ref):
    order, side, group = s.order, s.side, s.group
    used = side * side * group
    for i in range(s.cells[0]):
        for j in range(s.cells[1]):
            for k in range(s.cells[2]):
                first = k * order
                values = field_ref[i * order : i * order + side, j * order : j * order + side, first : first + group]
                values = values.reshape(used, s.waves)
                if s.padded > used:
                    values = jnp.concatenate([values, jnp.zeros((s.padded - used, s.waves), F32)], axis=0)
                product = jnp.dot(matrix_refs[i][j, k], values.astype(BF16), preferred_element_type=F32)
                product = product[0:used].reshape(side, side, group, s.waves)
                x0, x1, y0, y1 = i * order, i * order + side, j * order, j * order + side
                a, b = int(i > 0), int(j > 0)
                sums_ref[k, x0 + a : x1, y0 + b : y1] = product[a:, b:]
                if a:
                    sums_ref[k, x0, y0 + b : y1] += product[0, b:]
                if b:
                    sums_ref[k, x0 + a : x1, y0] += product[a:, 0]
                if a and b:
                    sums_ref[k, x0, y0] += product[0, 0]


def join_cells(s, sums_ref, out_ref):
    count = s.by
    for x in range(s.bx):
        out_ref[x, :, 0 : s.group, :] = sums_ref[0, x, 0:count]
        out_ref[x, :, s.group :, :] = jnp.zeros((count, s.bzp - s.group, s.waves), F32)
        for k in range(1, s.cells[2]):
            out_ref[x, :, k * s.order : k * s.order + s.group, :] += sums_ref[k, x, 0:count]


def join_sides(s, sums_ref, x_ref, y_ref, xy_ref):
    last = s.cells[2] - 1

    def join(rows_ref, at, x, y):
        for k in range(s.cells[2]):
            count = s.order + int(k == last)
            first = at + k * s.order
            rows_ref[first : first + count] = sums_ref[k, x, y, 0:count, :]
            if k:
                rows_ref[first : first + 1] += sums_ref[k - 1, x, y, s.order : s.order + 1, :]

    for n in range(s.by):
        join(x_ref, n * s.span, s.bx, n)
    for n in range(s.bx):
        join(y_ref, n * s.span, n, s.by)
    join(xy_ref, 0, s.bx, s.by)
    for ref, used in ((x_ref, s.x_rows), (y_ref, s.y_rows), (xy_ref, s.span)):
        blank(ref, used)


def stacked(totals):
    high, low = halves(totals)
    return jnp.concatenate([high, high, low], axis=0).astype(BF16)


def swap_body(s, block_ref, from_x_ref, from_y_ref, from_xy_ref, own_ref, lowest_by_node_ref, *refs):
    *msg_refs, x_ref, y_ref, xy_ref, low_ref, high_ref = refs
    x_part, y_part, corner = get_sides(s, (from_x_ref, from_y_ref, from_xy_ref), x_ref, y_ref, xy_ref)
    stack = stacked(from_columns(s, [corner, x_part, y_part, own_ref[...]]))
    low_ref[0 : s.z_rows] = jnp.dot(lowest_by_node_ref[...], stack, preferred_element_type=F32)
    for x in range(s.bx):
        low_ref[x * s.by : (x + 1) * s.by] += block_ref[x, :, 0, :]
        high_ref[x * s.by : (x + 1) * s.by] = block_ref[x, :, s.bz, :]
    for ref, z in ((low_ref, 0), (high_ref, s.bz)):
        for n in range(s.by):
            ref[n : n + 1] += x_ref[n * s.span + z : n * s.span + z + 1]
        for n in range(s.bx):
            ref[n * s.by : n * s.by + 1] += y_ref[n * s.span + z : n * s.span + z + 1]
        ref[0:1] += xy_ref[z : z + 1]
        blank(ref, s.z_rows)
    put_z(s, msg_refs, low_ref, high_ref)


def middle_body(s, block_ref, from_x_ref, from_y_ref, from_xy_ref, own_ref, by_node_ref, field_ref, x_ref, y_ref, xy_ref):
    x_part, y_part, corner = get_sides(s, (from_x_ref, from_y_ref, from_xy_ref), x_ref, y_ref, xy_ref)
    stack = stacked(from_columns(s, [corner, x_part, y_part, own_ref[...]]))
    for x in range(s.bx):
        image = jnp.dot(by_node_ref[x], stack, preferred_element_type=F32)
        field_ref[x, 0 : s.by] = image.reshape(s.by, s.bzp, s.waves) + block_ref[x]
    add_sides(s, field_ref, x_ref, y_ref, xy_ref)


def sums_body(s, field_ref, by_atom_ref, total_ref):
    total = jnp.zeros((s.locals, s.waves), F32)
    for x in range(s.bx):
        total = total + split_sums(by_atom_ref[x], s.locals, field_ref[x, 0 : s.by].reshape(s.by * s.bzp, s.waves))
    total_ref[...] = total


def second_down_body(s, before_ref, total_ref, lowest_ref, *refs):
    del before_ref
    count = 2 - s.pairs
    received, refs = refs[:count], refs[count:]
    field_ref, *msg_refs, part_ref, above_ref, below_ref, x_ref, y_ref, xy_ref = refs
    get_z(s, received, above_ref, below_ref)
    for x in range(s.bx):
        field_ref[x, 0 : s.by, s.bz, :] += above_ref[x * s.by : (x + 1) * s.by]
        field_ref[x, 0 : s.by, 0, :] += below_ref[x * s.by : (x + 1) * s.by]
    total = total_ref[...] + split_sums(lowest_ref[...], s.locals, below_ref[...])
    send_down(s, total, field_ref, msg_refs, part_ref, x_ref, y_ref, xy_ref)


def fold_body(s, before_ref, from_x_ref, from_y_ref, from_xy_ref, own_ref, *refs):
    del before_ref
    block_ref, *msg_refs, total_ref, x_ref, y_ref, xy_ref, low_ref, high_ref = refs
    x_part, y_part, corner = get_sides(s, (from_x_ref, from_y_ref, from_xy_ref), x_ref, y_ref, xy_ref)
    total = from_columns(s, [corner, x_part, y_part, own_ref[...]])
    total_ref[...] = total
    add_sides(s, block_ref, x_ref, y_ref, xy_ref)
    half = 4 * s.own
    for x in range(s.bx):
        high_ref[x * s.by : (x + 1) * s.by] = block_ref[x, :, s.bz, :]
    blank(high_ref, s.z_rows)
    blank(low_ref, 0)
    put_split(low_ref, 0, total[0:half])
    put_split(high_ref, s.z_rows, total[half:])
    put_z(s, msg_refs, low_ref, high_ref)


def last_body(s, start_ref, block_ref, total_ref, by_node_ref, *refs):
    count = 2 - s.pairs
    received, refs = refs[:count], refs[count:]
    out_hbm, above_ref, below_ref, plane_ref, out_ref, sems = refs
    get_z(s, received, above_ref, below_ref)
    half = 4 * s.own
    total = total_ref[...] + jnp.concatenate([get_split(below_ref, s.z_rows, half), get_split(above_ref, 0, half)], axis=0)
    stack = stacked(total)
    copies = []
    for x in range(s.bx):
        image = jnp.dot(by_node_ref[x], stack, preferred_element_type=F32)
        plane_ref[x] = image.reshape(s.by, s.bzp, s.waves) + block_ref[x]
        plane_ref[x, :, 0, :] += below_ref[x * s.by : (x + 1) * s.by]
        out_ref[x] = 2.0 * plane_ref[x, :, 0 : s.bz] - start_ref[x]
        if (x + 1) % s.few_out == 0:
            span = pl.ds(x + 1 - s.few_out, s.few_out)
            copies.append(pltpu.make_async_copy(out_ref.at[span], out_hbm.at[span], sems.at[x // s.few_out]))
            copies[-1].start()
    for copy in copies:
        copy.wait()


def selector(count, chosen):
    row = lax.broadcasted_iota(jnp.int32, count, 0)
    column = lax.broadcasted_iota(jnp.int32, count, 1)
    return chosen(row, column).astype(F32).astype(BF16)


def matrix_body(s, part, matrix_hbm, out_ref, raw_ref, flat_ref, half_ref, sems):
    cells_y, cells_z = s.cells[1:]
    side, group = s.side, s.group
    nodes = side**3
    copies = [pltpu.make_async_copy(matrix_hbm.at[part, j], raw_ref.at[j], sems.at[j]) for j in range(cells_y)]
    for copy in copies:
        copy.start()
    wide = 256 // group * side
    spans = []
    for first in range(0, s.padded, 256):
        low = first // group * side // 128 * 128
        high = min(nodes, first // group * side + wide)
        width = min(256, s.padded - first)
        spans.append((first, low, high, selector((high - low, width), lambda m, c, low=low, first=first: (
            ((c + first) % group < side) & (m + low == (c + first) // group * side + (c + first) % group)))))
    tall = 128 // group * side
    picks = jnp.concatenate(
        [
            selector((128, tall * cells_z), lambda r, m, k=k: (r % group < side) & (m == (r // group * side + r % group) * cells_z + k))
            for k in range(cells_z)
        ],
        axis=0,
    )
    for j in range(cells_y):
        copies[j].wait()
        flat_ref[...] = raw_ref[j].reshape(nodes * cells_z, nodes)
        for first, low, high, spread in spans:
            half = jnp.dot(flat_ref[:, low:high], spread, preferred_element_type=F32)
            half_ref[:, first : first + spread.shape[1]] = half.astype(BF16)
        for first in range(0, s.padded, 128):
            count = min(128, s.padded - first)
            low = first // group * side * cells_z
            high = min(nodes * cells_z, low + tall * cells_z)
            rows = jnp.dot(picks[:, 0 : high - low], half_ref[low:high], preferred_element_type=F32).astype(BF16)
            for k in range(cells_z):
                out_ref[j, k, first : first + count] = rows[128 * k : 128 * k + count]


def regrouped(s, cell_matrices, part):
    shape = cell_matrices.shape
    nodes = shape[3]
    return call(
        matrix_body,
        s,
        [jax.ShapeDtypeStruct(shape[1:3] + (s.padded, s.padded), BF16)],
        [
            pltpu.VMEM((shape[1], nodes, shape[2], nodes), BF16),
            pltpu.VMEM((nodes * shape[2], nodes), BF16),
            pltpu.VMEM((nodes * shape[2], s.padded), BF16),
            pltpu.SemaphoreType.DMA((shape[1],)),
        ],
        [cell_matrices.transpose(0, 1, 3, 2, 4)],
        spaces={0: pltpu.HBM},
        extra=(part,),
    )[0]


def along_z(s, msgs):
    if s.pairs:
        return [shifted(msgs[0], (0, 0, 1))]
    return [shifted(msgs[0], (0, 0, -1)), shifted(msgs[1], (0, 0, 1))]


def along_xy(msgs, by):
    return [shifted(msg, (by * dx, by * dy, 0)) for msg, dx, dy in zip(msgs, (1, 0, 1), (0, 1, 1))]


def local(wavefunctions, cell_matrices, projectors, slot_atoms, atom_coupling):
    atom_count = atom_coupling.shape[0]
    devices = 1
    for axis in AXES:
        devices *= lax.axis_size(axis)
    own = atom_count // devices
    s = Sizes(wavefunctions.shape, cell_matrices.shape, own, lax.axis_size("gz") == 2)
    plane = s.by * s.bzp
    sides = s.side_rows()
    field, by_atom, wide, *msgs, total, weight = call(
        first_body,
        s,
        [
            s.extended(),
            jax.ShapeDtypeStruct((s.bx, 2 * s.locals, plane), BF16),
            jax.ShapeDtypeStruct((s.z_rows, s.bzp, 2 * s.locals), F32),
        ]
        + s.z_msgs(s.z_both, s.z_sums)
        + [s.rows(s.locals), s.rows(s.locals)],
        [
            s.scratch(s.bx, s.by, s.bz),
            pltpu.VMEM(projectors.shape, F32),
            pltpu.VMEM(slot_atoms.shape, jnp.int32),
            pltpu.VMEM((1, atom_count), F32),
            pltpu.VMEM((s.bx * s.by * s.bz, 2 * s.locals), F32),
            s.scratch(s.z_both),
            s.scratch(s.z_sums),
            pltpu.SemaphoreType.DMA((1,)),
            pltpu.SemaphoreType.DMA((3,)),
        ],
        [wavefunctions, projectors, slot_atoms, atom_coupling[None, :]],
        spaces={0: pltpu.HBM, 1: pltpu.HBM, 2: pltpu.HBM, 3: pltpu.HBM},
    )
    matrices = [regrouped(s, cell_matrices, part) for part in range(s.cells[0])]
    received = along_z(s, msgs)
    field, *msgs, part = call(
        first_down_body,
        s,
        [s.extended()] + s.side_msgs() + [s.rows(2 * own)],
        [s.scratch(s.z_both), s.scratch(s.z_sums)] + sides,
        [field, total, matrices[0]] + received,
        aliases={0: 0},
    )

    def cells(field, msgs, part):
        received = along_xy(msgs, -1)
        _, sums, *msgs, mine = call(
            cell_body,
            s,
            [s.extended(), jax.ShapeDtypeStruct((s.cells[2], s.bx + 1, s.by + 1, s.group, s.waves), F32)]
            + s.side_msgs()
            + [s.rows(2 * own)],
            sides,
            [field] + received + [part, weight] + matrices,
            aliases={0: 0},
        )
        received = along_xy(msgs, 1)
        (block,) = call(join_cells, s, [s.block()], [], [sums])
        return block, received, mine

    block, received, mine = cells(field, msgs, part)
    by_node, lowest, lowest_by_node = call(
        node_body,
        s,
        [
            jax.ShapeDtypeStruct((s.bx, plane, 3 * s.locals), BF16),
            jax.ShapeDtypeStruct((2 * s.locals, s.z_plane), BF16),
            jax.ShapeDtypeStruct((s.z_rows, 3 * s.locals), BF16),
        ],
        [],
        [wide],
    )
    msgs = call(
        swap_body,
        s,
        s.z_msgs(s.z_plane, s.z_plane),
        sides + [s.scratch(s.z_plane), s.scratch(s.z_plane)],
        [block] + received + [mine, lowest_by_node],
    )
    swapped = along_z(s, msgs)
    (field,) = call(middle_body, s, [s.extended()], sides, [block] + received + [mine, by_node])
    received = swapped
    (total,) = call(sums_body, s, [s.rows(s.locals)], [], [field, by_atom])
    field, *msgs, part = call(
        second_down_body,
        s,
        [s.extended()] + s.side_msgs() + [s.rows(2 * own)],
        [s.scratch(s.z_plane), s.scratch(s.z_plane)] + sides,
        [field, total, lowest] + received,
        aliases={0: 0},
    )
    block, received, mine = cells(field, msgs, part)
    block, *msgs, total = call(
        fold_body,
        s,
        [s.block()] + s.z_msgs(s.z_sums, s.z_both) + [s.rows(s.locals)],
        sides + [s.scratch(s.z_sums), s.scratch(s.z_both)],
        [block] + received + [mine],
        aliases={0: 0},
    )
    received = along_z(s, msgs)
    (out,) = call(
        last_body,
        s,
        [jax.ShapeDtypeStruct(wavefunctions.shape, F32)],
        [
            s.scratch(s.z_sums),
            s.scratch(s.z_both),
            s.scratch(s.bx, s.by, s.bzp),
            s.scratch(s.bx, s.by, s.bz),
            pltpu.SemaphoreType.DMA((s.bx // s.few_out,)),
        ],
        [wavefunctions, block, total, by_node] + received,
        out_spaces={0: pltpu.HBM},
    )
    return out


def solution(mesh):
    return jax.shard_map(
        local,
        mesh=mesh,
        in_specs=(
            P("gx", "gy", "gz", None),
            P("gx", "gy", "gz", None, None),
            P(("gx", "gy", "gz"), None, None),
            P(("gx", "gy", "gz"), None),
            P(),
        ),
        out_specs=P("gx", "gy", "gz", None),
        check_vma=False,
    )
```

```python
import functools

import jax
import jax.numpy as jnp
from jax import lax
from jax.experimental import pallas as pl
from jax.experimental.pallas import tpu as pltpu
from jax.sharding import PartitionSpec as P

AXES = ("gx", "gy", "gz")
F32 = jnp.float32
BF16 = jnp.bfloat16
LIMIT = 12 * 1024 * 1024


def up_to(value, unit):
    return -(-value // unit) * unit


def shifted(value, shift):
    sizes = [lax.axis_size(axis) for axis in AXES]
    pairs = []
    for x in range(sizes[0]):
        for y in range(sizes[1]):
            for z in range(sizes[2]):
                here = (x * sizes[1] + y) * sizes[2] + z
                there = [(p + s) % n for p, s, n in zip((x, y, z), shift, sizes)]
                pairs.append((here, (there[0] * sizes[1] + there[1]) * sizes[2] + there[2]))
    return lax.ppermute(value, AXES, pairs)


def halves(value):
    high = value.astype(BF16).astype(F32)
    return high, value - high


def put_split(rows_ref, start, value):
    count = value.shape[0]
    high, low = halves(value)
    rows_ref[start : start + count] = high
    rows_ref[start + count : start + 2 * count] = low


def get_split(rows_ref, start, count):
    return rows_ref[start : start + count] + rows_ref[start + count : start + 2 * count]


class Sizes:
    def __init__(self, field_shape, cell_shape, own, pairs):
        self.bx, self.by, self.bz, self.waves = field_shape
        self.cells = cell_shape[:3]
        self.order = self.bx // cell_shape[0]
        self.side = self.order + 1
        self.group = up_to(self.side, 8)
        self.padded = up_to(self.side * self.side * self.group, 16)
        self.bzp = up_to(max(self.bz + 1, (cell_shape[2] - 1) * self.order + self.group), 16)
        self.few_out = max(n for n in (1, 2) if self.bx % n == 0)
        self.pairs = pairs
        self.own = own
        self.locals = 8 * own
        self.span = self.bz + 1
        self.z_rows = self.bx * self.by
        self.x_rows = self.by * self.span
        self.y_rows = self.bx * self.span
        self.x_msg = up_to(self.x_rows + 4 * own, 8)
        self.y_msg = up_to(self.y_rows + 4 * own, 8)
        self.xy_msg = up_to(self.span + 4 * own, 8)
        self.z_plane = up_to(self.z_rows, 16)
        self.z_sums = up_to(8 * own, 16)
        self.z_both = up_to(self.z_rows + 8 * own, 16)

    def extended(self):
        return jax.ShapeDtypeStruct((self.bx + 1, self.by + 1, self.bzp, self.waves), F32)

    def block(self):
        return jax.ShapeDtypeStruct((self.bx, self.by, self.bzp, self.waves), F32)

    def rows(self, count, dtype=F32):
        return jax.ShapeDtypeStruct((count, self.waves), dtype)

    def scratch(self, *shape):
        return pltpu.VMEM(shape + (self.waves,), F32)

    def z_msgs(self, down, up):
        return [self.rows(down + up, BF16)] if self.pairs else [self.rows(down, BF16), self.rows(up, BF16)]

    def side_msgs(self):
        return [self.rows(n, BF16) for n in (self.x_msg, self.y_msg, self.xy_msg)]

    def side_rows(self):
        return [self.scratch(n) for n in (self.x_msg, self.y_msg, self.xy_msg)]


VMEM = pltpu.VMEM


def call(body, sizes, outs, scratch, args, spaces=None, out_spaces=None, aliases=None, extra=()):
    spaces = spaces or {}
    out_spaces = out_spaces or {}
    outs = [out_spaces.get(n, VMEM)(out.shape, out.dtype) for n, out in enumerate(outs)]
    args = [pltpu.with_memory_space_constraint(arg, spaces.get(n, VMEM)) for n, arg in enumerate(args)]
    return pl.pallas_call(
        functools.partial(body, sizes, *extra),
        out_shape=outs,
        in_specs=[pl.BlockSpec(memory_space=spaces.get(n, VMEM)) for n in range(len(args))],
        out_specs=[pl.BlockSpec(memory_space=out_spaces.get(n, VMEM)) for n in range(len(outs))],
        scratch_shapes=scratch,
        input_output_aliases=aliases or {},
        compiler_params=pltpu.CompilerParams(vmem_limit_bytes=LIMIT),
    )(*args)


def local_atoms(own, shape):
    sizes = [lax.axis_size(axis) for axis in AXES]
    here = [lax.axis_index(axis) for axis in AXES]
    ids = []
    for dz in (1, 0):
        for dx in (1, 0):
            for dy in (1, 0):
                x, y, z = (lax.rem(h + n - d, n) for h, n, d in zip(here, sizes, (dx, dy, dz)))
                owner = (x * sizes[1] + y) * sizes[2] + z
                ids += [owner * own + a for a in range(own)]
    row = lax.broadcasted_iota(jnp.int32, shape, 0)
    table = jnp.zeros(shape, jnp.int32)
    for n, atom in enumerate(ids):
        table = jnp.where(row == n, atom, table)
    return table


def blank(rows_ref, first):
    count = rows_ref.shape[0] - first
    if count:
        rows_ref[first:] = jnp.zeros((count,) + rows_ref.shape[1:], F32)


def split_sums(by_atom, count, field):
    high = field.astype(BF16)
    low = (field - high.astype(F32)).astype(BF16)
    with_high = jnp.dot(by_atom, high, preferred_element_type=F32)
    with_low = jnp.dot(by_atom[0:count], low, preferred_element_type=F32)
    return with_high[0:count] + with_high[count : 2 * count] + with_low


def put_z(s, msg_refs, down_ref, up_ref):
    if s.pairs:
        count = down_ref.shape[0]
        msg_refs[0][0:count] = down_ref[...].astype(BF16)
        msg_refs[0][count:] = up_ref[...].astype(BF16)
    else:
        msg_refs[0][...] = down_ref[...].astype(BF16)
        msg_refs[1][...] = up_ref[...].astype(BF16)


def get_z(s, msg_refs, above_ref, below_ref):
    if s.pairs:
        count = above_ref.shape[0]
        above_ref[...] = msg_refs[0][0:count].astype(F32)
        below_ref[...] = msg_refs[0][count:].astype(F32)
    else:
        above_ref[...] = msg_refs[0][...].astype(F32)
        below_ref[...] = msg_refs[1][...].astype(F32)


def columns(s, totals):
    own, half = s.own, 4 * s.own
    return [
        jnp.concatenate([totals[n * own : (n + 1) * own], totals[half + n * own : half + (n + 1) * own]], axis=0) for n in range(4)
    ]


def from_columns(s, parts):
    own = s.own
    return jnp.concatenate([part[0:own] for part in parts] + [part[own : 2 * own] for part in parts], axis=0)


def first_body(
    s, start_hbm, rows_hbm, slots_hbm, coupling_hbm,
    field_ref, by_atom_ref, wide_ref, *refs
):
    *msg_refs, total_ref, weight_ref, start_ref, rows_ref, slots_ref, coupling_ref, tall_ref, low_ref, high_ref, sems, small_sems = refs
    small = [
        pltpu.make_async_copy(rows_hbm, rows_ref, small_sems.at[0]),
        pltpu.make_async_copy(slots_hbm, slots_ref, small_sems.at[1]),
        pltpu.make_async_copy(coupling_hbm, coupling_ref, small_sems.at[2]),
    ]
    for copy in small:
        copy.start()
    whole = pltpu.make_async_copy(start_hbm, start_ref, sems.at[0])
    whole.start()
    for copy in small:
        copy.wait()
    slots = slots_ref[...]
    chosen = (local_atoms(s.own, (s.locals, slots.shape[1])) == slots).astype(F32).astype(BF16)
    rows = rows_ref[0]
    high = rows.astype(BF16)
    low = (rows - high.astype(F32)).astype(BF16)
    parts = [jnp.dot(chosen, part, preferred_element_type=F32) for part in (high, low)]
    tall_ref[...] = jnp.concatenate(parts, axis=0).T
    wide_ref[:, s.bz : s.bzp, :] = jnp.zeros((s.bx * s.by, s.bzp - s.bz, 2 * s.locals), F32)
    for g in range(s.bx * s.by):
        wide_ref[g, 0 : s.bz, :] = tall_ref[g * s.bz : (g + 1) * s.bz, :]
    for x in range(s.bx):
        wide = wide_ref[x * s.by : (x + 1) * s.by].reshape(s.by * s.bzp, 2 * s.locals)
        by_atom_ref[x] = wide.T.astype(BF16)
    total = jnp.zeros((s.locals, s.waves), F32)
    whole.wait()
    for x in range(s.bx):
        plane = jnp.concatenate([start_ref[x], jnp.zeros((s.by, s.bzp - s.bz, s.waves), F32)], axis=1)
        field_ref[x, 0 : s.by] = plane
        total = total + split_sums(by_atom_ref[x], s.locals, plane.reshape(s.by * s.bzp, s.waves))
    total_ref[...] = total
    half = 4 * s.own
    for x in range(s.bx):
        low_ref[x * s.by : (x + 1) * s.by] = field_ref[x, 0 : s.by, 0, :]
    blank(low_ref, s.z_rows)
    blank(high_ref, 0)
    put_split(low_ref, s.z_rows, total[0:half])
    put_split(high_ref, 0, total[half:])
    put_z(s, msg_refs, low_ref, high_ref)
    atoms = lax.broadcasted_iota(jnp.int32, (s.locals, coupling_ref.shape[1]), 1)
    weight = jnp.sum(jnp.where(atoms == local_atoms(s.own, atoms.shape), coupling_ref[...], 0.0), axis=1, keepdims=True)
    weight_ref[...] = jnp.broadcast_to(weight, weight_ref.shape)


def node_body(s, wide_ref, by_node_ref, lowest_ref, lowest_by_node_ref):
    for x in range(s.bx):
        wide = wide_ref[x * s.by : (x + 1) * s.by].reshape(s.by * s.bzp, 2 * s.locals)
        by_node_ref[x] = jnp.concatenate([wide, wide[:, 0 : s.locals]], axis=1).astype(BF16)
    line = wide_ref[:, 0, :]
    lowest_by_node_ref[...] = jnp.concatenate([line, line[:, 0 : s.locals]], axis=1).astype(BF16)
    lowest = line.T
    if s.z_plane > s.z_rows:
        lowest = jnp.concatenate([lowest, jnp.zeros((2 * s.locals, s.z_plane - s.z_rows), F32)], axis=1)
    lowest_ref[...] = lowest.astype(BF16)


def put_sides(s, field_ref, x, y, x_ref, y_ref, xy_ref):
    for n in range(s.by):
        x_ref[n * s.span : (n + 1) * s.span] = field_ref[x, n, 0 : s.span, :]
    for n in range(s.bx):
        y_ref[n * s.span : (n + 1) * s.span] = field_ref[n, y, 0 : s.span, :]
    xy_ref[0 : s.span] = field_ref[x, y, 0 : s.span, :]
    for ref, used in ((x_ref, s.x_rows), (y_ref, s.y_rows), (xy_ref, s.span)):
        blank(ref, used)


def send_sides(s, x_ref, y_ref, xy_ref, msg_refs, parts):
    for ref, used, part, msg_ref in zip((x_ref, y_ref, xy_ref), (s.x_rows, s.y_rows, s.span), parts, msg_refs):
        put_split(ref, used, part)
        msg_ref[...] = ref[...].astype(BF16)


def get_sides(s, received, x_ref, y_ref, xy_ref):
    parts = []
    for ref, used, msg_ref in zip((x_ref, y_ref, xy_ref), (s.x_rows, s.y_rows, s.span), received):
        ref[...] = msg_ref[...].astype(F32)
        parts.append(get_split(ref, used, 2 * s.own))
    return parts


def add_sides(s, field_ref, x_ref, y_ref, xy_ref):
    for n in range(s.by):
        field_ref[0, n, 0 : s.span, :] += x_ref[n * s.span : (n + 1) * s.span]
    for n in range(s.bx):
        field_ref[n, 0, 0 : s.span, :] += y_ref[n * s.span : (n + 1) * s.span]
    field_ref[0, 0, 0 : s.span, :] += xy_ref[0 : s.span]


def add_ends(s, x_ref, y_ref, xy_ref, z, plane_ref):
    for n in range(s.by):
        at = n * s.span + z
        x_ref[at : at + 1] += plane_ref[n : n + 1]
    for n in range(s.bx):
        at = n * s.span + z
        y_ref[at : at + 1] += plane_ref[n * s.by : n * s.by + 1]
    xy_ref[z : z + 1] += plane_ref[0:1]


def send_down(s, total, msg_refs, part_ref, x_ref, y_ref, xy_ref):
    corner, x_part, y_part, own_part = columns(s, total)
    part_ref[...] = own_part
    send_sides(s, x_ref, y_ref, xy_ref, msg_refs, (x_part, y_part, corner))


def first_down_body(s, field_ref, total_ref, early_ref, *refs):
    del early_ref
    count = 2 - s.pairs
    received, refs = refs[:count], refs[count:]
    *msg_refs, part_ref, above_ref, below_ref, x_ref, y_ref, xy_ref = refs
    get_z(s, received, above_ref, below_ref)
    half = 4 * s.own
    total = total_ref[...] + jnp.concatenate([get_split(below_ref, 0, half), get_split(above_ref, s.z_rows, half)], axis=0)
    put_sides(s, field_ref, 0, 0, x_ref, y_ref, xy_ref)
    add_ends(s, x_ref, y_ref, xy_ref, s.bz, above_ref)
    send_down(s, total, msg_refs, part_ref, x_ref, y_ref, xy_ref)


def first_fill_body(s, before_ref, sent_ref, *refs):
    del before_ref, sent_ref
    count = 2 - s.pairs
    received, (field_ref, above_ref, below_ref) = refs[:count], refs[count:]
    get_z(s, received, above_ref, below_ref)
    for x in range(s.bx):
        field_ref[x, 0 : s.by, s.bz, :] = above_ref[x * s.by : (x + 1) * s.by]


def cell_body(s, before_ref, from_x_ref, from_y_ref, from_xy_ref, part_ref, weight_ref, *refs):
    matrix_refs, refs = refs[: s.cells[0]], refs[s.cells[0] :]
    field_ref, sums_ref, *msg_refs, own_ref, x_ref, y_ref, xy_ref = refs
    del before_ref
    parts = get_sides(s, (from_x_ref, from_y_ref, from_xy_ref), x_ref, y_ref, xy_ref)
    rest = jnp.zeros((s.bzp - s.span, s.waves), F32)
    for n in range(s.by):
        field_ref[s.bx, n, 0 : s.span, :] = x_ref[n * s.span : (n + 1) * s.span]
        field_ref[s.bx, n, s.span :, :] = rest
    for n in range(s.bx):
        field_ref[n, s.by, 0 : s.span, :] = y_ref[n * s.span : (n + 1) * s.span]
        field_ref[n, s.by, s.span :, :] = rest
    field_ref[s.bx, s.by, 0 : s.span, :] = xy_ref[0 : s.span]
    field_ref[s.bx, s.by, s.span :, :] = rest
    weight = columns(s, weight_ref[...])[3]
    total = (part_ref[...] + parts[0] + parts[1] + parts[2]) * weight
    own_ref[...] = total
    apply_cells(s, field_ref, matrix_refs, sums_ref)
    join_sides(s, sums_ref, x_ref, y_ref, xy_ref)
    send_sides(s, x_ref, y_ref, xy_ref, msg_refs, (total, total, total))


def apply_cells(s, field_ref, matrix_refs, sums_ref):
    order, side, group = s.order, s.side, s.group
    used = side * side * group
    for i in range(s.cells[0]):
        for j in range(s.cells[1]):
            for k in range(s.cells[2]):
                first = k * order
                values = field_ref[i * order : i * order + side, j * order : j * order + side, first : first + group]
                values = values.reshape(used, s.waves)
                if s.padded > used:
                    values = jnp.concatenate([values, jnp.zeros((s.padded - used, s.waves), F32)], axis=0)
                product = jnp.dot(matrix_refs[i][j, k], values.astype(BF16), preferred_element_type=F32)
                product = product[0:used].reshape(side, side, group, s.waves)
                x0, x1, y0, y1 = i * order, i * order + side, j * order, j * order + side
                a, b = int(i > 0), int(j > 0)
                sums_ref[k, x0 + a : x1, y0 + b : y1] = product[a:, b:]
                if a:
                    sums_ref[k, x0, y0 + b : y1] += product[0, b:]
                if b:
                    sums_ref[k, x0 + a : x1, y0] += product[a:, 0]
                if a and b:
                    sums_ref[k, x0, y0] += product[0, 0]


def join_cells(s, sums_ref, out_ref):
    count = s.by
    for x in range(s.bx):
        out_ref[x, :, 0 : s.group, :] = sums_ref[0, x, 0:count]
        out_ref[x, :, s.group :, :] = jnp.zeros((count, s.bzp - s.group, s.waves), F32)
        for k in range(1, s.cells[2]):
            out_ref[x, :, k * s.order : k * s.order + s.group, :] += sums_ref[k, x, 0:count]


def join_sides(s, sums_ref, x_ref, y_ref, xy_ref):
    last = s.cells[2] - 1

    def join(rows_ref, at, x, y):
        for k in range(s.cells[2]):
            count = s.order + int(k == last)
            first = at + k * s.order
            rows_ref[first : first + count] = sums_ref[k, x, y, 0:count, :]
            if k:
                rows_ref[first : first + 1] += sums_ref[k - 1, x, y, s.order : s.order + 1, :]

    for n in range(s.by):
        join(x_ref, n * s.span, s.bx, n)
    for n in range(s.bx):
        join(y_ref, n * s.span, n, s.by)
    join(xy_ref, 0, s.bx, s.by)
    for ref, used in ((x_ref, s.x_rows), (y_ref, s.y_rows), (xy_ref, s.span)):
        blank(ref, used)


def stacked(totals):
    high, low = halves(totals)
    return jnp.concatenate([high, high, low], axis=0).astype(BF16)


def swap_body(s, block_ref, from_x_ref, from_y_ref, from_xy_ref, own_ref, lowest_by_node_ref, *refs):
    *msg_refs, x_ref, y_ref, xy_ref, low_ref, high_ref = refs
    x_part, y_part, corner = get_sides(s, (from_x_ref, from_y_ref, from_xy_ref), x_ref, y_ref, xy_ref)
    stack = stacked(from_columns(s, [corner, x_part, y_part, own_ref[...]]))
    low_ref[0 : s.z_rows] = jnp.dot(lowest_by_node_ref[...], stack, preferred_element_type=F32)
    for x in range(s.bx):
        low_ref[x * s.by : (x + 1) * s.by] += block_ref[x, :, 0, :]
        high_ref[x * s.by : (x + 1) * s.by] = block_ref[x, :, s.bz, :]
    for ref, z in ((low_ref, 0), (high_ref, s.bz)):
        for n in range(s.by):
            ref[n : n + 1] += x_ref[n * s.span + z : n * s.span + z + 1]
        for n in range(s.bx):
            ref[n * s.by : n * s.by + 1] += y_ref[n * s.span + z : n * s.span + z + 1]
        ref[0:1] += xy_ref[z : z + 1]
        blank(ref, s.z_rows)
    put_z(s, msg_refs, low_ref, high_ref)


def middle_body(s, block_ref, from_x_ref, from_y_ref, from_xy_ref, own_ref, by_node_ref, field_ref, x_ref, y_ref, xy_ref):
    x_part, y_part, corner = get_sides(s, (from_x_ref, from_y_ref, from_xy_ref), x_ref, y_ref, xy_ref)
    stack = stacked(from_columns(s, [corner, x_part, y_part, own_ref[...]]))
    for x in range(s.bx):
        image = jnp.dot(by_node_ref[x], stack, preferred_element_type=F32)
        field_ref[x, 0 : s.by] = image.reshape(s.by, s.bzp, s.waves) + block_ref[x]
    add_sides(s, field_ref, x_ref, y_ref, xy_ref)


def sums_body(s, field_ref, by_atom_ref, total_ref):
    total = jnp.zeros((s.locals, s.waves), F32)
    for x in range(s.bx):
        total = total + split_sums(by_atom_ref[x], s.locals, field_ref[x, 0 : s.by].reshape(s.by * s.bzp, s.waves))
    total_ref[...] = total


def second_down_body(s, field_ref, total_ref, lowest_ref, *refs):
    count = 2 - s.pairs
    received, refs = refs[:count], refs[count:]
    *msg_refs, part_ref, above_ref, below_ref, x_ref, y_ref, xy_ref = refs
    get_z(s, received, above_ref, below_ref)
    total = total_ref[...] + split_sums(lowest_ref[...], s.locals, below_ref[...])
    put_sides(s, field_ref, 0, 0, x_ref, y_ref, xy_ref)
    add_ends(s, x_ref, y_ref, xy_ref, s.bz, above_ref)
    add_ends(s, x_ref, y_ref, xy_ref, 0, below_ref)
    send_down(s, total, msg_refs, part_ref, x_ref, y_ref, xy_ref)


def second_fill_body(s, before_ref, sent_ref, *refs):
    del before_ref, sent_ref
    count = 2 - s.pairs
    received, (field_ref, above_ref, below_ref) = refs[:count], refs[count:]
    get_z(s, received, above_ref, below_ref)
    for x in range(s.bx):
        field_ref[x, 0 : s.by, s.bz, :] += above_ref[x * s.by : (x + 1) * s.by]
        field_ref[x, 0 : s.by, 0, :] += below_ref[x * s.by : (x + 1) * s.by]


def fold_body(s, before_ref, from_x_ref, from_y_ref, from_xy_ref, own_ref, *refs):
    del before_ref
    block_ref, *msg_refs, total_ref, x_ref, y_ref, xy_ref, low_ref, high_ref = refs
    x_part, y_part, corner = get_sides(s, (from_x_ref, from_y_ref, from_xy_ref), x_ref, y_ref, xy_ref)
    total = from_columns(s, [corner, x_part, y_part, own_ref[...]])
    total_ref[...] = total
    add_sides(s, block_ref, x_ref, y_ref, xy_ref)
    half = 4 * s.own
    for x in range(s.bx):
        high_ref[x * s.by : (x + 1) * s.by] = block_ref[x, :, s.bz, :]
    blank(high_ref, s.z_rows)
    blank(low_ref, 0)
    put_split(low_ref, 0, total[0:half])
    put_split(high_ref, s.z_rows, total[half:])
    put_z(s, msg_refs, low_ref, high_ref)


def last_body(s, start_ref, block_ref, total_ref, by_node_ref, *refs):
    count = 2 - s.pairs
    received, refs = refs[:count], refs[count:]
    out_hbm, above_ref, below_ref, plane_ref, out_ref, sems = refs
    get_z(s, received, above_ref, below_ref)
    half = 4 * s.own
    total = total_ref[...] + jnp.concatenate([get_split(below_ref, s.z_rows, half), get_split(above_ref, 0, half)], axis=0)
    stack = stacked(total)
    copies = []
    for x in range(s.bx):
        image = jnp.dot(by_node_ref[x], stack, preferred_element_type=F32)
        plane_ref[x] = image.reshape(s.by, s.bzp, s.waves) + block_ref[x]
        plane_ref[x, :, 0, :] += below_ref[x * s.by : (x + 1) * s.by]
        out_ref[x] = 2.0 * plane_ref[x, :, 0 : s.bz] - start_ref[x]
        if (x + 1) % s.few_out == 0:
            span = pl.ds(x + 1 - s.few_out, s.few_out)
            copies.append(pltpu.make_async_copy(out_ref.at[span], out_hbm.at[span], sems.at[x // s.few_out]))
            copies[-1].start()
    for copy in copies:
        copy.wait()


def selector(count, chosen):
    row = lax.broadcasted_iota(jnp.int32, count, 0)
    column = lax.broadcasted_iota(jnp.int32, count, 1)
    return chosen(row, column).astype(F32).astype(BF16)


def matrix_body(s, part, matrix_hbm, out_ref, raw_ref, flat_ref, half_ref, sems):
    cells_y, cells_z = s.cells[1:]
    side, group = s.side, s.group
    nodes = side**3
    copies = [pltpu.make_async_copy(matrix_hbm.at[part, j], raw_ref.at[j], sems.at[j]) for j in range(cells_y)]
    for copy in copies:
        copy.start()
    wide = 256 // group * side
    spans = []
    for first in range(0, s.padded, 256):
        low = first // group * side // 128 * 128
        high = min(nodes, first // group * side + wide)
        width = min(256, s.padded - first)
        spans.append((first, low, high, selector((high - low, width), lambda m, c, low=low, first=first: (
            ((c + first) % group < side) & (m + low == (c + first) // group * side + (c + first) % group)))))
    tall = 128 // group * side
    picks = jnp.concatenate(
        [
            selector((128, tall * cells_z), lambda r, m, k=k: (r % group < side) & (m == (r // group * side + r % group) * cells_z + k))
            for k in range(cells_z)
        ],
        axis=0,
    )
    for j in range(cells_y):
        copies[j].wait()
        flat_ref[...] = raw_ref[j].reshape(nodes * cells_z, nodes)
        for first, low, high, spread in spans:
            half = jnp.dot(flat_ref[:, low:high], spread, preferred_element_type=F32)
            half_ref[:, first : first + spread.shape[1]] = half.astype(BF16)
        for first in range(0, s.padded, 128):
            count = min(128, s.padded - first)
            low = first // group * side * cells_z
            high = min(nodes * cells_z, low + tall * cells_z)
            rows = jnp.dot(picks[:, 0 : high - low], half_ref[low:high], preferred_element_type=F32).astype(BF16)
            for k in range(cells_z):
                out_ref[j, k, first : first + count] = rows[128 * k : 128 * k + count]


def regrouped(s, cell_matrices, part):
    shape = cell_matrices.shape
    nodes = shape[3]
    return call(
        matrix_body,
        s,
        [jax.ShapeDtypeStruct(shape[1:3] + (s.padded, s.padded), BF16)],
        [
            pltpu.VMEM((shape[1], nodes, shape[2], nodes), BF16),
            pltpu.VMEM((nodes * shape[2], nodes), BF16),
            pltpu.VMEM((nodes * shape[2], s.padded), BF16),
            pltpu.SemaphoreType.DMA((shape[1],)),
        ],
        [cell_matrices.transpose(0, 1, 3, 2, 4)],
        spaces={0: pltpu.HBM},
        extra=(part,),
    )[0]


def along_z(s, msgs):
    if s.pairs:
        return [shifted(msgs[0], (0, 0, 1))]
    return [shifted(msgs[0], (0, 0, -1)), shifted(msgs[1], (0, 0, 1))]


def along_xy(msgs, by):
    return [shifted(msg, (by * dx, by * dy, 0)) for msg, dx, dy in zip(msgs, (1, 0, 1), (0, 1, 1))]


def local(wavefunctions, cell_matrices, projectors, slot_atoms, atom_coupling):
    atom_count = atom_coupling.shape[0]
    devices = 1
    for axis in AXES:
        devices *= lax.axis_size(axis)
    own = atom_count // devices
    s = Sizes(wavefunctions.shape, cell_matrices.shape, own, lax.axis_size("gz") == 2)
    plane = s.by * s.bzp
    sides = s.side_rows()
    field, by_atom, wide, *msgs, total, weight = call(
        first_body,
        s,
        [
            s.extended(),
            jax.ShapeDtypeStruct((s.bx, 2 * s.locals, plane), BF16),
            jax.ShapeDtypeStruct((s.z_rows, s.bzp, 2 * s.locals), F32),
        ]
        + s.z_msgs(s.z_both, s.z_sums)
        + [s.rows(s.locals), s.rows(s.locals)],
        [
            s.scratch(s.bx, s.by, s.bz),
            pltpu.VMEM(projectors.shape, F32),
            pltpu.VMEM(slot_atoms.shape, jnp.int32),
            pltpu.VMEM((1, atom_count), F32),
            pltpu.VMEM((s.bx * s.by * s.bz, 2 * s.locals), F32),
            s.scratch(s.z_both),
            s.scratch(s.z_sums),
            pltpu.SemaphoreType.DMA((1,)),
            pltpu.SemaphoreType.DMA((3,)),
        ],
        [wavefunctions, projectors, slot_atoms, atom_coupling[None, :]],
        spaces={0: pltpu.HBM, 1: pltpu.HBM, 2: pltpu.HBM, 3: pltpu.HBM},
    )
    matrices = [regrouped(s, cell_matrices, part) for part in range(s.cells[0])]
    received = along_z(s, msgs)
    *msgs, part = call(
        first_down_body,
        s,
        s.side_msgs() + [s.rows(2 * own)],
        [s.scratch(s.z_both), s.scratch(s.z_sums)] + sides,
        [field, total, matrices[0]] + received,
    )
    fills = (first_fill_body, [s.scratch(s.z_both), s.scratch(s.z_sums)], received)

    def cells(field, msgs, part, fills):
        body, scratch, along = fills
        received = along_xy(msgs, -1)
        (field,) = call(body, s, [s.extended()], scratch, [field, part] + along, aliases={0: 0})
        _, sums, *msgs, mine = call(
            cell_body,
            s,
            [s.extended(), jax.ShapeDtypeStruct((s.cells[2], s.bx + 1, s.by + 1, s.group, s.waves), F32)]
            + s.side_msgs()
            + [s.rows(2 * own)],
            sides,
            [field] + received + [part, weight] + matrices,
            aliases={0: 0},
        )
        received = along_xy(msgs, 1)
        (block,) = call(join_cells, s, [s.block()], [], [sums])
        return block, received, mine

    block, received, mine = cells(field, msgs, part, fills)
    by_node, lowest, lowest_by_node = call(
        node_body,
        s,
        [
            jax.ShapeDtypeStruct((s.bx, plane, 3 * s.locals), BF16),
            jax.ShapeDtypeStruct((2 * s.locals, s.z_plane), BF16),
            jax.ShapeDtypeStruct((s.z_rows, 3 * s.locals), BF16),
        ],
        [],
        [wide],
    )
    msgs = call(
        swap_body,
        s,
        s.z_msgs(s.z_plane, s.z_plane),
        sides + [s.scratch(s.z_plane), s.scratch(s.z_plane)],
        [block] + received + [mine, lowest_by_node],
    )
    swapped = along_z(s, msgs)
    (field,) = call(middle_body, s, [s.extended()], sides, [block] + received + [mine, by_node])
    received = swapped
    (total,) = call(sums_body, s, [s.rows(s.locals)], [], [field, by_atom])
    *msgs, part = call(
        second_down_body,
        s,
        s.side_msgs() + [s.rows(2 * own)],
        [s.scratch(s.z_plane), s.scratch(s.z_plane)] + sides,
        [field, total, lowest] + received,
    )
    fills = (second_fill_body, [s.scratch(s.z_plane), s.scratch(s.z_plane)], received)
    block, received, mine = cells(field, msgs, part, fills)
    block, *msgs, total = call(
        fold_body,
        s,
        [s.block()] + s.z_msgs(s.z_sums, s.z_both) + [s.rows(s.locals)],
        sides + [s.scratch(s.z_sums), s.scratch(s.z_both)],
        [block] + received + [mine],
        aliases={0: 0},
    )
    received = along_z(s, msgs)
    (out,) = call(
        last_body,
        s,
        [jax.ShapeDtypeStruct(wavefunctions.shape, F32)],
        [
            s.scratch(s.z_sums),
            s.scratch(s.z_both),
            s.scratch(s.bx, s.by, s.bzp),
            s.scratch(s.bx, s.by, s.bz),
            pltpu.SemaphoreType.DMA((s.bx // s.few_out,)),
        ],
        [wavefunctions, block, total, by_node] + received,
        out_spaces={0: pltpu.HBM},
    )
    return out


def solution(mesh):
    return jax.shard_map(
        local,
        mesh=mesh,
        in_specs=(
            P("gx", "gy", "gz", None),
            P("gx", "gy", "gz", None, None),
            P(("gx", "gy", "gz"), None, None),
            P(("gx", "gy", "gz"), None),
            P(),
        ),
        out_specs=P("gx", "gy", "gz", None),
        check_vma=False,
    )
```

```python
import functools

import jax
import jax.numpy as jnp
from jax import lax
from jax.experimental import pallas as pl
from jax.experimental.pallas import tpu as pltpu
from jax.sharding import PartitionSpec as P

AXES = ("gx", "gy", "gz")
F32 = jnp.float32
BF16 = jnp.bfloat16
LIMIT = 12 * 1024 * 1024


def up_to(value, unit):
    return -(-value // unit) * unit


def shifted(value, shift):
    sizes = [lax.axis_size(axis) for axis in AXES]
    pairs = []
    for x in range(sizes[0]):
        for y in range(sizes[1]):
            for z in range(sizes[2]):
                here = (x * sizes[1] + y) * sizes[2] + z
                there = [(p + s) % n for p, s, n in zip((x, y, z), shift, sizes)]
                pairs.append((here, (there[0] * sizes[1] + there[1]) * sizes[2] + there[2]))
    return lax.ppermute(value, AXES, pairs)


def halves(value):
    high = value.astype(BF16).astype(F32)
    return high, value - high


def put_split(rows_ref, start, value):
    count = value.shape[0]
    high, low = halves(value)
    rows_ref[start : start + count] = high
    rows_ref[start + count : start + 2 * count] = low


def get_split(rows_ref, start, count):
    return rows_ref[start : start + count] + rows_ref[start + count : start + 2 * count]


class Sizes:
    def __init__(self, field_shape, cell_shape, own, pairs):
        self.bx, self.by, self.bz, self.waves = field_shape
        self.cells = cell_shape[:3]
        self.order = self.bx // cell_shape[0]
        self.side = self.order + 1
        self.group = up_to(self.side, 8)
        self.padded = up_to(self.side * self.side * self.group, 16)
        self.bzp = up_to(max(self.bz + 1, (cell_shape[2] - 1) * self.order + self.group), 16)
        self.few_out = max(n for n in (1, 2) if self.bx % n == 0)
        self.pairs = pairs
        self.own = own
        self.locals = 8 * own
        self.span = self.bz + 1
        self.z_rows = self.bx * self.by
        self.x_rows = self.by * self.span
        self.y_rows = self.bx * self.span
        self.x_msg = up_to(self.x_rows + 4 * own, 8)
        self.y_msg = up_to(self.y_rows + 4 * own, 8)
        self.xy_msg = up_to(self.span + 4 * own, 8)
        self.z_plane = up_to(self.z_rows, 16)
        self.z_sums = up_to(8 * own, 16)
        self.z_both = up_to(self.z_rows + 8 * own, 16)

    def extended(self):
        return jax.ShapeDtypeStruct((self.bx + 1, self.by + 1, self.bzp, self.waves), F32)

    def block(self):
        return jax.ShapeDtypeStruct((self.bx, self.by, self.bzp, self.waves), F32)

    def rows(self, count, dtype=F32):
        return jax.ShapeDtypeStruct((count, self.waves), dtype)

    def scratch(self, *shape):
        return pltpu.VMEM(shape + (self.waves,), F32)

    def z_msgs(self, down, up):
        return [self.rows(down + up, BF16)] if self.pairs else [self.rows(down, BF16), self.rows(up, BF16)]

    def side_msgs(self):
        return [self.rows(n, BF16) for n in (self.x_msg, self.y_msg, self.xy_msg)]

    def side_rows(self):
        return [self.scratch(n) for n in (self.x_msg, self.y_msg, self.xy_msg)]


VMEM = pltpu.VMEM


def call(body, sizes, outs, scratch, args, spaces=None, out_spaces=None, aliases=None, extra=()):
    spaces = spaces or {}
    out_spaces = out_spaces or {}
    outs = [out_spaces.get(n, VMEM)(out.shape, out.dtype) for n, out in enumerate(outs)]
    args = [pltpu.with_memory_space_constraint(arg, spaces.get(n, VMEM)) for n, arg in enumerate(args)]
    return pl.pallas_call(
        functools.partial(body, sizes, *extra),
        out_shape=outs,
        in_specs=[pl.BlockSpec(memory_space=spaces.get(n, VMEM)) for n in range(len(args))],
        out_specs=[pl.BlockSpec(memory_space=out_spaces.get(n, VMEM)) for n in range(len(outs))],
        scratch_shapes=scratch,
        input_output_aliases=aliases or {},
        compiler_params=pltpu.CompilerParams(vmem_limit_bytes=LIMIT),
    )(*args)


def local_atoms(own, shape):
    sizes = [lax.axis_size(axis) for axis in AXES]
    here = [lax.axis_index(axis) for axis in AXES]
    ids = []
    for dz in (1, 0):
        for dx in (1, 0):
            for dy in (1, 0):
                x, y, z = (lax.rem(h + n - d, n) for h, n, d in zip(here, sizes, (dx, dy, dz)))
                owner = (x * sizes[1] + y) * sizes[2] + z
                ids += [owner * own + a for a in range(own)]
    row = lax.broadcasted_iota(jnp.int32, shape, 0)
    table = jnp.zeros(shape, jnp.int32)
    for n, atom in enumerate(ids):
        table = jnp.where(row == n, atom, table)
    return table


def blank(rows_ref, first):
    count = rows_ref.shape[0] - first
    if count:
        rows_ref[first:] = jnp.zeros((count,) + rows_ref.shape[1:], F32)


def split_sums(by_atom, count, field):
    high = field.astype(BF16)
    low = (field - high.astype(F32)).astype(BF16)
    with_high = jnp.dot(by_atom, high, preferred_element_type=F32)
    with_low = jnp.dot(by_atom[0:count], low, preferred_element_type=F32)
    return with_high[0:count] + with_high[count : 2 * count] + with_low


def put_z(s, msg_refs, down_ref, up_ref):
    if s.pairs:
        count = down_ref.shape[0]
        msg_refs[0][0:count] = down_ref[...].astype(BF16)
        msg_refs[0][count:] = up_ref[...].astype(BF16)
    else:
        msg_refs[0][...] = down_ref[...].astype(BF16)
        msg_refs[1][...] = up_ref[...].astype(BF16)


def get_z(s, msg_refs, above_ref, below_ref):
    if s.pairs:
        count = above_ref.shape[0]
        above_ref[...] = msg_refs[0][0:count].astype(F32)
        below_ref[...] = msg_refs[0][count:].astype(F32)
    else:
        above_ref[...] = msg_refs[0][...].astype(F32)
        below_ref[...] = msg_refs[1][...].astype(F32)


def columns(s, totals):
    own, half = s.own, 4 * s.own
    return [
        jnp.concatenate([totals[n * own : (n + 1) * own], totals[half + n * own : half + (n + 1) * own]], axis=0) for n in range(4)
    ]


def from_columns(s, parts):
    own = s.own
    return jnp.concatenate([part[0:own] for part in parts] + [part[own : 2 * own] for part in parts], axis=0)


def first_body(
    s, start_hbm, rows_hbm, slots_hbm, coupling_hbm,
    field_ref, by_atom_ref, wide_ref, *refs
):
    *msg_refs, total_ref, weight_ref, start_ref, rows_ref, slots_ref, coupling_ref, tall_ref, low_ref, high_ref, sems, small_sems = refs
    small = [
        pltpu.make_async_copy(rows_hbm, rows_ref, small_sems.at[0]),
        pltpu.make_async_copy(slots_hbm, slots_ref, small_sems.at[1]),
        pltpu.make_async_copy(coupling_hbm, coupling_ref, small_sems.at[2]),
    ]
    for copy in small:
        copy.start()
    whole = pltpu.make_async_copy(start_hbm, start_ref, sems.at[0])
    whole.start()
    for copy in small:
        copy.wait()
    slots = slots_ref[...]
    chosen = (local_atoms(s.own, (s.locals, slots.shape[1])) == slots).astype(F32).astype(BF16)
    rows = rows_ref[0]
    high = rows.astype(BF16)
    low = (rows - high.astype(F32)).astype(BF16)
    parts = [jnp.dot(chosen, part, preferred_element_type=F32) for part in (high, low)]
    tall_ref[...] = jnp.concatenate(parts, axis=0).T
    wide_ref[:, s.bz : s.bzp, :] = jnp.zeros((s.bx * s.by, s.bzp - s.bz, 2 * s.locals), F32)
    for g in range(s.bx * s.by):
        wide_ref[g, 0 : s.bz, :] = tall_ref[g * s.bz : (g + 1) * s.bz, :]
    for x in range(s.bx):
        wide = wide_ref[x * s.by : (x + 1) * s.by].reshape(s.by * s.bzp, 2 * s.locals)
        by_atom_ref[x] = wide.T.astype(BF16)
    total = jnp.zeros((s.locals, s.waves), F32)
    atoms = lax.broadcasted_iota(jnp.int32, (s.locals, coupling_ref.shape[1]), 1)
    weight = jnp.sum(jnp.where(atoms == local_atoms(s.own, atoms.shape), coupling_ref[...], 0.0), axis=1, keepdims=True)
    weight_ref[...] = jnp.broadcast_to(weight, weight_ref.shape)
    blank(low_ref, s.z_rows)
    blank(high_ref, 0)
    whole.wait()
    for x in range(s.bx):
        plane = jnp.concatenate([start_ref[x], jnp.zeros((s.by, s.bzp - s.bz, s.waves), F32)], axis=1)
        field_ref[x, 0 : s.by] = plane
        total = total + split_sums(by_atom_ref[x], s.locals, plane.reshape(s.by * s.bzp, s.waves))
    total_ref[...] = total
    half = 4 * s.own
    for x in range(s.bx):
        low_ref[x * s.by : (x + 1) * s.by] = field_ref[x, 0 : s.by, 0, :]
    put_split(low_ref, s.z_rows, total[0:half])
    put_split(high_ref, 0, total[half:])
    put_z(s, msg_refs, low_ref, high_ref)


def node_body(s, wide_ref, by_node_ref, lowest_ref, lowest_by_node_ref):
    for x in range(s.bx):
        wide = wide_ref[x * s.by : (x + 1) * s.by].reshape(s.by * s.bzp, 2 * s.locals)
        by_node_ref[x] = jnp.concatenate([wide, wide[:, 0 : s.locals]], axis=1).astype(BF16)
    line = wide_ref[:, 0, :]
    lowest_by_node_ref[...] = jnp.concatenate([line, line[:, 0 : s.locals]], axis=1).astype(BF16)
    lowest = line.T
    if s.z_plane > s.z_rows:
        lowest = jnp.concatenate([lowest, jnp.zeros((2 * s.locals, s.z_plane - s.z_rows), F32)], axis=1)
    lowest_ref[...] = lowest.astype(BF16)


def put_sides(s, field_ref, x, y, x_ref, y_ref, xy_ref):
    for n in range(s.by):
        x_ref[n * s.span : (n + 1) * s.span] = field_ref[x, n, 0 : s.span, :]
    for n in range(s.bx):
        y_ref[n * s.span : (n + 1) * s.span] = field_ref[n, y, 0 : s.span, :]
    xy_ref[0 : s.span] = field_ref[x, y, 0 : s.span, :]
    for ref, used in ((x_ref, s.x_rows), (y_ref, s.y_rows), (xy_ref, s.span)):
        blank(ref, used)


def send_sides(s, x_ref, y_ref, xy_ref, msg_refs, parts):
    for ref, used, part, msg_ref in zip((x_ref, y_ref, xy_ref), (s.x_rows, s.y_rows, s.span), parts, msg_refs):
        put_split(ref, used, part)
        msg_ref[...] = ref[...].astype(BF16)


def get_sides(s, received, x_ref, y_ref, xy_ref):
    parts = []
    for ref, used, msg_ref in zip((x_ref, y_ref, xy_ref), (s.x_rows, s.y_rows, s.span), received):
        ref[...] = msg_ref[...].astype(F32)
        parts.append(get_split(ref, used, 2 * s.own))
    return parts


def add_sides(s, field_ref, x_ref, y_ref, xy_ref):
    for n in range(s.by):
        field_ref[0, n, 0 : s.span, :] += x_ref[n * s.span : (n + 1) * s.span]
    for n in range(s.bx):
        field_ref[n, 0, 0 : s.span, :] += y_ref[n * s.span : (n + 1) * s.span]
    field_ref[0, 0, 0 : s.span, :] += xy_ref[0 : s.span]


def add_ends(s, x_ref, y_ref, xy_ref, z, plane_ref):
    for n in range(s.by):
        at = n * s.span + z
        x_ref[at : at + 1] += plane_ref[n : n + 1]
    for n in range(s.bx):
        at = n * s.span + z
        y_ref[at : at + 1] += plane_ref[n * s.by : n * s.by + 1]
    xy_ref[z : z + 1] += plane_ref[0:1]


def send_down(s, total, msg_refs, part_ref, x_ref, y_ref, xy_ref):
    corner, x_part, y_part, own_part = columns(s, total)
    part_ref[...] = own_part
    send_sides(s, x_ref, y_ref, xy_ref, msg_refs, (x_part, y_part, corner))


def first_down_body(s, field_ref, total_ref, early_ref, *refs):
    del early_ref
    count = 2 - s.pairs
    received, refs = refs[:count], refs[count:]
    *msg_refs, part_ref, above_ref, below_ref, x_ref, y_ref, xy_ref = refs
    get_z(s, received, above_ref, below_ref)
    half = 4 * s.own
    total = total_ref[...] + jnp.concatenate([get_split(below_ref, 0, half), get_split(above_ref, s.z_rows, half)], axis=0)
    put_sides(s, field_ref, 0, 0, x_ref, y_ref, xy_ref)
    add_ends(s, x_ref, y_ref, xy_ref, s.bz, above_ref)
    send_down(s, total, msg_refs, part_ref, x_ref, y_ref, xy_ref)


def first_fill_body(s, before_ref, sent_ref, *refs):
    del before_ref, sent_ref
    count = 2 - s.pairs
    received, (field_ref, above_ref, below_ref) = refs[:count], refs[count:]
    get_z(s, received, above_ref, below_ref)
    for x in range(s.bx):
        field_ref[x, 0 : s.by, s.bz, :] = above_ref[x * s.by : (x + 1) * s.by]


def cell_body(s, before_ref, from_x_ref, from_y_ref, from_xy_ref, part_ref, weight_ref, *refs):
    matrix_refs, refs = refs[: s.cells[0]], refs[s.cells[0] :]
    field_ref, sums_ref, *msg_refs, own_ref, x_ref, y_ref, xy_ref = refs
    del before_ref
    parts = get_sides(s, (from_x_ref, from_y_ref, from_xy_ref), x_ref, y_ref, xy_ref)
    rest = jnp.zeros((s.bzp - s.span, s.waves), F32)
    for n in range(s.by):
        field_ref[s.bx, n, 0 : s.span, :] = x_ref[n * s.span : (n + 1) * s.span]
        field_ref[s.bx, n, s.span :, :] = rest
    for n in range(s.bx):
        field_ref[n, s.by, 0 : s.span, :] = y_ref[n * s.span : (n + 1) * s.span]
        field_ref[n, s.by, s.span :, :] = rest
    field_ref[s.bx, s.by, 0 : s.span, :] = xy_ref[0 : s.span]
    field_ref[s.bx, s.by, s.span :, :] = rest
    weight = columns(s, weight_ref[...])[3]
    total = (part_ref[...] + parts[0] + parts[1] + parts[2]) * weight
    own_ref[...] = total
    apply_cells(s, field_ref, matrix_refs, sums_ref)
    join_sides(s, sums_ref, x_ref, y_ref, xy_ref)
    send_sides(s, x_ref, y_ref, xy_ref, msg_refs, (total, total, total))


def apply_cells(s, field_ref, matrix_refs, sums_ref):
    order, side, group = s.order, s.side, s.group
    used = side * side * group
    for i in range(s.cells[0]):
        for j in range(s.cells[1]):
            for k in range(s.cells[2]):
                first = k * order
                values = field_ref[i * order : i * order + side, j * order : j * order + side, first : first + group]
                values = values.reshape(used, s.waves)
                if s.padded > used:
                    values = jnp.concatenate([values, jnp.zeros((s.padded - used, s.waves), F32)], axis=0)
                product = jnp.dot(matrix_refs[i][j, k], values.astype(BF16), preferred_element_type=F32)
                product = product[0:used].reshape(side, side, group, s.waves)
                x0, x1, y0, y1 = i * order, i * order + side, j * order, j * order + side
                a, b = int(i > 0), int(j > 0)
                sums_ref[k, x0 + a : x1, y0 + b : y1] = product[a:, b:]
                if a:
                    sums_ref[k, x0, y0 + b : y1] += product[0, b:]
                if b:
                    sums_ref[k, x0 + a : x1, y0] += product[a:, 0]
                if a and b:
                    sums_ref[k, x0, y0] += product[0, 0]


def join_cells(s, sums_ref, out_ref):
    count = s.by
    for x in range(s.bx):
        out_ref[x, :, 0 : s.group, :] = sums_ref[0, x, 0:count]
        out_ref[x, :, s.group :, :] = jnp.zeros((count, s.bzp - s.group, s.waves), F32)
        for k in range(1, s.cells[2]):
            out_ref[x, :, k * s.order : k * s.order + s.group, :] += sums_ref[k, x, 0:count]


def join_sides(s, sums_ref, x_ref, y_ref, xy_ref):
    last = s.cells[2] - 1

    def join(rows_ref, at, x, y):
        for k in range(s.cells[2]):
            count = s.order + int(k == last)
            first = at + k * s.order
            rows_ref[first : first + count] = sums_ref[k, x, y, 0:count, :]
            if k:
                rows_ref[first : first + 1] += sums_ref[k - 1, x, y, s.order : s.order + 1, :]

    for n in range(s.by):
        join(x_ref, n * s.span, s.bx, n)
    for n in range(s.bx):
        join(y_ref, n * s.span, n, s.by)
    join(xy_ref, 0, s.bx, s.by)
    for ref, used in ((x_ref, s.x_rows), (y_ref, s.y_rows), (xy_ref, s.span)):
        blank(ref, used)


def stacked(totals):
    high, low = halves(totals)
    return jnp.concatenate([high, high, low], axis=0).astype(BF16)


def swap_body(s, block_ref, from_x_ref, from_y_ref, from_xy_ref, own_ref, lowest_by_node_ref, *refs):
    *msg_refs, x_ref, y_ref, xy_ref, low_ref, high_ref = refs
    x_part, y_part, corner = get_sides(s, (from_x_ref, from_y_ref, from_xy_ref), x_ref, y_ref, xy_ref)
    stack = stacked(from_columns(s, [corner, x_part, y_part, own_ref[...]]))
    low_ref[0 : s.z_rows] = jnp.dot(lowest_by_node_ref[...], stack, preferred_element_type=F32)
    for x in range(s.bx):
        low_ref[x * s.by : (x + 1) * s.by] += block_ref[x, :, 0, :]
        high_ref[x * s.by : (x + 1) * s.by] = block_ref[x, :, s.bz, :]
    for ref, z in ((low_ref, 0), (high_ref, s.bz)):
        for n in range(s.by):
            ref[n : n + 1] += x_ref[n * s.span + z : n * s.span + z + 1]
        for n in range(s.bx):
            ref[n * s.by : n * s.by + 1] += y_ref[n * s.span + z : n * s.span + z + 1]
        ref[0:1] += xy_ref[z : z + 1]
        blank(ref, s.z_rows)
    put_z(s, msg_refs, low_ref, high_ref)


def middle_body(s, block_ref, from_x_ref, from_y_ref, from_xy_ref, own_ref, by_node_ref, field_ref, x_ref, y_ref, xy_ref):
    x_part, y_part, corner = get_sides(s, (from_x_ref, from_y_ref, from_xy_ref), x_ref, y_ref, xy_ref)
    stack = stacked(from_columns(s, [corner, x_part, y_part, own_ref[...]]))
    for x in range(s.bx):
        image = jnp.dot(by_node_ref[x], stack, preferred_element_type=F32)
        field_ref[x, 0 : s.by] = image.reshape(s.by, s.bzp, s.waves) + block_ref[x]
    add_sides(s, field_ref, x_ref, y_ref, xy_ref)


def sums_body(s, field_ref, by_atom_ref, total_ref):
    total = jnp.zeros((s.locals, s.waves), F32)
    for x in range(s.bx):
        total = total + split_sums(by_atom_ref[x], s.locals, field_ref[x, 0 : s.by].reshape(s.by * s.bzp, s.waves))
    total_ref[...] = total


def second_down_body(s, field_ref, total_ref, lowest_ref, *refs):
    count = 2 - s.pairs
    received, refs = refs[:count], refs[count:]
    *msg_refs, part_ref, above_ref, below_ref, x_ref, y_ref, xy_ref = refs
    get_z(s, received, above_ref, below_ref)
    total = total_ref[...] + split_sums(lowest_ref[...], s.locals, below_ref[...])
    put_sides(s, field_ref, 0, 0, x_ref, y_ref, xy_ref)
    add_ends(s, x_ref, y_ref, xy_ref, s.bz, above_ref)
    add_ends(s, x_ref, y_ref, xy_ref, 0, below_ref)
    send_down(s, total, msg_refs, part_ref, x_ref, y_ref, xy_ref)


def second_fill_body(s, before_ref, sent_ref, *refs):
    del before_ref, sent_ref
    count = 2 - s.pairs
    received, (field_ref, above_ref, below_ref) = refs[:count], refs[count:]
    get_z(s, received, above_ref, below_ref)
    for x in range(s.bx):
        field_ref[x, 0 : s.by, s.bz, :] += above_ref[x * s.by : (x + 1) * s.by]
        field_ref[x, 0 : s.by, 0, :] += below_ref[x * s.by : (x + 1) * s.by]


def fold_body(s, before_ref, from_x_ref, from_y_ref, from_xy_ref, own_ref, *refs):
    del before_ref
    block_ref, *msg_refs, total_ref, x_ref, y_ref, xy_ref, low_ref, high_ref = refs
    x_part, y_part, corner = get_sides(s, (from_x_ref, from_y_ref, from_xy_ref), x_ref, y_ref, xy_ref)
    total = from_columns(s, [corner, x_part, y_part, own_ref[...]])
    total_ref[...] = total
    add_sides(s, block_ref, x_ref, y_ref, xy_ref)
    half = 4 * s.own
    for x in range(s.bx):
        high_ref[x * s.by : (x + 1) * s.by] = block_ref[x, :, s.bz, :]
    blank(high_ref, s.z_rows)
    blank(low_ref, 0)
    put_split(low_ref, 0, total[0:half])
    put_split(high_ref, s.z_rows, total[half:])
    put_z(s, msg_refs, low_ref, high_ref)


def last_body(s, start_ref, block_ref, total_ref, by_node_ref, *refs):
    count = 2 - s.pairs
    received, refs = refs[:count], refs[count:]
    out_hbm, above_ref, below_ref, plane_ref, out_ref, sems = refs
    get_z(s, received, above_ref, below_ref)
    half = 4 * s.own
    total = total_ref[...] + jnp.concatenate([get_split(below_ref, s.z_rows, half), get_split(above_ref, 0, half)], axis=0)
    stack = stacked(total)
    copies = []
    for x in range(s.bx):
        image = jnp.dot(by_node_ref[x], stack, preferred_element_type=F32)
        plane_ref[x] = image.reshape(s.by, s.bzp, s.waves) + block_ref[x]
        plane_ref[x, :, 0, :] += below_ref[x * s.by : (x + 1) * s.by]
        out_ref[x] = 2.0 * plane_ref[x, :, 0 : s.bz] - start_ref[x]
        if (x + 1) % s.few_out == 0:
            span = pl.ds(x + 1 - s.few_out, s.few_out)
            copies.append(pltpu.make_async_copy(out_ref.at[span], out_hbm.at[span], sems.at[x // s.few_out]))
            copies[-1].start()
    for copy in copies:
        copy.wait()


def selector(count, chosen):
    row = lax.broadcasted_iota(jnp.int32, count, 0)
    column = lax.broadcasted_iota(jnp.int32, count, 1)
    return chosen(row, column).astype(F32).astype(BF16)


def matrix_body(s, part, matrix_hbm, out_ref, raw_ref, flat_ref, half_ref, sems):
    cells_y, cells_z = s.cells[1:]
    side, group = s.side, s.group
    nodes = side**3
    copies = [pltpu.make_async_copy(matrix_hbm.at[part, j], raw_ref.at[j], sems.at[j]) for j in range(cells_y)]
    for copy in copies:
        copy.start()
    wide = 256 // group * side
    spans = []
    for first in range(0, s.padded, 256):
        low = first // group * side // 128 * 128
        high = min(nodes, first // group * side + wide)
        width = min(256, s.padded - first)
        spans.append((first, low, high, selector((high - low, width), lambda m, c, low=low, first=first: (
            ((c + first) % group < side) & (m + low == (c + first) // group * side + (c + first) % group)))))
    tall = 128 // group * side
    picks = jnp.concatenate(
        [
            selector((128, tall * cells_z), lambda r, m, k=k: (r % group < side) & (m == (r // group * side + r % group) * cells_z + k))
            for k in range(cells_z)
        ],
        axis=0,
    )
    for j in range(cells_y):
        copies[j].wait()
        flat_ref[...] = raw_ref[j].reshape(nodes * cells_z, nodes)
        for first, low, high, spread in spans:
            half = jnp.dot(flat_ref[:, low:high], spread, preferred_element_type=F32)
            half_ref[:, first : first + spread.shape[1]] = half.astype(BF16)
        for first in range(0, s.padded, 128):
            count = min(128, s.padded - first)
            low = first // group * side * cells_z
            high = min(nodes * cells_z, low + tall * cells_z)
            rows = jnp.dot(picks[:, 0 : high - low], half_ref[low:high], preferred_element_type=F32).astype(BF16)
            for k in range(cells_z):
                out_ref[j, k, first : first + count] = rows[128 * k : 128 * k + count]


def regrouped(s, cell_matrices, part):
    shape = cell_matrices.shape
    nodes = shape[3]
    return call(
        matrix_body,
        s,
        [jax.ShapeDtypeStruct(shape[1:3] + (s.padded, s.padded), BF16)],
        [
            pltpu.VMEM((shape[1], nodes, shape[2], nodes), BF16),
            pltpu.VMEM((nodes * shape[2], nodes), BF16),
            pltpu.VMEM((nodes * shape[2], s.padded), BF16),
            pltpu.SemaphoreType.DMA((shape[1],)),
        ],
        [cell_matrices.transpose(0, 1, 3, 2, 4)],
        spaces={0: pltpu.HBM},
        extra=(part,),
    )[0]


def along_z(s, msgs):
    if s.pairs:
        return [shifted(msgs[0], (0, 0, 1))]
    return [shifted(msgs[0], (0, 0, -1)), shifted(msgs[1], (0, 0, 1))]


def along_xy(msgs, by):
    return [shifted(msg, (by * dx, by * dy, 0)) for msg, dx, dy in zip(msgs, (1, 0, 1), (0, 1, 1))]


def local(wavefunctions, cell_matrices, projectors, slot_atoms, atom_coupling):
    atom_count = atom_coupling.shape[0]
    devices = 1
    for axis in AXES:
        devices *= lax.axis_size(axis)
    own = atom_count // devices
    s = Sizes(wavefunctions.shape, cell_matrices.shape, own, lax.axis_size("gz") == 2)
    plane = s.by * s.bzp
    sides = s.side_rows()
    field, by_atom, wide, *msgs, total, weight = call(
        first_body,
        s,
        [
            s.extended(),
            jax.ShapeDtypeStruct((s.bx, 2 * s.locals, plane), BF16),
            jax.ShapeDtypeStruct((s.z_rows, s.bzp, 2 * s.locals), F32),
        ]
        + s.z_msgs(s.z_both, s.z_sums)
        + [s.rows(s.locals), s.rows(s.locals)],
        [
            s.scratch(s.bx, s.by, s.bz),
            pltpu.VMEM(projectors.shape, F32),
            pltpu.VMEM(slot_atoms.shape, jnp.int32),
            pltpu.VMEM((1, atom_count), F32),
            pltpu.VMEM((s.bx * s.by * s.bz, 2 * s.locals), F32),
            s.scratch(s.z_both),
            s.scratch(s.z_sums),
            pltpu.SemaphoreType.DMA((1,)),
            pltpu.SemaphoreType.DMA((3,)),
        ],
        [wavefunctions, projectors, slot_atoms, atom_coupling[None, :]],
        spaces={0: pltpu.HBM, 1: pltpu.HBM, 2: pltpu.HBM, 3: pltpu.HBM},
    )
    matrices = [regrouped(s, cell_matrices, part) for part in range(s.cells[0])]
    received = along_z(s, msgs)
    *msgs, part = call(
        first_down_body,
        s,
        s.side_msgs() + [s.rows(2 * own)],
        [s.scratch(s.z_both), s.scratch(s.z_sums)] + sides,
        [field, total, matrices[0]] + received,
    )
    fills = (first_fill_body, [s.scratch(s.z_both), s.scratch(s.z_sums)], received)

    def cells(field, msgs, part, fills):
        body, scratch, along = fills
        received = along_xy(msgs, -1)
        (field,) = call(body, s, [s.extended()], scratch, [field, part] + along, aliases={0: 0})
        _, sums, *msgs, mine = call(
            cell_body,
            s,
            [s.extended(), jax.ShapeDtypeStruct((s.cells[2], s.bx + 1, s.by + 1, s.group, s.waves), F32)]
            + s.side_msgs()
            + [s.rows(2 * own)],
            sides,
            [field] + received + [part, weight] + matrices,
            aliases={0: 0},
        )
        received = along_xy(msgs, 1)
        (block,) = call(join_cells, s, [s.block()], [], [sums])
        return block, received, mine

    block, received, mine = cells(field, msgs, part, fills)
    by_node, lowest, lowest_by_node = call(
        node_body,
        s,
        [
            jax.ShapeDtypeStruct((s.bx, plane, 3 * s.locals), BF16),
            jax.ShapeDtypeStruct((2 * s.locals, s.z_plane), BF16),
            jax.ShapeDtypeStruct((s.z_rows, 3 * s.locals), BF16),
        ],
        [],
        [wide],
    )
    msgs = call(
        swap_body,
        s,
        s.z_msgs(s.z_plane, s.z_plane),
        sides + [s.scratch(s.z_plane), s.scratch(s.z_plane)],
        [block] + received + [mine, lowest_by_node],
    )
    swapped = along_z(s, msgs)
    (field,) = call(middle_body, s, [s.extended()], sides, [block] + received + [mine, by_node])
    received = swapped
    (total,) = call(sums_body, s, [s.rows(s.locals)], [], [field, by_atom])
    *msgs, part = call(
        second_down_body,
        s,
        s.side_msgs() + [s.rows(2 * own)],
        [s.scratch(s.z_plane), s.scratch(s.z_plane)] + sides,
        [field, total, lowest] + received,
    )
    fills = (second_fill_body, [s.scratch(s.z_plane), s.scratch(s.z_plane)], received)
    block, received, mine = cells(field, msgs, part, fills)
    block, *msgs, total = call(
        fold_body,
        s,
        [s.block()] + s.z_msgs(s.z_sums, s.z_both) + [s.rows(s.locals)],
        sides + [s.scratch(s.z_sums), s.scratch(s.z_both)],
        [block] + received + [mine],
        aliases={0: 0},
    )
    received = along_z(s, msgs)
    (out,) = call(
        last_body,
        s,
        [jax.ShapeDtypeStruct(wavefunctions.shape, F32)],
        [
            s.scratch(s.z_sums),
            s.scratch(s.z_both),
            s.scratch(s.bx, s.by, s.bzp),
            s.scratch(s.bx, s.by, s.bz),
            pltpu.SemaphoreType.DMA((s.bx // s.few_out,)),
        ],
        [wavefunctions, block, total, by_node] + received,
        out_spaces={0: pltpu.HBM},
    )
    return out


def solution(mesh):
    return jax.shard_map(
        local,
        mesh=mesh,
        in_specs=(
            P("gx", "gy", "gz", None),
            P("gx", "gy", "gz", None, None),
            P(("gx", "gy", "gz"), None, None),
            P(("gx", "gy", "gz"), None),
            P(),
        ),
        out_specs=P("gx", "gy", "gz", None),
        check_vma=False,
    )
```

```python
import functools

import jax
import jax.numpy as jnp
from jax import lax
from jax.experimental import pallas as pl
from jax.experimental.pallas import tpu as pltpu
from jax.sharding import PartitionSpec as P

AXES = ("gx", "gy", "gz")
F32 = jnp.float32
BF16 = jnp.bfloat16
LIMIT = 12 * 1024 * 1024


def up_to(value, unit):
    return -(-value // unit) * unit


def shifted(value, shift):
    sizes = [lax.axis_size(axis) for axis in AXES]
    pairs = []
    for x in range(sizes[0]):
        for y in range(sizes[1]):
            for z in range(sizes[2]):
                here = (x * sizes[1] + y) * sizes[2] + z
                there = [(p + s) % n for p, s, n in zip((x, y, z), shift, sizes)]
                pairs.append((here, (there[0] * sizes[1] + there[1]) * sizes[2] + there[2]))
    return lax.ppermute(value, AXES, pairs)


def halves(value):
    high = value.astype(BF16).astype(F32)
    return high, value - high


def put_split(rows_ref, start, value):
    count = value.shape[0]
    high, low = halves(value)
    rows_ref[start : start + count] = high
    rows_ref[start + count : start + 2 * count] = low


def get_split(rows_ref, start, count):
    return rows_ref[start : start + count] + rows_ref[start + count : start + 2 * count]


class Sizes:
    def __init__(self, field_shape, cell_shape, own, pairs):
        self.bx, self.by, self.bz, self.waves = field_shape
        self.cells = cell_shape[:3]
        self.order = self.bx // cell_shape[0]
        self.side = self.order + 1
        self.group = up_to(self.side, 8)
        self.padded = up_to(self.side * self.side * self.group, 16)
        self.bzp = up_to(max(self.bz + 1, (cell_shape[2] - 1) * self.order + self.group), 16)
        self.few_out = max(n for n in (1, 2) if self.bx % n == 0)
        self.pairs = pairs
        self.own = own
        self.locals = 8 * own
        self.span = self.bz + 1
        self.z_rows = self.bx * self.by
        self.x_rows = self.by * self.span
        self.y_rows = self.bx * self.span
        self.x_msg = up_to(self.x_rows + 4 * own, 8)
        self.y_msg = up_to(self.y_rows + 4 * own, 8)
        self.xy_msg = up_to(self.span + 4 * own, 8)
        self.z_plane = up_to(self.z_rows, 16)
        self.z_sums = up_to(8 * own, 16)
        self.z_both = up_to(self.z_rows + 8 * own, 16)

    def extended(self):
        return jax.ShapeDtypeStruct((self.bx + 1, self.by + 1, self.bzp, self.waves), F32)

    def block(self):
        return jax.ShapeDtypeStruct((self.bx, self.by, self.bzp, self.waves), F32)

    def rows(self, count, dtype=F32):
        return jax.ShapeDtypeStruct((count, self.waves), dtype)

    def scratch(self, *shape):
        return pltpu.VMEM(shape + (self.waves,), F32)

    def z_msgs(self, down, up):
        return [self.rows(down + up, BF16)] if self.pairs else [self.rows(down, BF16), self.rows(up, BF16)]

    def side_msgs(self):
        return [self.rows(n, BF16) for n in (self.x_msg, self.y_msg, self.xy_msg)]

    def side_rows(self):
        return [self.scratch(n) for n in (self.x_msg, self.y_msg, self.xy_msg)]


VMEM = pltpu.VMEM


def call(body, sizes, outs, scratch, args, spaces=None, out_spaces=None, aliases=None, extra=()):
    spaces = spaces or {}
    out_spaces = out_spaces or {}
    outs = [out_spaces.get(n, VMEM)(out.shape, out.dtype) for n, out in enumerate(outs)]
    args = [pltpu.with_memory_space_constraint(arg, spaces.get(n, VMEM)) for n, arg in enumerate(args)]
    return pl.pallas_call(
        functools.partial(body, sizes, *extra),
        out_shape=outs,
        in_specs=[pl.BlockSpec(memory_space=spaces.get(n, VMEM)) for n in range(len(args))],
        out_specs=[pl.BlockSpec(memory_space=out_spaces.get(n, VMEM)) for n in range(len(outs))],
        scratch_shapes=scratch,
        input_output_aliases=aliases or {},
        compiler_params=pltpu.CompilerParams(vmem_limit_bytes=LIMIT),
    )(*args)


def local_atoms(own, shape):
    sizes = [lax.axis_size(axis) for axis in AXES]
    here = [lax.axis_index(axis) for axis in AXES]
    ids = []
    for dz in (1, 0):
        for dx in (1, 0):
            for dy in (1, 0):
                x, y, z = (lax.rem(h + n - d, n) for h, n, d in zip(here, sizes, (dx, dy, dz)))
                owner = (x * sizes[1] + y) * sizes[2] + z
                ids += [owner * own + a for a in range(own)]
    row = lax.broadcasted_iota(jnp.int32, shape, 0)
    table = jnp.zeros(shape, jnp.int32)
    for n, atom in enumerate(ids):
        table = jnp.where(row == n, atom, table)
    return table


def blank(rows_ref, first):
    count = rows_ref.shape[0] - first
    if count:
        rows_ref[first:] = jnp.zeros((count,) + rows_ref.shape[1:], F32)


def split_sums(by_atom, count, field):
    high = field.astype(BF16)
    low = (field - high.astype(F32)).astype(BF16)
    with_high = jnp.dot(by_atom, high, preferred_element_type=F32)
    with_low = jnp.dot(by_atom[0:count], low, preferred_element_type=F32)
    return with_high[0:count] + with_high[count : 2 * count] + with_low


def put_z(s, msg_refs, down_ref, up_ref):
    if s.pairs:
        count = down_ref.shape[0]
        msg_refs[0][0:count] = down_ref[...].astype(BF16)
        msg_refs[0][count:] = up_ref[...].astype(BF16)
    else:
        msg_refs[0][...] = down_ref[...].astype(BF16)
        msg_refs[1][...] = up_ref[...].astype(BF16)


def get_z(s, msg_refs, above_ref, below_ref):
    if s.pairs:
        count = above_ref.shape[0]
        above_ref[...] = msg_refs[0][0:count].astype(F32)
        below_ref[...] = msg_refs[0][count:].astype(F32)
    else:
        above_ref[...] = msg_refs[0][...].astype(F32)
        below_ref[...] = msg_refs[1][...].astype(F32)


def columns(s, totals):
    own, half = s.own, 4 * s.own
    return [
        jnp.concatenate([totals[n * own : (n + 1) * own], totals[half + n * own : half + (n + 1) * own]], axis=0) for n in range(4)
    ]


def from_columns(s, parts):
    own = s.own
    return jnp.concatenate([part[0:own] for part in parts] + [part[own : 2 * own] for part in parts], axis=0)


def first_body(
    s, start_hbm, rows_hbm, slots_hbm, coupling_hbm,
    field_ref, by_atom_ref, wide_ref, *refs
):
    *msg_refs, total_ref, weight_ref, start_ref, rows_ref, slots_ref, coupling_ref, tall_ref, low_ref, high_ref, sems, small_sems = refs
    small = [
        pltpu.make_async_copy(rows_hbm, rows_ref, small_sems.at[0]),
        pltpu.make_async_copy(slots_hbm, slots_ref, small_sems.at[1]),
        pltpu.make_async_copy(coupling_hbm, coupling_ref, small_sems.at[2]),
    ]
    for copy in small:
        copy.start()
    whole = pltpu.make_async_copy(start_hbm, start_ref, sems.at[0])
    whole.start()
    for copy in small:
        copy.wait()
    slots = slots_ref[...]
    chosen = (local_atoms(s.own, (s.locals, slots.shape[1])) == slots).astype(F32).astype(BF16)
    rows = rows_ref[0]
    high = rows.astype(BF16)
    low = (rows - high.astype(F32)).astype(BF16)
    parts = [jnp.dot(chosen, part, preferred_element_type=F32) for part in (high, low)]
    tall_ref[...] = jnp.concatenate(parts, axis=0).T
    wide_ref[:, s.bz : s.bzp, :] = jnp.zeros((s.bx * s.by, s.bzp - s.bz, 2 * s.locals), F32)
    for g in range(s.bx * s.by):
        wide_ref[g, 0 : s.bz, :] = tall_ref[g * s.bz : (g + 1) * s.bz, :]
    for x in range(s.bx):
        wide = wide_ref[x * s.by : (x + 1) * s.by].reshape(s.by * s.bzp, 2 * s.locals)
        by_atom_ref[x] = wide.T.astype(BF16)
    sums = []
    atoms = lax.broadcasted_iota(jnp.int32, (s.locals, coupling_ref.shape[1]), 1)
    weight = jnp.sum(jnp.where(atoms == local_atoms(s.own, atoms.shape), coupling_ref[...], 0.0), axis=1, keepdims=True)
    weight_ref[...] = jnp.broadcast_to(weight, weight_ref.shape)
    blank(low_ref, s.z_rows)
    blank(high_ref, 0)
    whole.wait()
    for x in range(s.bx):
        plane = jnp.concatenate([start_ref[x], jnp.zeros((s.by, s.bzp - s.bz, s.waves), F32)], axis=1)
        field_ref[x, 0 : s.by] = plane
        sums.append(split_sums(by_atom_ref[x], s.locals, plane.reshape(s.by * s.bzp, s.waves)))
    total = sum(sums[1:], sums[0])
    total_ref[...] = total
    half = 4 * s.own
    for x in range(s.bx):
        low_ref[x * s.by : (x + 1) * s.by] = field_ref[x, 0 : s.by, 0, :]
    put_split(low_ref, s.z_rows, total[0:half])
    put_split(high_ref, 0, total[half:])
    put_z(s, msg_refs, low_ref, high_ref)


def node_body(s, wide_ref, by_node_ref, lowest_ref, lowest_by_node_ref):
    for x in range(s.bx):
        wide = wide_ref[x * s.by : (x + 1) * s.by].reshape(s.by * s.bzp, 2 * s.locals)
        by_node_ref[x] = jnp.concatenate([wide, wide[:, 0 : s.locals]], axis=1).astype(BF16)
    line = wide_ref[:, 0, :]
    lowest_by_node_ref[...] = jnp.concatenate([line, line[:, 0 : s.locals]], axis=1).astype(BF16)
    lowest = line.T
    if s.z_plane > s.z_rows:
        lowest = jnp.concatenate([lowest, jnp.zeros((2 * s.locals, s.z_plane - s.z_rows), F32)], axis=1)
    lowest_ref[...] = lowest.astype(BF16)


def put_sides(s, field_ref, x, y, x_ref, y_ref, xy_ref):
    for n in range(s.by):
        x_ref[n * s.span : (n + 1) * s.span] = field_ref[x, n, 0 : s.span, :]
    for n in range(s.bx):
        y_ref[n * s.span : (n + 1) * s.span] = field_ref[n, y, 0 : s.span, :]
    xy_ref[0 : s.span] = field_ref[x, y, 0 : s.span, :]
    for ref, used in ((x_ref, s.x_rows), (y_ref, s.y_rows), (xy_ref, s.span)):
        blank(ref, used)


def send_sides(s, x_ref, y_ref, xy_ref, msg_refs, parts):
    for ref, used, part, msg_ref in zip((x_ref, y_ref, xy_ref), (s.x_rows, s.y_rows, s.span), parts, msg_refs):
        put_split(ref, used, part)
        msg_ref[...] = ref[...].astype(BF16)


def get_sides(s, received, x_ref, y_ref, xy_ref):
    parts = []
    for ref, used, msg_ref in zip((x_ref, y_ref, xy_ref), (s.x_rows, s.y_rows, s.span), received):
        ref[...] = msg_ref[...].astype(F32)
        parts.append(get_split(ref, used, 2 * s.own))
    return parts


def add_sides(s, field_ref, x_ref, y_ref, xy_ref):
    for n in range(s.by):
        field_ref[0, n, 0 : s.span, :] += x_ref[n * s.span : (n + 1) * s.span]
    for n in range(s.bx):
        field_ref[n, 0, 0 : s.span, :] += y_ref[n * s.span : (n + 1) * s.span]
    field_ref[0, 0, 0 : s.span, :] += xy_ref[0 : s.span]


def add_ends(s, x_ref, y_ref, xy_ref, z, plane_ref):
    for n in range(s.by):
        at = n * s.span + z
        x_ref[at : at + 1] += plane_ref[n : n + 1]
    for n in range(s.bx):
        at = n * s.span + z
        y_ref[at : at + 1] += plane_ref[n * s.by : n * s.by + 1]
    xy_ref[z : z + 1] += plane_ref[0:1]


def send_down(s, total, msg_refs, part_ref, x_ref, y_ref, xy_ref):
    corner, x_part, y_part, own_part = columns(s, total)
    part_ref[...] = own_part
    send_sides(s, x_ref, y_ref, xy_ref, msg_refs, (x_part, y_part, corner))


def first_down_body(s, field_ref, total_ref, early_ref, *refs):
    del early_ref
    count = 2 - s.pairs
    received, refs = refs[:count], refs[count:]
    *msg_refs, part_ref, above_ref, below_ref, x_ref, y_ref, xy_ref = refs
    get_z(s, received, above_ref, below_ref)
    half = 4 * s.own
    total = total_ref[...] + jnp.concatenate([get_split(below_ref, 0, half), get_split(above_ref, s.z_rows, half)], axis=0)
    put_sides(s, field_ref, 0, 0, x_ref, y_ref, xy_ref)
    add_ends(s, x_ref, y_ref, xy_ref, s.bz, above_ref)
    send_down(s, total, msg_refs, part_ref, x_ref, y_ref, xy_ref)


def first_fill_body(s, before_ref, sent_ref, *refs):
    del before_ref, sent_ref
    count = 2 - s.pairs
    received, (field_ref, above_ref, below_ref) = refs[:count], refs[count:]
    get_z(s, received, above_ref, below_ref)
    for x in range(s.bx):
        field_ref[x, 0 : s.by, s.bz, :] = above_ref[x * s.by : (x + 1) * s.by]


def cell_body(s, before_ref, from_x_ref, from_y_ref, from_xy_ref, part_ref, weight_ref, *refs):
    matrix_refs, refs = refs[: s.cells[0]], refs[s.cells[0] :]
    field_ref, sums_ref, *msg_refs, own_ref, x_ref, y_ref, xy_ref = refs
    del before_ref
    parts = get_sides(s, (from_x_ref, from_y_ref, from_xy_ref), x_ref, y_ref, xy_ref)
    rest = jnp.zeros((s.bzp - s.span, s.waves), F32)
    for n in range(s.by):
        field_ref[s.bx, n, 0 : s.span, :] = x_ref[n * s.span : (n + 1) * s.span]
        field_ref[s.bx, n, s.span :, :] = rest
    for n in range(s.bx):
        field_ref[n, s.by, 0 : s.span, :] = y_ref[n * s.span : (n + 1) * s.span]
        field_ref[n, s.by, s.span :, :] = rest
    field_ref[s.bx, s.by, 0 : s.span, :] = xy_ref[0 : s.span]
    field_ref[s.bx, s.by, s.span :, :] = rest
    weight = columns(s, weight_ref[...])[3]
    total = (part_ref[...] + parts[0] + parts[1] + parts[2]) * weight
    own_ref[...] = total
    apply_cells(s, field_ref, matrix_refs, sums_ref)
    join_sides(s, sums_ref, x_ref, y_ref, xy_ref)
    send_sides(s, x_ref, y_ref, xy_ref, msg_refs, (total, total, total))


def apply_cells(s, field_ref, matrix_refs, sums_ref):
    order, side, group = s.order, s.side, s.group
    used = side * side * group
    for i in range(s.cells[0]):
        for j in range(s.cells[1]):
            for k in range(s.cells[2]):
                first = k * order
                values = field_ref[i * order : i * order + side, j * order : j * order + side, first : first + group]
                values = values.reshape(used, s.waves)
                if s.padded > used:
                    values = jnp.concatenate([values, jnp.zeros((s.padded - used, s.waves), F32)], axis=0)
                product = jnp.dot(matrix_refs[i][j, k], values.astype(BF16), preferred_element_type=F32)
                product = product[0:used].reshape(side, side, group, s.waves)
                x0, x1, y0, y1 = i * order, i * order + side, j * order, j * order + side
                a, b = int(i > 0), int(j > 0)
                sums_ref[k, x0 + a : x1, y0 + b : y1] = product[a:, b:]
                if a:
                    sums_ref[k, x0, y0 + b : y1] += product[0, b:]
                if b:
                    sums_ref[k, x0 + a : x1, y0] += product[a:, 0]
                if a and b:
                    sums_ref[k, x0, y0] += product[0, 0]


def join_cells(s, sums_ref, out_ref):
    count = s.by
    for x in range(s.bx):
        out_ref[x, :, 0 : s.group, :] = sums_ref[0, x, 0:count]
        out_ref[x, :, s.group :, :] = jnp.zeros((count, s.bzp - s.group, s.waves), F32)
        for k in range(1, s.cells[2]):
            out_ref[x, :, k * s.order : k * s.order + s.group, :] += sums_ref[k, x, 0:count]


def join_sides(s, sums_ref, x_ref, y_ref, xy_ref):
    last = s.cells[2] - 1

    def join(rows_ref, at, x, y):
        for k in range(s.cells[2]):
            count = s.order + int(k == last)
            first = at + k * s.order
            rows_ref[first : first + count] = sums_ref[k, x, y, 0:count, :]
            if k:
                rows_ref[first : first + 1] += sums_ref[k - 1, x, y, s.order : s.order + 1, :]

    for n in range(s.by):
        join(x_ref, n * s.span, s.bx, n)
    for n in range(s.bx):
        join(y_ref, n * s.span, n, s.by)
    join(xy_ref, 0, s.bx, s.by)
    for ref, used in ((x_ref, s.x_rows), (y_ref, s.y_rows), (xy_ref, s.span)):
        blank(ref, used)


def stacked(totals):
    high, low = halves(totals)
    return jnp.concatenate([high, high, low], axis=0).astype(BF16)


def swap_body(s, block_ref, from_x_ref, from_y_ref, from_xy_ref, own_ref, lowest_by_node_ref, *refs):
    *msg_refs, x_ref, y_ref, xy_ref, low_ref, high_ref = refs
    x_part, y_part, corner = get_sides(s, (from_x_ref, from_y_ref, from_xy_ref), x_ref, y_ref, xy_ref)
    stack = stacked(from_columns(s, [corner, x_part, y_part, own_ref[...]]))
    low_ref[0 : s.z_rows] = jnp.dot(lowest_by_node_ref[...], stack, preferred_element_type=F32)
    for x in range(s.bx):
        low_ref[x * s.by : (x + 1) * s.by] += block_ref[x, :, 0, :]
        high_ref[x * s.by : (x + 1) * s.by] = block_ref[x, :, s.bz, :]
    for ref, z in ((low_ref, 0), (high_ref, s.bz)):
        for n in range(s.by):
            ref[n : n + 1] += x_ref[n * s.span + z : n * s.span + z + 1]
        for n in range(s.bx):
            ref[n * s.by : n * s.by + 1] += y_ref[n * s.span + z : n * s.span + z + 1]
        ref[0:1] += xy_ref[z : z + 1]
        blank(ref, s.z_rows)
    put_z(s, msg_refs, low_ref, high_ref)


def middle_body(s, block_ref, from_x_ref, from_y_ref, from_xy_ref, own_ref, by_node_ref, field_ref, x_ref, y_ref, xy_ref):
    x_part, y_part, corner = get_sides(s, (from_x_ref, from_y_ref, from_xy_ref), x_ref, y_ref, xy_ref)
    stack = stacked(from_columns(s, [corner, x_part, y_part, own_ref[...]]))
    for x in range(s.bx):
        image = jnp.dot(by_node_ref[x], stack, preferred_element_type=F32)
        field_ref[x, 0 : s.by] = image.reshape(s.by, s.bzp, s.waves) + block_ref[x]
    add_sides(s, field_ref, x_ref, y_ref, xy_ref)


def sums_body(s, field_ref, by_atom_ref, total_ref):
    total = jnp.zeros((s.locals, s.waves), F32)
    for x in range(s.bx):
        total = total + split_sums(by_atom_ref[x], s.locals, field_ref[x, 0 : s.by].reshape(s.by * s.bzp, s.waves))
    total_ref[...] = total


def second_down_body(s, field_ref, total_ref, lowest_ref, *refs):
    count = 2 - s.pairs
    received, refs = refs[:count], refs[count:]
    *msg_refs, part_ref, above_ref, below_ref, x_ref, y_ref, xy_ref = refs
    get_z(s, received, above_ref, below_ref)
    total = total_ref[...] + split_sums(lowest_ref[...], s.locals, below_ref[...])
    put_sides(s, field_ref, 0, 0, x_ref, y_ref, xy_ref)
    add_ends(s, x_ref, y_ref, xy_ref, s.bz, above_ref)
    add_ends(s, x_ref, y_ref, xy_ref, 0, below_ref)
    send_down(s, total, msg_refs, part_ref, x_ref, y_ref, xy_ref)


def second_fill_body(s, before_ref, sent_ref, *refs):
    del before_ref, sent_ref
    count = 2 - s.pairs
    received, (field_ref, above_ref, below_ref) = refs[:count], refs[count:]
    get_z(s, received, above_ref, below_ref)
    for x in range(s.bx):
        field_ref[x, 0 : s.by, s.bz, :] += above_ref[x * s.by : (x + 1) * s.by]
        field_ref[x, 0 : s.by, 0, :] += below_ref[x * s.by : (x + 1) * s.by]


def fold_body(s, before_ref, from_x_ref, from_y_ref, from_xy_ref, own_ref, *refs):
    del before_ref
    block_ref, *msg_refs, total_ref, x_ref, y_ref, xy_ref, low_ref, high_ref = refs
    x_part, y_part, corner = get_sides(s, (from_x_ref, from_y_ref, from_xy_ref), x_ref, y_ref, xy_ref)
    total = from_columns(s, [corner, x_part, y_part, own_ref[...]])
    total_ref[...] = total
    add_sides(s, block_ref, x_ref, y_ref, xy_ref)
    half = 4 * s.own
    for x in range(s.bx):
        high_ref[x * s.by : (x + 1) * s.by] = block_ref[x, :, s.bz, :]
    blank(high_ref, s.z_rows)
    blank(low_ref, 0)
    put_split(low_ref, 0, total[0:half])
    put_split(high_ref, s.z_rows, total[half:])
    put_z(s, msg_refs, low_ref, high_ref)


def last_body(s, start_ref, block_ref, total_ref, by_node_ref, *refs):
    count = 2 - s.pairs
    received, refs = refs[:count], refs[count:]
    out_hbm, above_ref, below_ref, plane_ref, out_ref, sems = refs
    get_z(s, received, above_ref, below_ref)
    half = 4 * s.own
    total = total_ref[...] + jnp.concatenate([get_split(below_ref, s.z_rows, half), get_split(above_ref, 0, half)], axis=0)
    stack = stacked(total)
    copies = []
    for x in range(s.bx):
        image = jnp.dot(by_node_ref[x], stack, preferred_element_type=F32)
        plane_ref[x] = image.reshape(s.by, s.bzp, s.waves) + block_ref[x]
        plane_ref[x, :, 0, :] += below_ref[x * s.by : (x + 1) * s.by]
        out_ref[x] = 2.0 * plane_ref[x, :, 0 : s.bz] - start_ref[x]
        if (x + 1) % s.few_out == 0:
            span = pl.ds(x + 1 - s.few_out, s.few_out)
            copies.append(pltpu.make_async_copy(out_ref.at[span], out_hbm.at[span], sems.at[x // s.few_out]))
            copies[-1].start()
    for copy in copies:
        copy.wait()


def selector(count, chosen):
    row = lax.broadcasted_iota(jnp.int32, count, 0)
    column = lax.broadcasted_iota(jnp.int32, count, 1)
    return chosen(row, column).astype(F32).astype(BF16)


def matrix_body(s, part, matrix_hbm, out_ref, raw_ref, flat_ref, half_ref, sems):
    cells_y, cells_z = s.cells[1:]
    side, group = s.side, s.group
    nodes = side**3
    copies = [pltpu.make_async_copy(matrix_hbm.at[part, j], raw_ref.at[j], sems.at[j]) for j in range(cells_y)]
    for copy in copies:
        copy.start()
    wide = 256 // group * side
    spans = []
    for first in range(0, s.padded, 256):
        low = first // group * side // 128 * 128
        high = min(nodes, first // group * side + wide)
        width = min(256, s.padded - first)
        spans.append((first, low, high, selector((high - low, width), lambda m, c, low=low, first=first: (
            ((c + first) % group < side) & (m + low == (c + first) // group * side + (c + first) % group)))))
    tall = 128 // group * side
    picks = jnp.concatenate(
        [
            selector((128, tall * cells_z), lambda r, m, k=k: (r % group < side) & (m == (r // group * side + r % group) * cells_z + k))
            for k in range(cells_z)
        ],
        axis=0,
    )
    for j in range(cells_y):
        copies[j].wait()
        flat_ref[...] = raw_ref[j].reshape(nodes * cells_z, nodes)
        for first, low, high, spread in spans:
            half = jnp.dot(flat_ref[:, low:high], spread, preferred_element_type=F32)
            half_ref[:, first : first + spread.shape[1]] = half.astype(BF16)
        for first in range(0, s.padded, 128):
            count = min(128, s.padded - first)
            low = first // group * side * cells_z
            high = min(nodes * cells_z, low + tall * cells_z)
            rows = jnp.dot(picks[:, 0 : high - low], half_ref[low:high], preferred_element_type=F32).astype(BF16)
            for k in range(cells_z):
                out_ref[j, k, first : first + count] = rows[128 * k : 128 * k + count]


def regrouped(s, cell_matrices, part):
    shape = cell_matrices.shape
    nodes = shape[3]
    return call(
        matrix_body,
        s,
        [jax.ShapeDtypeStruct(shape[1:3] + (s.padded, s.padded), BF16)],
        [
            pltpu.VMEM((shape[1], nodes, shape[2], nodes), BF16),
            pltpu.VMEM((nodes * shape[2], nodes), BF16),
            pltpu.VMEM((nodes * shape[2], s.padded), BF16),
            pltpu.SemaphoreType.DMA((shape[1],)),
        ],
        [cell_matrices.transpose(0, 1, 3, 2, 4)],
        spaces={0: pltpu.HBM},
        extra=(part,),
    )[0]


def along_z(s, msgs):
    if s.pairs:
        return [shifted(msgs[0], (0, 0, 1))]
    return [shifted(msgs[0], (0, 0, -1)), shifted(msgs[1], (0, 0, 1))]


def along_xy(msgs, by):
    return [shifted(msg, (by * dx, by * dy, 0)) for msg, dx, dy in zip(msgs, (1, 0, 1), (0, 1, 1))]


def local(wavefunctions, cell_matrices, projectors, slot_atoms, atom_coupling):
    atom_count = atom_coupling.shape[0]
    devices = 1
    for axis in AXES:
        devices *= lax.axis_size(axis)
    own = atom_count // devices
    s = Sizes(wavefunctions.shape, cell_matrices.shape, own, lax.axis_size("gz") == 2)
    plane = s.by * s.bzp
    sides = s.side_rows()
    field, by_atom, wide, *msgs, total, weight = call(
        first_body,
        s,
        [
            s.extended(),
            jax.ShapeDtypeStruct((s.bx, 2 * s.locals, plane), BF16),
            jax.ShapeDtypeStruct((s.z_rows, s.bzp, 2 * s.locals), F32),
        ]
        + s.z_msgs(s.z_both, s.z_sums)
        + [s.rows(s.locals), s.rows(s.locals)],
        [
            s.scratch(s.bx, s.by, s.bz),
            pltpu.VMEM(projectors.shape, F32),
            pltpu.VMEM(slot_atoms.shape, jnp.int32),
            pltpu.VMEM((1, atom_count), F32),
            pltpu.VMEM((s.bx * s.by * s.bz, 2 * s.locals), F32),
            s.scratch(s.z_both),
            s.scratch(s.z_sums),
            pltpu.SemaphoreType.DMA((1,)),
            pltpu.SemaphoreType.DMA((3,)),
        ],
        [wavefunctions, projectors, slot_atoms, atom_coupling[None, :]],
        spaces={0: pltpu.HBM, 1: pltpu.HBM, 2: pltpu.HBM, 3: pltpu.HBM},
    )
    matrices = [regrouped(s, cell_matrices, part) for part in range(s.cells[0])]
    received = along_z(s, msgs)
    *msgs, part = call(
        first_down_body,
        s,
        s.side_msgs() + [s.rows(2 * own)],
        [s.scratch(s.z_both), s.scratch(s.z_sums)] + sides,
        [field, total, matrices[0]] + received,
    )
    fills = (first_fill_body, [s.scratch(s.z_both), s.scratch(s.z_sums)], received)

    def cells(field, msgs, part, fills):
        body, scratch, along = fills
        received = along_xy(msgs, -1)
        (field,) = call(body, s, [s.extended()], scratch, [field, part] + along, aliases={0: 0})
        _, sums, *msgs, mine = call(
            cell_body,
            s,
            [s.extended(), jax.ShapeDtypeStruct((s.cells[2], s.bx + 1, s.by + 1, s.group, s.waves), F32)]
            + s.side_msgs()
            + [s.rows(2 * own)],
            sides,
            [field] + received + [part, weight] + matrices,
            aliases={0: 0},
        )
        received = along_xy(msgs, 1)
        (block,) = call(join_cells, s, [s.block()], [], [sums])
        return block, received, mine

    block, received, mine = cells(field, msgs, part, fills)
    by_node, lowest, lowest_by_node = call(
        node_body,
        s,
        [
            jax.ShapeDtypeStruct((s.bx, plane, 3 * s.locals), BF16),
            jax.ShapeDtypeStruct((2 * s.locals, s.z_plane), BF16),
            jax.ShapeDtypeStruct((s.z_rows, 3 * s.locals), BF16),
        ],
        [],
        [wide],
    )
    msgs = call(
        swap_body,
        s,
        s.z_msgs(s.z_plane, s.z_plane),
        sides + [s.scratch(s.z_plane), s.scratch(s.z_plane)],
        [block] + received + [mine, lowest_by_node],
    )
    swapped = along_z(s, msgs)
    (field,) = call(middle_body, s, [s.extended()], sides, [block] + received + [mine, by_node])
    received = swapped
    (total,) = call(sums_body, s, [s.rows(s.locals)], [], [field, by_atom])
    *msgs, part = call(
        second_down_body,
        s,
        s.side_msgs() + [s.rows(2 * own)],
        [s.scratch(s.z_plane), s.scratch(s.z_plane)] + sides,
        [field, total, lowest] + received,
    )
    fills = (second_fill_body, [s.scratch(s.z_plane), s.scratch(s.z_plane)], received)
    block, received, mine = cells(field, msgs, part, fills)
    block, *msgs, total = call(
        fold_body,
        s,
        [s.block()] + s.z_msgs(s.z_sums, s.z_both) + [s.rows(s.locals)],
        sides + [s.scratch(s.z_sums), s.scratch(s.z_both)],
        [block] + received + [mine],
        aliases={0: 0},
    )
    received = along_z(s, msgs)
    (out,) = call(
        last_body,
        s,
        [jax.ShapeDtypeStruct(wavefunctions.shape, F32)],
        [
            s.scratch(s.z_sums),
            s.scratch(s.z_both),
            s.scratch(s.bx, s.by, s.bzp),
            s.scratch(s.bx, s.by, s.bz),
            pltpu.SemaphoreType.DMA((s.bx // s.few_out,)),
        ],
        [wavefunctions, block, total, by_node] + received,
        out_spaces={0: pltpu.HBM},
    )
    return out


def solution(mesh):
    return jax.shard_map(
        local,
        mesh=mesh,
        in_specs=(
            P("gx", "gy", "gz", None),
            P("gx", "gy", "gz", None, None),
            P(("gx", "gy", "gz"), None, None),
            P(("gx", "gy", "gz"), None),
            P(),
        ),
        out_specs=P("gx", "gy", "gz", None),
        check_vma=False,
    )
```
